32 devices in a mesh: fsdp: 4 (over x, core), ctx: 8 (over z, y).
Axes of the slice: x: 2, y: 2, z: 4, core: 2. Of those that a mesh axis runs over, the one named last changes fastest.
Arguments:
- tokens: bfloat16 [4096, 2048], P(('fsdp', 'ctx')), may hold values from -12 to 12
- gain_attn: bfloat16 [2048], P('fsdp'), may hold values from 0.099609375 to 1.8984375
- w_query: bfloat16 [2048, 2048], P('fsdp'), may hold values from -0.125 to 0.125
- w_key: bfloat16 [2048, 2048], P('fsdp'), may hold values from -0.125 to 0.125
- w_value: bfloat16 [2048, 2048], P('fsdp'), may hold values from -0.125 to 0.125
- w_out: bfloat16 [2048, 2048], P('fsdp'), may hold values from -0.5 to 0.5
- gain_mlp: bfloat16 [2048], P('fsdp'), may hold values from 0.099609375 to 1.8984375
- w_gate: bfloat16 [2048, 8192], P('fsdp'), may hold values from -0.125 to 0.125
- w_up: bfloat16 [2048, 8192], P('fsdp'), may hold values from -0.125 to 0.125
- w_down: bfloat16 [8192, 2048], P('fsdp'), may hold values from -0.0625 to 0.0625
- cotangent: bfloat16 [4096, 2048], P(('fsdp', 'ctx')), may hold values from -6 to 6
Outputs:
- output: bfloat16 [4096, 2048], P(('fsdp', 'ctx'))
- input_grad: bfloat16 [4096, 2048], P(('fsdp', 'ctx'))
- gain_attn_grad: float32 [2048], P(('fsdp', 'ctx'))
- w_query_grad: float32 [2048, 2048], P(('fsdp', 'ctx'))
- w_key_grad: float32 [2048, 2048], P(('fsdp', 'ctx'))
- w_value_grad: float32 [2048, 2048], P(('fsdp', 'ctx'))
- w_out_grad: float32 [2048, 2048], P(('fsdp', 'ctx'))
- gain_mlp_grad: float32 [2048], P(('fsdp', 'ctx'))
- w_gate_grad: float32 [2048, 8192], P(('fsdp', 'ctx'))
- w_up_grad: float32 [2048, 8192], P(('fsdp', 'ctx'))
- w_down_grad: float32 [8192, 2048], P(('fsdp', 'ctx'))
The draws below stay inside these ranges and needn't reach their ends.
All inputs are finite; a program needn't handle non-finite values.
Results may differ from the reference program's by a relative error of at most 0.02.
Values may be sent and summed in bfloat16 or wider, within the bound.
No kernel may reach another device: no remote copies, remote signals or barrier semaphores. Data moves between devices by JAX's collectives and lax.ppermute only.
A program may use at most 512 MiB of HBM per device.

```python
import jax
import jax.numpy as jnp
from jax import lax

D = 2048
HEADS = 32
HEAD_DIM = 64
FF = 8192
CTX_TOK = 128
LENGTH = 1024
TOKENS = 4096
N_FSDP = 4
N_CTX = 8


def spiked(array, own_key, source, target, parts, factor):
    def block_of(axis_at):
        return (jnp.arange(array.shape[axis_at]) // (array.shape[axis_at] // parts)).reshape((-1,) + (1,) * (array.ndim - 1 - axis_at))

    first = jax.random.permutation(own_key, parts)[block_of(target)]
    far = (block_of(target) + parts // 2) % parts
    return jnp.where((block_of(source) == first) | (block_of(source) == far), factor * array, array)


def shard_levels(own_key, extent, pieces, low, high):
    factor_of, own = 1.0, jax.random.fold_in(own_key, 6)
    for axis_at, blocks in pieces:
        heights = jnp.exp(jax.random.uniform(jax.random.fold_in(own, axis_at), (blocks,), jnp.float32, low / len(pieces), high / len(pieces)))
        factor_of = factor_of * jnp.repeat(heights, extent[axis_at] // blocks).reshape([-1 if axis == axis_at else 1 for axis in range(len(extent))])
    return factor_of


def noise(key, dims, scale, reach, pieces=(), kind=jnp.bfloat16):
    drawn = scale * jax.random.normal(key, dims, jnp.float32)
    if pieces:
        drawn = drawn * shard_levels(key, dims, pieces, -0.22, 0.18)
    return jnp.clip(drawn, -reach, reach).astype(kind)


def bell_draw_with(rng, extent, scale, limit, cuts, heavy, kind=jnp.bfloat16):
    drawn = scale * jax.random.normal(rng, extent, jnp.float32)
    if cuts:
        drawn = drawn * shard_levels(rng, extent, cuts, -0.22, 0.18)
    return jnp.clip(spiked(drawn, jax.random.fold_in(rng, 3), *heavy), -limit, limit).astype(kind)


def setup_inputs(seed: int = 0) -> dict:
    arg_keys = jax.random.split(jax.random.key(seed), 12)
    tokens = bell_draw_with(arg_keys[0], (TOKENS, D), 1.0, 12.0, ((0, 32),), (0, 1, 32, 2.75))
    gain_attn = jnp.clip(1.0 + 0.18 * jax.random.normal(arg_keys[1], (D,), jnp.float32), 0.099609375, 1.8984375).astype(jnp.bfloat16)
    w_query = noise(arg_keys[2], (D, D), D ** -0.5, 0.125, ((0, 4),))
    w_key = noise(arg_keys[3], (D, D), D ** -0.5, 0.125, ((0, 4),))
    w_value = noise(arg_keys[4], (D, D), D ** -0.5, 0.125, ((0, 4),))
    w_out = noise(arg_keys[5], (D, D), (D // 16) ** -0.5, 0.5, ((0, 4),))
    gain_mlp = jnp.clip(1.0 + 0.18 * jax.random.normal(arg_keys[6], (D,), jnp.float32), 0.099609375, 1.8984375).astype(jnp.bfloat16)
    w_gate = noise(arg_keys[7], (D, FF), D ** -0.5, 0.125, ((0, 4),))
    w_up = noise(arg_keys[8], (D, FF), D ** -0.5, 0.125, ((0, 4),))
    w_down = noise(arg_keys[9], (FF, D), FF ** -0.5, 0.0625, ((0, 4),))
    cotangent = noise(arg_keys[10], (TOKENS, D), 1.0, 6.0, ((0, 32),))
    return {"tokens": tokens, "gain_attn": gain_attn, "w_query": w_query, "w_key": w_key, "w_value": w_value, "w_out": w_out, "gain_mlp": gain_mlp, "w_gate": w_gate, "w_up": w_up, "w_down": w_down, "cotangent": cotangent}


@jax.custom_vjp
def low(v):
    return lax.optimization_barrier(v.astype(jnp.bfloat16)).astype(jnp.float32)

@jax.custom_vjp
def low_back(v):
    return v

def low_keep(v):
    return (low(v), None)

def low_pass(kept, grad):
    return (grad,)

def back_keep(v):
    return (v, None)

def back_low(kept, grad):
    return (low(grad),)
low.defvjp(low_keep, low_pass)
low_back.defvjp(back_keep, back_low)
EPS = 1e-05
THETA = 130000.0
HIGH = lax.Precision.HIGHEST
MASKED = -1e+30

def product(left, right):
    return jnp.dot(left, right, precision=HIGH, preferred_element_type=jnp.float32)

def slot_positions(slots, per_device, devices):
    half = per_device // 2
    block = slots // per_device
    inner = slots % per_device
    return jnp.where(inner < half, block * half + inner, (2 * devices - 1 - block) * half + inner - half).astype(jnp.int32)

def rotate(matrix, positions, heads, sign):
    row_count = matrix.shape[0]
    width = matrix.shape[1] // heads
    half = width // 2
    freqs = THETA ** (-(jnp.arange(half, dtype=jnp.float32) * 2.0 / width))
    angles = positions.astype(jnp.float32)[:, None] * freqs[None, :]
    cosine = jnp.cos(angles)[:, None, :]
    sine = sign * jnp.sin(angles)[:, None, :]
    split = matrix.reshape(row_count, heads, width)
    first = split[:, :, :half]
    second = split[:, :, half:]
    return jnp.concatenate([first * cosine - second * sine, second * cosine + first * sine], axis=2).reshape(row_count, heads * width)

def rms_scale(matrix, gain):
    return matrix * lax.rsqrt(lax.optimization_barrier(jnp.mean(matrix * matrix, axis=-1, keepdims=True)) + EPS) * gain

def attend_block(block, keys, values, key_places):
    queries, query_places = block
    row_count = queries.shape[0]
    queries_3d = queries.reshape(row_count, HEADS, HEAD_DIM)
    keys_3d = keys.reshape(keys.shape[0], HEADS, HEAD_DIM)
    values_3d = values.reshape(values.shape[0], HEADS, HEAD_DIM)
    scores = jnp.einsum('qhd,khd->hqk', queries_3d, keys_3d, precision=HIGH) * HEAD_DIM ** (-0.5)
    scores = low_back(scores)
    allowed = key_places[None, None, :] <= query_places[None, :, None]
    scores = jnp.where(allowed, scores, MASKED)
    row_max = lax.optimization_barrier(jnp.max(scores, axis=-1, keepdims=True))
    raised = jnp.exp(scores - row_max)
    shares = raised / lax.optimization_barrier(jnp.sum(raised, axis=-1, keepdims=True))
    mixed = jnp.einsum('hqk,khd->qhd', low(shares), values_3d, precision=HIGH)
    return mixed.reshape(row_count, HEADS * HEAD_DIM)

def layer(inputs, gain_attn, w_query, w_key, w_value, w_out, gain_mlp, w_gate, w_up, w_down, positions):
    normed = low(rms_scale(inputs, gain_attn))
    queries = low(rotate(low_back(product(normed, w_query)), positions, HEADS, 1.0))
    keys = low(rotate(low_back(product(normed, w_key)), positions, HEADS, 1.0))
    values = low(low_back(product(normed, w_value)))
    block_rows = min(512, LENGTH)
    block_count = LENGTH // block_rows

    def one_block(block):
        return attend_block(block, keys, values, positions)
    mixed = lax.map(jax.checkpoint(one_block), (queries.reshape(block_count, block_rows, D), positions.reshape(block_count, block_rows)))
    mixed = low_back(low(mixed.reshape(LENGTH, D)))
    branch = low_back(product(mixed, w_out))
    middle = inputs + branch
    normed_mlp = low(rms_scale(middle, gain_mlp))
    gate = low_back(product(normed_mlp, w_gate))
    upward = low_back(product(normed_mlp, w_up))
    hidden = low(jax.nn.silu(gate) * upward)
    return middle + product(hidden, w_down)

def reference(tokens, gain_attn, w_query, w_key, w_value, w_out, gain_mlp, w_gate, w_up, w_down, cotangent):
    positions = slot_positions(jnp.arange(LENGTH, dtype=jnp.int32), CTX_TOK, N_CTX)
    float_weights = tuple((item.astype(jnp.float32) for item in (gain_attn, w_query, w_key, w_value, w_out, gain_mlp, w_gate, w_up, w_down)))
    inputs = tokens.astype(jnp.float32).reshape(N_FSDP, LENGTH, D)
    upstream = cotangent.astype(jnp.float32).reshape(N_FSDP, LENGTH, D)

    def one_sequence(totals, pair):
        sequence, arriving = pair

        def forward(inputs_one, *weights):
            return layer(inputs_one, *weights, positions)
        result, pull = jax.vjp(forward, sequence, *float_weights)
        gradients = pull(arriving)
        totals = tuple((total + grad for total, grad in zip(totals, gradients[1:])))
        return (totals, (result.astype(jnp.bfloat16), gradients[0].astype(jnp.bfloat16)))
    start = tuple((jnp.zeros_like(item) for item in float_weights))
    totals, (results, input_grads) = lax.scan(one_sequence, start, (inputs, upstream))
    return (results.reshape(TOKENS, D), input_grads.reshape(TOKENS, D), totals[0], totals[1], totals[2], totals[3], totals[4], totals[5], totals[6], totals[7], totals[8])
```

```python
import functools

import jax
import jax.numpy as jnp
import numpy as np
from jax import lax
from jax.experimental import pallas as pl
from jax.experimental.pallas import tpu as pltpu
from jax.sharding import PartitionSpec as P

HEADS = 32
EPS = 1e-05
THETA = 130000.0
MASKED = -1e30
BF = jnp.bfloat16
F32 = jnp.float32


def dot(left, right, left_axis, right_axis):
    return lax.dot_general(
        left, right, (((left_axis,), (right_axis,)), ((), ())), preferred_element_type=F32
    )


def norm_parts(matrix):
    scale = lax.rsqrt(jnp.mean(matrix * matrix, axis=-1, keepdims=True) + EPS)
    return (matrix * scale, scale)


def norm_back(grad_scaled, normed, scale):
    return scale * (grad_scaled - normed * jnp.mean(grad_scaled * normed, axis=-1, keepdims=True))


def angle_tables(length, head_width):
    half = head_width // 2
    freqs = np.float32(THETA) ** (-(np.arange(half, dtype=np.float32) * np.float32(2.0 / head_width)))
    angles = freqs[:, None].astype(np.float32) * np.arange(length, dtype=np.float32)[None, :]
    return jnp.asarray(np.cos(angles), F32), jnp.asarray(np.sin(angles), F32)


def low_lanes(block):
    return lax.broadcasted_iota(jnp.int32, block.shape, 1) < block.shape[1] // 2


def sort_columns(matrix, blocks):
    size = matrix.shape[1] // blocks
    early, late = [], []
    for j in range(blocks // 2):
        first = matrix[:, 2 * j * size : (2 * j + 1) * size]
        second = pltpu.roll(matrix[:, (2 * j + 1) * size : (2 * j + 2) * size], size // 2, 1)
        low = low_lanes(first)
        early.append(jnp.where(low, first, second))
        late.append(jnp.where(low, second, first))
    return jnp.concatenate(early + late[::-1], axis=1)


def deal_columns(matrix, blocks):
    size = matrix.shape[1] // blocks
    out = []
    for j in range(blocks // 2):
        early = matrix[:, j * size : (j + 1) * size]
        late = matrix[:, (blocks - 1 - j) * size : (blocks - j) * size]
        low = low_lanes(early)
        out.append(jnp.where(low, early, late))
        out.append(pltpu.roll(jnp.where(low, late, early), size // 2, 1))
    return jnp.concatenate(out, axis=1)


def turn(matrix, cosine, sine):
    half = matrix.shape[0] // 2
    first, second = matrix[:half], matrix[half:]
    return jnp.concatenate([first * cosine - second * sine, second * cosine + first * sine], axis=0)


def masked_block(scores, chunk):
    keys = scores.shape[0]
    places = lax.broadcasted_iota(jnp.int32, (chunk, chunk), 0)
    wants = lax.broadcasted_iota(jnp.int32, (chunk, chunk), 1)
    last = jnp.where(places <= wants, scores[keys - chunk :], MASKED)
    if keys == chunk:
        return last
    return jnp.concatenate([scores[: keys - chunk], last], axis=0)


def attend_kernel(blocks, chunk, q_ref, k_ref, v_ref, cos_ref, sin_ref, o_ref, qs_ref, ks_ref, vs_ref, lse_ref):
    width, length = q_ref.shape
    cosine, sine = cos_ref[...], sin_ref[...]
    query = turn(sort_columns(q_ref[...], blocks), cosine, sine).astype(BF)
    key = turn(sort_columns(k_ref[...], blocks), cosine, sine).astype(BF)
    value = sort_columns(v_ref[...], blocks).astype(BF)
    scaled = query * jnp.asarray(width ** (-0.5), BF)
    qs_ref[...] = scaled
    ks_ref[...] = key
    vs_ref[...] = value
    mixed, logs = [], []
    for i in range(length // chunk):
        count = (i + 1) * chunk
        scores = dot(key[:, :count], scaled[:, i * chunk : count], 0, 0)
        scores = masked_block(scores, chunk)
        top = jnp.max(scores, axis=0, keepdims=True)
        raised = jnp.exp(scores - top)
        total = jnp.sum(raised, axis=0, keepdims=True)
        mixed.append(dot(value[:, :count], raised.astype(BF), 1, 0) / total)
        logs.append(top + jnp.log(total))
    o_ref[...] = deal_columns(jnp.concatenate(mixed, axis=1), blocks).astype(BF)
    lse_ref[0] = jnp.concatenate(logs, axis=1)


def attend_back_kernel(blocks, chunk, q_ref, k_ref, v_ref, o_ref, do_ref, lse_ref, cos_ref, sin_ref, d_ref, dk_ref, dv_ref):
    width, length = q_ref.shape
    factor = width ** (-0.5)
    cosine, sine = cos_ref[...], -sin_ref[...]
    scaled, key, value = q_ref[...], k_ref[...], v_ref[...]
    grad_f32 = sort_columns(do_ref[...].astype(F32), blocks)
    center = jnp.sum(grad_f32 * sort_columns(o_ref[...].astype(F32), blocks), axis=0, keepdims=True)
    grad = grad_f32.astype(BF)
    logs = lse_ref[0]
    dq = []
    for i in reversed(range(length // chunk)):
        count = (i + 1) * chunk
        here = slice(i * chunk, count)
        scores = masked_block(dot(key[:, :count], scaled[:, here], 0, 0), chunk)
        shares = jnp.exp(scores - logs[:, here])
        grad_shares = dot(value[:, :count], grad[:, here], 0, 0)
        grad_scores = (shares * (grad_shares - center[:, here])).astype(BF)
        dq.append(dot(key[:, :count], grad_scores, 1, 0))
        dk_part = dot(scaled[:, here], grad_scores, 1, 1)
        dv_part = dot(grad[:, here], shares.astype(BF), 1, 1)
        if count == length:
            dk_ref[...] = dk_part
            dv_ref[...] = dv_part
        else:
            dk_ref[:, :count] += dk_part
            dv_ref[:, :count] += dv_part
    dq = turn(jnp.concatenate(dq[::-1], axis=1) * factor, cosine, sine)
    d_ref[0] = deal_columns(dq, blocks).astype(BF)
    d_ref[1] = deal_columns(turn(dk_ref[...], cosine, sine), blocks).astype(BF)
    d_ref[2] = deal_columns(dv_ref[...], blocks).astype(BF)


def attend(raw, cosine, sine, heads, blocks):
    width, length = raw.shape[0] // (3 * heads), raw.shape[1]
    chunk = min(256, length)
    head = lambda shift: pl.BlockSpec((width, length), lambda h: (h + shift * heads, 0))
    table = pl.BlockSpec((width // 2, length), lambda h: (0, 0))
    flat = jax.ShapeDtypeStruct((heads * width, length), BF)
    return pl.pallas_call(
        functools.partial(attend_kernel, blocks, chunk),
        grid=(heads,),
        in_specs=[head(0), head(1), head(2), table, table],
        out_specs=[head(0), head(0), head(0), head(0), pl.BlockSpec((1, 1, length), lambda h: (h, 0, 0))],
        out_shape=[flat, flat, flat, flat, jax.ShapeDtypeStruct((heads, 1, length), F32)],
        compiler_params=pltpu.CompilerParams(vmem_limit_bytes=40 * 1024 * 1024),
        name="attend",
    )(raw, raw, raw, cosine, sine)


def attend_back(query, key, value, mixed, grad, logs, cosine, sine, heads, blocks):
    width, length = query.shape[0] // heads, query.shape[1]
    chunk = min(256, length)
    head = pl.BlockSpec((width, length), lambda h: (h, 0))
    table = pl.BlockSpec((width // 2, length), lambda h: (0, 0))
    return pl.pallas_call(
        functools.partial(attend_back_kernel, blocks, chunk),
        grid=(heads,),
        in_specs=[head, head, head, head, head, pl.BlockSpec((1, 1, length), lambda h: (h, 0, 0)), table, table],
        out_specs=pl.BlockSpec((3, width, length), lambda h: (0, h, 0)),
        out_shape=jax.ShapeDtypeStruct((3, heads * width, length), BF),
        scratch_shapes=[pltpu.VMEM((width, length), F32), pltpu.VMEM((width, length), F32)],
        compiler_params=pltpu.CompilerParams(vmem_limit_bytes=40 * 1024 * 1024),
        name="attend_back",
    )(query, key, value, mixed, grad, logs, cosine, sine)


def gather(piece, axis):
    return lax.all_gather(piece, axis, axis=0, tiled=True)


def scatter(partial, axis):
    return lax.psum_scatter(partial.astype(BF), axis, scatter_dimension=0, tiled=True).astype(F32)


def body(
    tokens, gain_attn, w_query, w_key, w_value, w_out, gain_mlp, w_gate, w_up, w_down, cotangent
):
    row_count, width = tokens.shape
    hidden_width = w_gate.shape[1]
    fsdp, ctx = lax.axis_size("fsdp"), lax.axis_size("ctx")
    place = lax.axis_index("ctx")
    length = row_count * ctx
    heads = HEADS // ctx
    head_width = width // HEADS
    dealt = (HEADS // fsdp) % ctx == 0
    own_rows = width // (fsdp * ctx)
    cosine, sine = angle_tables(length, head_width)

    def own_columns(weight, split):
        rows, columns = weight.shape
        if not split:
            return lax.dynamic_slice_in_dim(weight, place * (columns // ctx), columns // ctx, 1)
        blocks = weight.reshape(rows, fsdp, ctx, columns // (fsdp * ctx))
        return lax.dynamic_index_in_dim(blocks, place, 2, keepdims=False).reshape(rows, -1)

    def all_columns(received, split):
        rows = received.shape[1]
        if not split:
            return received.transpose(1, 0, 2).reshape(rows, -1)
        blocks = received.reshape(ctx, rows, fsdp, -1)
        return blocks.transpose(1, 2, 0, 3).reshape(rows, -1)

    def own_row_share(weight):
        size = weight.shape[0] // ctx
        return gather(lax.dynamic_slice_in_dim(weight, place * size, size, 0), "fsdp")

    def to_owners(partial):
        summed = lax.psum_scatter(partial.astype(BF), "fsdp", scatter_dimension=0, tiled=True)
        return lax.all_to_all(summed, "ctx", 0, 0, tiled=True).reshape(ctx, own_rows, -1).astype(F32)

    w_qkv = gather(
        jnp.concatenate([own_columns(item, dealt) for item in (w_query, w_key, w_value)], axis=1), "fsdp"
    )
    gains = gather(jnp.stack([gain_attn, gain_mlp], axis=1), "fsdp").astype(F32)
    gain_one, gain_two = gains[:, 0], gains[:, 1]

    inputs = tokens.astype(F32)
    normed_attn, scale_attn = norm_parts(inputs)
    first_all = gather((normed_attn * gain_one).astype(BF), "ctx")
    raw = dot(w_qkv, first_all, 0, 1)
    mixed, query, key, value, logs = attend(raw, cosine, sine, heads, ctx)
    if dealt:
        out_share = own_row_share(w_out)
    else:
        out_share = lax.dynamic_slice_in_dim(
            gather(w_out, "fsdp"), place * heads * head_width, heads * head_width, 0
        )
    branch = scatter(dot(mixed, out_share, 0, 0), "ctx")
    middle = inputs + branch
    normed_mid, scale_mid = norm_parts(middle)
    second_all = gather((normed_mid * gain_two).astype(BF), "ctx")
    w_gate_up = gather(
        jnp.concatenate([own_columns(item, True) for item in (w_gate, w_up)], axis=1), "fsdp"
    )
    down_share = own_row_share(w_down)
    cotangent_all = gather(cotangent, "ctx")
    share = hidden_width // ctx
    gate_up = dot(second_all, w_gate_up, 1, 0)
    gate, upward = gate_up[:, :share], gate_up[:, share:]
    grad_hidden = dot(cotangent_all, down_share, 1, 1)
    sigmoid = jax.nn.sigmoid(gate)
    hidden = (gate * sigmoid * upward).astype(BF)
    grad_gate = (grad_hidden * upward * (sigmoid + gate * sigmoid * (1.0 - sigmoid))).astype(BF)
    grad_up = (grad_hidden * (gate * sigmoid)).astype(BF)
    grad_gate_up = jnp.concatenate([grad_gate, grad_up], axis=1)
    grad_normed = scatter(dot(grad_gate_up, w_gate_up, 1, 1), "ctx")
    output = (middle + scatter(dot(hidden, down_share, 1, 0), "ctx")).astype(BF)

    gain_mlp_term = jnp.sum(grad_normed * normed_mid, axis=0)
    grad_middle = cotangent.astype(F32) + norm_back(grad_normed * gain_two, normed_mid, scale_mid)
    branch_all = gather(grad_middle.astype(BF), "ctx")
    grad_mixed = dot(out_share, branch_all, 1, 1).astype(BF)
    grad_raw = attend_back(query, key, value, mixed, grad_mixed, logs, cosine, sine, heads, ctx)
    grad_raw = grad_raw.reshape(-1, length)
    grad_normed = scatter(dot(grad_raw, w_qkv, 0, 1), "ctx")
    gain_attn_term = jnp.sum(grad_normed * normed_attn, axis=0)
    input_grad = (grad_middle + norm_back(grad_normed * gain_one, normed_attn, scale_attn)).astype(BF)

    down_grad = scatter(dot(hidden, cotangent_all, 0, 0), "fsdp")
    if dealt:
        out_grad = scatter(dot(mixed, branch_all, 1, 0), "fsdp")
    else:
        whole = jnp.zeros((width, width), BF)
        whole = lax.dynamic_update_slice_in_dim(
            whole, dot(mixed, branch_all, 1, 0).astype(BF), place * heads * head_width, 0
        )
        out_grad = scatter(whole, ("fsdp", "ctx"))
    gate_up_rows = to_owners(dot(second_all, grad_gate_up, 0, 0))
    qkv_rows = to_owners(dot(first_all, grad_raw, 0, 1))
    part = heads * head_width
    gain_terms = jnp.stack([gain_attn_term, gain_mlp_term]).reshape(2, fsdp * ctx, own_rows)
    gain_grads = jnp.sum(
        lax.all_to_all(gain_terms.transpose(1, 0, 2), ("fsdp", "ctx"), 0, 0, tiled=True), axis=0
    )
    return (
        output,
        input_grad,
        gain_grads[0],
        all_columns(qkv_rows[:, :, :part], dealt),
        all_columns(qkv_rows[:, :, part : 2 * part], dealt),
        all_columns(qkv_rows[:, :, 2 * part :], dealt),
        out_grad,
        gain_grads[1],
        all_columns(gate_up_rows[:, :, :share], True),
        all_columns(gate_up_rows[:, :, share:], True),
        down_grad,
    )


def solution(mesh):
    both = ("fsdp", "ctx")
    matrix = P("fsdp", None)
    in_specs = (P(both, None), P("fsdp"), matrix, matrix, matrix, matrix, P("fsdp"), matrix, matrix, matrix, P(both, None))
    rows = P(both, None)
    out_specs = (rows, rows, P(both), rows, rows, rows, rows, P(both), rows, rows, rows)
    return jax.shard_map(body, mesh=mesh, in_specs=in_specs, out_specs=out_specs, check_vma=False)
```

```python
import functools

import jax
import jax.numpy as jnp
import numpy as np
from jax import lax
from jax.experimental import pallas as pl
from jax.experimental.pallas import tpu as pltpu
from jax.sharding import PartitionSpec as P

HEADS = 32
EPS = 1e-05
THETA = 130000.0
MASKED = -1e30
BF = jnp.bfloat16
F32 = jnp.float32


def dot(left, right, left_axis, right_axis):
    return lax.dot_general(
        left, right, (((left_axis,), (right_axis,)), ((), ())), preferred_element_type=F32
    )


def norm_parts(matrix):
    scale = lax.rsqrt(jnp.mean(matrix * matrix, axis=-1, keepdims=True) + EPS)
    return (matrix * scale, scale)


def norm_back(grad_scaled, normed, scale):
    return scale * (grad_scaled - normed * jnp.mean(grad_scaled * normed, axis=-1, keepdims=True))


def angle_tables(length, head_width):
    half = head_width // 2
    freqs = np.float32(THETA) ** (-(np.arange(half, dtype=np.float32) * np.float32(2.0 / head_width)))
    angles = freqs[:, None].astype(np.float32) * np.arange(length, dtype=np.float32)[None, :]
    return jnp.asarray(np.cos(angles), F32), jnp.asarray(np.sin(angles), F32)


def low_lanes(block):
    return lax.broadcasted_iota(jnp.int32, block.shape, 1) < block.shape[1] // 2


def sort_columns(matrix, blocks):
    size = matrix.shape[1] // blocks
    early, late = [], []
    for j in range(blocks // 2):
        first = matrix[:, 2 * j * size : (2 * j + 1) * size]
        second = pltpu.roll(matrix[:, (2 * j + 1) * size : (2 * j + 2) * size], size // 2, 1)
        low = low_lanes(first)
        early.append(jnp.where(low, first, second))
        late.append(jnp.where(low, second, first))
    return jnp.concatenate(early + late[::-1], axis=1)


def deal_columns(matrix, blocks):
    size = matrix.shape[1] // blocks
    out = []
    for j in range(blocks // 2):
        early = matrix[:, j * size : (j + 1) * size]
        late = matrix[:, (blocks - 1 - j) * size : (blocks - j) * size]
        low = low_lanes(early)
        out.append(jnp.where(low, early, late))
        out.append(pltpu.roll(jnp.where(low, late, early), size // 2, 1))
    return jnp.concatenate(out, axis=1)


def turn(matrix, cosine, sine):
    half = matrix.shape[0] // 2
    first, second = matrix[:half], matrix[half:]
    return jnp.concatenate([first * cosine - second * sine, second * cosine + first * sine], axis=0)


def by_blocks(ref):
    return jnp.concatenate([ref[block].astype(F32) for block in range(ref.shape[0])], axis=1)


def masked_block(scores, chunk):
    keys = scores.shape[0]
    places = lax.broadcasted_iota(jnp.int32, (chunk, chunk), 0)
    wants = lax.broadcasted_iota(jnp.int32, (chunk, chunk), 1)
    last = jnp.where(places <= wants, scores[keys - chunk :], MASKED)
    if keys == chunk:
        return last
    return jnp.concatenate([scores[: keys - chunk], last], axis=0)


def attend_kernel(blocks, chunk, q_ref, k_ref, v_ref, cos_ref, sin_ref, o_ref, qs_ref, ks_ref, vs_ref, lse_ref):
    width, length = q_ref.shape
    cosine, sine = cos_ref[...], sin_ref[...]
    query = turn(sort_columns(q_ref[...], blocks), cosine, sine).astype(BF)
    key = turn(sort_columns(k_ref[...], blocks), cosine, sine).astype(BF)
    value = sort_columns(v_ref[...], blocks).astype(BF)
    scaled = query * jnp.asarray(width ** (-0.5), BF)
    qs_ref[...] = scaled
    ks_ref[...] = key
    vs_ref[...] = value
    mixed, logs = [], []
    for i in range(length // chunk):
        count = (i + 1) * chunk
        scores = dot(key[:, :count], scaled[:, i * chunk : count], 0, 0)
        scores = masked_block(scores, chunk)
        top = jnp.max(scores, axis=0, keepdims=True)
        raised = jnp.exp(scores - top)
        total = jnp.sum(raised, axis=0, keepdims=True)
        mixed.append(dot(value[:, :count], raised.astype(BF), 1, 0) / total)
        logs.append(top + jnp.log(total))
    size = length // blocks
    dealt = deal_columns(jnp.concatenate(mixed, axis=1), blocks).astype(BF)
    for block in range(blocks):
        o_ref[block] = dealt[:, block * size : (block + 1) * size]
    lse_ref[0] = jnp.concatenate(logs, axis=1)


def attend_back_kernel(blocks, chunk, q_ref, k_ref, v_ref, o_ref, do_ref, lse_ref, cos_ref, sin_ref, d_ref, dk_ref, dv_ref):
    width, length = q_ref.shape
    factor = width ** (-0.5)
    cosine, sine = cos_ref[...], -sin_ref[...]
    scaled, key, value = q_ref[...], k_ref[...], v_ref[...]
    grad_f32 = sort_columns(by_blocks(do_ref), blocks)
    center = jnp.sum(grad_f32 * sort_columns(by_blocks(o_ref), blocks), axis=0, keepdims=True)
    grad = grad_f32.astype(BF)
    logs = lse_ref[0]
    dq = []
    for i in reversed(range(length // chunk)):
        count = (i + 1) * chunk
        here = slice(i * chunk, count)
        scores = masked_block(dot(key[:, :count], scaled[:, here], 0, 0), chunk)
        shares = jnp.exp(scores - logs[:, here])
        grad_shares = dot(value[:, :count], grad[:, here], 0, 0)
        grad_scores = (shares * (grad_shares - center[:, here])).astype(BF)
        dq.append(dot(key[:, :count], grad_scores, 1, 0))
        dk_part = dot(scaled[:, here], grad_scores, 1, 1)
        dv_part = dot(grad[:, here], shares.astype(BF), 1, 1)
        if count == length:
            dk_ref[...] = dk_part
            dv_ref[...] = dv_part
        else:
            dk_ref[:, :count] += dk_part
            dv_ref[:, :count] += dv_part
    dq = turn(jnp.concatenate(dq[::-1], axis=1) * factor, cosine, sine)
    d_ref[0] = deal_columns(dq, blocks).astype(BF)
    d_ref[1] = deal_columns(turn(dk_ref[...], cosine, sine), blocks).astype(BF)
    d_ref[2] = deal_columns(dv_ref[...], blocks).astype(BF)


def attend(raw, cosine, sine, heads, blocks):
    width, length = raw.shape[0] // (3 * heads), raw.shape[1]
    chunk = min(256, length)
    head = lambda shift: pl.BlockSpec((width, length), lambda h: (h + shift * heads, 0))
    table = pl.BlockSpec((width // 2, length), lambda h: (0, 0))
    flat = jax.ShapeDtypeStruct((heads * width, length), BF)
    return pl.pallas_call(
        functools.partial(attend_kernel, blocks, chunk),
        grid=(heads,),
        in_specs=[head(0), head(1), head(2), table, table],
        out_specs=[
            pl.BlockSpec((blocks, width, length // blocks), lambda h: (0, h, 0)),
            head(0),
            head(0),
            head(0),
            pl.BlockSpec((1, 1, length), lambda h: (h, 0, 0)),
        ],
        out_shape=[
            jax.ShapeDtypeStruct((blocks, heads * width, length // blocks), BF),
            flat,
            flat,
            flat, jax.ShapeDtypeStruct((heads, 1, length), F32),
        ],
        compiler_params=pltpu.CompilerParams(vmem_limit_bytes=40 * 1024 * 1024),
        name="attend",
    )(raw, raw, raw, cosine, sine)


def attend_back(query, key, value, mixed, grad, logs, cosine, sine, heads, blocks):
    width, length = query.shape[0] // heads, query.shape[1]
    chunk = min(256, length)
    head = pl.BlockSpec((width, length), lambda h: (h, 0))
    block = pl.BlockSpec((blocks, width, length // blocks), lambda h: (0, h, 0))
    table = pl.BlockSpec((width // 2, length), lambda h: (0, 0))
    return pl.pallas_call(
        functools.partial(attend_back_kernel, blocks, chunk),
        grid=(heads,),
        in_specs=[head, head, head, block, block, pl.BlockSpec((1, 1, length), lambda h: (h, 0, 0)), table, table],
        out_specs=pl.BlockSpec((3, width, length), lambda h: (0, h, 0)),
        out_shape=jax.ShapeDtypeStruct((3, heads * width, length), BF),
        scratch_shapes=[pltpu.VMEM((width, length), F32), pltpu.VMEM((width, length), F32)],
        compiler_params=pltpu.CompilerParams(vmem_limit_bytes=40 * 1024 * 1024),
        name="attend_back",
    )(query, key, value, mixed, grad, logs, cosine, sine)


def swap(item, axis, bit):
    pairs = [(i, i ^ bit) for i in range(lax.axis_size(axis))]
    return lax.ppermute(item, axis, pairs)


def step_on(item):
    count = lax.axis_size("ctx")
    return lax.ppermute(item, "ctx", [(i, (i + 2) % count) for i in range(count)])


def after(item, *others):
    return lax.optimization_barrier((item,) + others)[0]


def gather_rows(piece):
    count, place = lax.axis_size("ctx"), lax.axis_index("ctx")
    rows = jnp.zeros((count,) + piece.shape, piece.dtype)
    for hop in range(count // 2):
        if hop:
            piece = step_on(piece)
        source = lax.rem(place + count - 2 * hop, count)
        rows = lax.dynamic_update_slice(rows, piece[None], (source, 0, 0))
        rows = lax.dynamic_update_slice(rows, swap(piece, "ctx", 1)[None], (source ^ 1, 0, 0))
    return rows.reshape(-1, rows.shape[2])


def scatter_rows(partial):
    count, place = lax.axis_size("ctx"), lax.axis_index("ctx")
    blocks = partial.astype(BF).reshape(count, -1, partial.shape[1])
    total = None
    for hop in range(1, count // 2 + 1):
        target = lax.rem(place + count - 2 * hop, count)
        mine = lax.dynamic_index_in_dim(blocks, target, 0, keepdims=False)
        other = lax.dynamic_index_in_dim(blocks, target ^ 1, 0, keepdims=False)
        term = mine.astype(F32) + swap(other, "ctx", 1).astype(F32)
        total = term if total is None else term + total.astype(F32)
        if hop < count // 2:
            total = step_on(total.astype(BF))
    return total


def gather_weight(piece):
    if lax.axis_size("fsdp") != 4:
        return lax.all_gather(piece, "fsdp", axis=0, tiled=True)
    place = lax.axis_index("fsdp")
    rows = jnp.zeros((4,) + piece.shape, piece.dtype)
    far = swap(piece, "fsdp", 2)
    for source, item in (
        (place, piece),
        (place ^ 1, swap(piece, "fsdp", 1)),
        (place ^ 2, far),
        (place ^ 3, swap(far, "fsdp", 1)),
    ):
        rows = lax.dynamic_update_slice(rows, item[None], (source, 0, 0))
    return rows.reshape(-1, piece.shape[1])


def scatter(partial, axis):
    return lax.psum_scatter(partial.astype(BF), axis, scatter_dimension=0, tiled=True)


def general_body(
    tokens, gain_attn, w_query, w_key, w_value, w_out, gain_mlp, w_gate, w_up, w_down, cotangent
):
    width = tokens.shape[1]
    hidden_width = w_gate.shape[1]
    fsdp, ctx = lax.axis_size("fsdp"), lax.axis_size("ctx")
    place = lax.axis_index("ctx")
    length = tokens.shape[0] * ctx
    heads = HEADS // ctx
    part = width // ctx
    share = hidden_width // ctx
    own_rows = width // (fsdp * ctx)
    cosine, sine = angle_tables(length, width // HEADS)

    def head_columns(weight):
        return lax.dynamic_slice_in_dim(weight, place * part, part, 1)

    def hidden_columns(weight):
        rows = weight.shape[0]
        blocks = weight.reshape(rows, fsdp, ctx, share // fsdp)
        return lax.dynamic_index_in_dim(blocks, place, 2, keepdims=False).reshape(rows, share)

    def to_owners(partial):
        summed = scatter(partial, "fsdp")
        return lax.all_to_all(summed, "ctx", 0, 0, tiled=True).reshape(ctx, own_rows, -1).astype(F32)

    def of_heads(received):
        return received.transpose(1, 0, 2).reshape(own_rows, -1)

    def of_hidden(received):
        blocks = received.reshape(ctx, own_rows, fsdp, -1)
        return blocks.transpose(1, 2, 0, 3).reshape(own_rows, -1)

    def normed_rows(rows):
        return norm_parts(rows.astype(F32))[0]

    w_qkv_piece = jnp.concatenate([head_columns(item) for item in (w_query, w_key, w_value)], axis=1)
    w_qkv = gather_weight(w_qkv_piece)
    gains = lax.all_gather(jnp.stack([gain_attn, gain_mlp]), "fsdp", axis=1, tiled=True).astype(F32)
    gain_one, gain_two = gains[0], gains[1]
    tokens_all = gather_rows(tokens)
    first_all = (normed_rows(tokens_all) * gain_one).astype(BF)
    raw = dot(w_qkv, first_all, 0, 1)
    mixed, query, key, value, logs = attend(raw, cosine, sine, heads, ctx)
    w_out_all = gather_weight(after(w_out, w_qkv))
    w_gate_up = gather_weight(
        after(jnp.concatenate([hidden_columns(w_gate), hidden_columns(w_up)], axis=1), w_out_all)
    )
    down_size = w_down.shape[0] // ctx
    down_share = gather_weight(
        after(lax.dynamic_slice_in_dim(w_down, place * down_size, down_size, 0), w_gate_up)
    )
    cotangent_all = gather_rows(after(cotangent, tokens_all))

    inputs = tokens.astype(F32)
    mixed_own = lax.all_to_all(mixed, "ctx", 0, 0, tiled=True).reshape(width, -1)
    middle = inputs + dot(mixed_own, w_out_all, 0, 0)
    normed_mid, scale_mid = norm_parts(middle)
    second_all = gather_rows((normed_mid * gain_two).astype(BF))
    gate_up = dot(second_all, w_gate_up, 1, 0)
    gate, upward = gate_up[:, :share], gate_up[:, share:]
    grad_hidden = dot(cotangent_all, down_share, 1, 1)
    sigmoid = jax.nn.sigmoid(gate)
    hidden = (gate * sigmoid * upward).astype(BF)
    grad_gate = (grad_hidden * upward * (sigmoid + gate * sigmoid * (1.0 - sigmoid))).astype(BF)
    grad_up = (grad_hidden * (gate * sigmoid)).astype(BF)
    grad_gate_up = jnp.concatenate([grad_gate, grad_up], axis=1)
    grad_second = scatter_rows(dot(grad_gate_up, w_gate_up, 1, 1))
    output = (middle + scatter_rows(after(dot(hidden, down_share, 1, 0), grad_second))).astype(BF)

    gain_mlp_term = jnp.sum(grad_second * normed_mid, axis=0)
    grad_middle = cotangent.astype(F32) + norm_back(grad_second * gain_two, normed_mid, scale_mid)
    grad_branch = grad_middle.astype(BF)
    grad_mixed_own = dot(w_out_all, grad_branch, 1, 1).astype(BF)
    grad_mixed = lax.all_to_all(grad_mixed_own.reshape(ctx, part, -1), "ctx", 0, 0, tiled=True)
    grad_raw = attend_back(query, key, value, mixed, grad_mixed, logs, cosine, sine, heads, ctx)
    grad_raw = grad_raw.reshape(-1, length)
    branch_all = gather_rows(after(grad_branch, grad_mixed))
    first_partial = dot(grad_raw, w_qkv, 0, 1)
    grad_first = scatter_rows(first_partial)
    inputs_normed, scale_attn = norm_parts(inputs)
    gain_attn_term = jnp.sum(grad_first * inputs_normed, axis=0)
    input_grad = (grad_middle + norm_back(grad_first * gain_one, inputs_normed, scale_attn)).astype(BF)

    down_grad = scatter(dot(hidden, cotangent_all, 0, 0), "fsdp").astype(F32)
    mixed_rows = mixed.transpose(1, 0, 2).reshape(part, length)
    out_grad = scatter(dot(mixed_rows, branch_all, 1, 0), "fsdp")
    out_grad = lax.ppermute(
        out_grad,
        ("fsdp", "ctx"),
        [(i * ctx + j, j * fsdp + i) for i in range(fsdp) for j in range(ctx)],
    ).astype(F32)
    gate_up_rows = to_owners(dot(second_all, grad_gate_up, 0, 0))
    qkv_rows = to_owners(dot(first_all, grad_raw, 0, 1))
    gain_terms = jnp.stack([gain_attn_term, gain_mlp_term]).reshape(2, fsdp * ctx, own_rows)
    gain_grads = jnp.sum(
        lax.all_to_all(gain_terms.transpose(1, 0, 2), ("fsdp", "ctx"), 0, 0, tiled=True), axis=0
    )
    return (
        output,
        input_grad,
        gain_grads[0],
        of_heads(qkv_rows[:, :, :part]),
        of_heads(qkv_rows[:, :, part : 2 * part]),
        of_heads(qkv_rows[:, :, 2 * part :]),
        out_grad,
        gain_grads[1],
        of_hidden(gate_up_rows[:, :, :share]),
        of_hidden(gate_up_rows[:, :, share:]),
        down_grad,
    )


def together(*items):
    return lax.optimization_barrier(items)


def pick(blocks, index, axis=0):
    return lax.dynamic_index_in_dim(blocks, index, axis, keepdims=False)


def put(blocks, item, index):
    return lax.dynamic_update_slice(blocks, item[None], (index,) + (0,) * item.ndim)


def halves(own, other, index):
    return put(put(jnp.zeros((2,) + own.shape, own.dtype), own, index), other, 1 - index)


def add(*items):
    return sum(item.astype(F32) for item in items)


def swap_x(item):
    return swap(item, "fsdp", 2)


def swap_core(item):
    return swap(item, "fsdp", 1)


def swap_y(item):
    return swap(item, "ctx", 1)


def ring_on(item, steps=1):
    count = lax.axis_size("ctx")
    return lax.ppermute(item, "ctx", [(i, (i + 2 * steps) % count) for i in range(count)])


def columns_kernel(place_ref, gate_ref, up_ref, own_ref, other_ref, *piece_refs):
    step, steps = pl.program_id(0), pl.num_programs(0)
    size, rows = own_ref.shape[1], piece_refs[0].shape[0]
    own = pl.ds(pl.multiple_of(place_ref[1] * size, size), size)
    other = pl.ds(pl.multiple_of((1 - place_ref[1]) * size, size), size)

    def take(weight_ref):
        own_ref[...] = weight_ref[:, own]
        other_ref[...] = weight_ref[:, other]
        for i, piece_ref in enumerate(piece_refs):
            start = pl.multiple_of((2 * place_ref[2] + i % 2) * rows, rows)
            piece_ref[...] = weight_ref[pl.ds(start, rows), own if i < 2 else other]

    @pl.when(step < steps // 2)
    def _():
        take(gate_ref)

    @pl.when(step >= steps // 2)
    def _():
        take(up_ref)


def shared_columns(w_gate, w_up, place, ctx):
    rows, columns = w_gate.shape
    blocks = lax.axis_size("fsdp")
    size = columns // (ctx * blocks)
    pairs = ctx // 2
    gate = pl.BlockSpec((rows, 2 * size), lambda s, at: (0, jnp.minimum(s, blocks - 1) * pairs + at[0]))
    up = pl.BlockSpec((rows, 2 * size), lambda s, at: (0, jnp.maximum(s - blocks, 0) * pairs + at[0]))
    counts = (rows, rows) + (rows // 4,) * 4
    wide = 2 * blocks * size
    return pl.pallas_call(
        columns_kernel,
        grid_spec=pltpu.PrefetchScalarGridSpec(
            num_scalar_prefetch=1,
            grid=(2 * blocks,),
            in_specs=[gate, up],
            out_specs=[pl.BlockSpec((count, size), lambda s, at: (0, s)) for count in counts],
        ),
        out_shape=[jax.ShapeDtypeStruct((count, wide), BF) for count in counts],
        compiler_params=pltpu.CompilerParams(vmem_limit_bytes=56 * 1024 * 1024),
        name="columns",
    )(place, w_gate, w_up)


def mlp_back(second, cotangent, w_gate_up, down_share):
    share = down_share.shape[0]
    gate_up = dot(second, w_gate_up, 1, 0)
    gate, upward = gate_up[:, :share], gate_up[:, share:]
    grad_hidden = dot(cotangent, down_share, 1, 1)
    sigmoid = jax.nn.sigmoid(gate)
    hidden = (gate * sigmoid * upward).astype(BF)
    grad_gate = (grad_hidden * upward * (sigmoid + gate * sigmoid * (1.0 - sigmoid))).astype(BF)
    grad_up = (grad_hidden * (gate * sigmoid)).astype(BF)
    both = jnp.concatenate([grad_gate, grad_up], axis=1)
    return hidden, grad_gate, grad_up, dot(both, w_gate_up, 1, 1).astype(BF)


def paired_body(
    tokens, gain_attn, w_query, w_key, w_value, w_out, gain_mlp, w_gate, w_up, w_down, cotangent
):
    rows, width = tokens.shape
    fsdp, ctx = lax.axis_size("fsdp"), lax.axis_size("ctx")
    place, fsdp_place = lax.axis_index("ctx"), lax.axis_index("fsdp")
    x_bit, core, ring, y_bit = fsdp_place // 2, fsdp_place & 1, place // 2, place & 1
    index = 2 * ring + core
    hops = ctx // 2
    length = rows * ctx
    heads = HEADS // ctx
    part = width // ctx
    share = w_gate.shape[1] // ctx
    own_rows = width // (fsdp * ctx)
    cosine, sine = angle_tables(length, width // HEADS)

    def block_of(hop):
        return 2 * lax.rem(ring + hops - hop, hops) + y_bit

    def blank(shape, *wait):
        return jnp.broadcast_to(together(jnp.zeros((), BF), *wait)[0], shape)

    def place_rows(buffer, item, index):
        return put(buffer, item, fsdp_place ^ index)

    def row_at(buffer, index, piece=0):
        return (buffer.shape[0] // 4) * (fsdp_place ^ index) + piece

    def put_piece(buffer, item, index, piece):
        return put(buffer, item, row_at(buffer, index, piece))

    def put_whole(buffer, item, index):
        return lax.dynamic_update_slice(buffer, item.reshape((-1,) + buffer.shape[1:]), (row_at(buffer, index), 0, 0))

    def finish(buffer, item, index, piece):
        here = lax.broadcasted_iota(jnp.int32, (buffer.shape[0], 1, 1), 0) == row_at(buffer, index, piece)
        return jnp.where(here, item[None], buffer).reshape(-1, buffer.shape[2])

    straight = lambda i: 2 * y_bit + i
    crossed = lambda i: 2 * (1 - y_bit) + i

    piece = jnp.concatenate(
        [lax.dynamic_slice_in_dim(item, place * part, part, 1) for item in (w_query, w_key, w_value)], axis=1
    )
    gains = jnp.stack([gain_attn, gain_mlp]).reshape(8, -1)
    z, y = ring_on(tokens), swap_y(tokens)
    gains_far, gains_near = swap_x(gains), swap_core(gains)
    qkv_far = swap_x(piece)
    w_qkv = place_rows(blank((4,) + piece.shape), piece, 0)

    t, y, gains_far, gains_near = together(z, y, gains_far, gains_near)
    hop_1, y_0 = t, y
    z, y = ring_on(hop_1), swap_y(hop_1)
    gains_last = swap_core(gains_far)
    quarter = w_out.shape[0] // 4
    out_a, out_b = [
        lax.dynamic_slice_in_dim(after(w_out, t), straight(i) * quarter, quarter, 0) for i in range(2)
    ]
    own, other, own_a, own_b, other_a, other_b = shared_columns(
        after(w_gate, t), w_up, jnp.stack([ring, core, y_bit]).astype(jnp.int32), ctx
    )

    t, y, gains_last, qkv_far, out_a, out_b, own_a, own_b, other_a, other_b = together(
        z, y, gains_last, qkv_far, out_a, out_b, own_a, own_b, other_a, other_b
    )
    hop_2, y_1 = t, y
    z, y = ring_on(hop_2), swap_y(hop_2)
    out_ax = swap_x(out_a)
    qkv_near, qkv_last = swap_core(after(piece, t)), swap_core(qkv_far)
    gains_all = blank((4,) + gains.shape)
    for i, item in enumerate((gains, gains_near, gains_far, gains_last)):
        gains_all = place_rows(gains_all, item, i)
    gains_all = gains_all.reshape(4, 2, -1).transpose(1, 0, 2).reshape(2, width).astype(F32)
    gain_one, gain_two = gains_all[0], gains_all[1]
    first_all = blank((ctx,) + tokens.shape, t)

    def take_rows(buffer, item, hop, mate):
        normed = (norm_parts(item.astype(F32))[0] * gain_one).astype(BF)
        return put(buffer, normed, block_of(hop) ^ mate)

    for item, hop, mate in ((tokens, 0, 0), (y_0, 0, 1), (hop_1, 1, 0), (y_1, 1, 1)):
        first_all = take_rows(first_all, item, hop, mate)

    t, y, qkv_near, qkv_last, first_all, out_ax = together(z, y, qkv_near, qkv_last, first_all, out_ax)
    hop_3 = t
    for item, hop, mate in ((hop_2, 2, 0), (y, 2, 1), (hop_3, 3, 0)):
        first_all = take_rows(first_all, item, hop, mate)
    y = swap_y(hop_3)
    cot_1 = ring_on(after(cotangent, t))
    out_bx, own_ax = swap_x(after(out_b, t)), swap_x(after(own_a, t))
    for i, item in enumerate((qkv_near, qkv_far, qkv_last)):
        w_qkv = place_rows(w_qkv, item, i + 1)
    w_qkv = w_qkv.reshape(width, -1)

    t, cot_1, out_bx, own_ax, w_qkv, first_all = together(y, cot_1, out_bx, own_ax, w_qkv, first_all)
    out_ay = swap_y(out_ax)
    cot_2 = ring_on(cot_1)
    out_al = swap_core(out_ax)
    own_bx = swap_x(after(own_b, t))
    first_all = take_rows(first_all, t, 3, 1).reshape(length, width)
    raw = dot(w_qkv, first_all, 0, 1)
    mixed, query, key, value, logs = attend(raw, cosine, sine, heads, ctx)

    t, out_al, out_ay, cot_2, own_bx = together(mixed, out_al, out_ay, cot_2, own_bx)
    mixed_own = lax.all_to_all(t, "ctx", 0, 0, tiled=True)
    size = w_down.shape[0] // (2 * ctx)
    down_wait = after(w_down, t)
    down_own, down_other = [
        lax.dynamic_slice_in_dim(down_wait, 2 * i * size, 2 * size, 0) for i in (index, index ^ 1)
    ]
    out_near = swap_core(after(w_out, t))
    out_by = swap_y(after(out_bx, t))
    other_ax = swap_x(after(other_a, t))
    w_out_all = blank((16, quarter, width), t)
    w_out_all = put_whole(w_out_all, w_out, 0)
    for i, item, source in ((0, out_ax, 2), (1, out_bx, 2), (0, out_al, 3)):
        w_out_all = put_piece(w_out_all, item, source, straight(i))
    w_out_all = put_piece(w_out_all, out_ay, 2, crossed(0))
    w_gate_up = blank((16,) + own_a.shape, t)
    w_gate_up = put_whole(w_gate_up, own, 0)
    w_gate_up = put_piece(w_gate_up, own_ax, 2, straight(0))
    w_gate_up = put_piece(w_gate_up, own_bx, 2, straight(1))

    t, out_by, out_near, other_ax, w_out_all, w_gate_up, down_own, down_other = together(
        mixed_own, out_by, out_near, other_ax, w_out_all, w_gate_up, down_own, down_other
    )
    out_bl, out_ayl, out_byl = [swap_core(item) for item in (after(out_bx, t), after(out_ay, t), out_by)]
    own_ay = swap_y(after(own_ax, t))
    other_bx = swap_x(after(other_b, t))
    cot_3 = ring_on(after(cot_2, t))
    w_out_all = put_whole(w_out_all, out_near, 1)
    w_out_all = put_piece(w_out_all, out_by, 2, crossed(1))
    w_out_all = put_piece(w_out_all, out_bl, 3, straight(1))
    w_out_all = put_piece(w_out_all, out_ayl, 3, crossed(0))
    w_out_all = put_piece(w_out_all, out_byl, 3, crossed(1)).reshape(width, width)
    mixed_own = t.reshape(width, rows)
    inputs = tokens.astype(F32)
    middle = inputs + dot(mixed_own, w_out_all, 0, 0)
    normed_mid, scale_mid = norm_parts(middle)
    second = (normed_mid * gain_two).astype(BF)

    t, own_ay, other_bx = together(second, own_ay, other_bx)
    z, near = ring_on(t), swap_core(t)
    own_by = swap_y(after(own_bx, t))
    down_ax = swap_x(after(down_own[:size], t))
    gate_up_near = swap_core(after(other, t))
    second_all = put(blank((2 * hops, rows, width), t), second, 0)
    cot_all = put(blank((2 * hops, rows, width), t), cotangent, 0)
    w_gate_up = put_piece(w_gate_up, own_ay, 2, crossed(0))

    t, near, own_by, cot_3, gate_up_near, second_all, cot_all, w_gate_up, down_ax = together(
        z, near, own_by, cot_3, gate_up_near, second_all, cot_all, w_gate_up, down_ax
    )
    z, near_1 = ring_on(t), swap_core(t)
    other_ay = swap_y(after(other_ax, t))
    down_bx = swap_x(after(down_own[size:], t))
    other_al, cot_near = swap_core(after(other_ax, t)), swap_core(after(cotangent, t))
    second_all = put(put(second_all, near, 1), t, 2)
    w_gate_up = put_whole(w_gate_up, gate_up_near, 1)
    w_gate_up = put_piece(w_gate_up, own_by, 2, crossed(1))
    down_share = put_whole(blank((8,) + down_ax.shape, t), down_own, 0)

    t, near_1, other_ay, down_bx, other_al, cot_near, second_all, w_gate_up, down_share = together(
        z, near_1, other_ay, down_bx, other_al, cot_near, second_all, w_gate_up, down_share
    )
    hop_2 = t
    z, near_2 = ring_on(t), swap_core(t)
    other_by = swap_y(after(other_bx, t))
    down_cx = swap_x(after(down_other[:size], t))
    down_near, other_bl, cot_near_1 = [swap_core(after(item, t)) for item in (down_other, other_bx, cot_1)]
    second_all = put(put(second_all, near_1, 3), t, 4)
    cot_all = put(put(cot_all, cot_near, 1), cot_1, 2)
    cot_all = put(put(cot_all, cot_2, 4), cot_3, 6)
    w_gate_up = put_piece(w_gate_up, other_al, 3, straight(0))
    down_share = put(put(down_share, down_ax, row_at(down_share, 2)), down_bx, row_at(down_share, 2, 1))

    t, near_2, other_by, down_cx, down_near, other_bl, cot_near_1, second_all, cot_all, w_gate_up, down_share = (
        together(
            z, near_2, other_by, down_cx, down_near, other_bl, cot_near_1, second_all, cot_all, w_gate_up, down_share
        )
    )
    down_dx = swap_x(after(down_other[size:], t))
    near_3, other_ayl, other_byl, down_cl, cot_near_2, cot_near_3 = [
        swap_core(item)
        for item in (t, after(other_ay, t), other_by, down_cx, after(cot_2, t), after(cot_3, t))
    ]
    second_all = put(put(second_all, near_2, 5), t, 6)
    cot_all = put(cot_all, cot_near_1, 3)
    w_gate_up = put_piece(w_gate_up, other_bl, 3, straight(1))
    w_gate_up = put_piece(w_gate_up, other_ayl, 3, crossed(0))
    down_share = put_whole(down_share, down_near, 1)
    down_share = put(down_share, down_cl, row_at(down_share, 3))
    second_all = put(second_all, near_3, 7).reshape(length, width)
    cot_all = put(put(cot_all, cot_near_2, 5), cot_near_3, 7).reshape(length, width)
    t, down_dx, second_all, cot_all, w_gate_up, down_share, other_byl = together(
        near_3, down_dx, second_all, cot_all, w_gate_up, down_share, other_byl
    )
    down_dl = swap_core(down_dx)
    w_gate_up = finish(w_gate_up, other_byl, 3, crossed(1))
    down_share = finish(down_share, down_dl, 3, 1)

    back = [None] * hops
    buffers = [blank((hops, 2 * rows, share), t) for _ in range(3)]
    chunk = lambda matrix, hop: matrix[2 * hop * rows : 2 * (hop + 1) * rows]

    def run_chunk(hop, buffers, *wait):
        rows_in = after(chunk(second_all, hop), *wait) if wait else chunk(second_all, hop)
        *items, back[hop] = mlp_back(rows_in, chunk(cot_all, hop), w_gate_up, down_share)
        return [put(buffer, item, hop) for buffer, item in zip(buffers, items)]

    buffers = run_chunk(1, buffers)
    near_1 = swap_core(back[1][rows:])
    t = add(back[1][:rows], near_1).astype(BF)
    z = ring_on(t)
    buffers = run_chunk(2, buffers, t)
    near_2 = swap_core(back[2][rows:])
    buffers = run_chunk(3, buffers, t)
    near_3 = swap_core(back[3][rows:])
    z, near_2, near_3, *buffers = together(z, near_2, near_3, *buffers)
    t = add(back[2][:rows], near_2, z).astype(BF)
    z = ring_on(t)
    hidden, grad_gate, grad_up = [item.reshape(length, share) for item in run_chunk(0, buffers, t)]
    near_0 = swap_core(back[0][rows:])
    gate_partial = dot(second_all, grad_gate, 0, 0).astype(BF)
    z, near_0, gate_partial = together(z, near_0, gate_partial)
    t = add(back[3][:rows], near_3, z).astype(BF)
    z = ring_on(t)

    def given(blocks, bit, dim):
        return pick(blocks, 1 - bit, dim)

    def kept(blocks, bit, dim, arrived):
        return add(pick(blocks, bit, dim), arrived).astype(BF)

    def row_blocks(matrix):
        return matrix.reshape(2, 2, hops, 2, own_rows, -1)

    gate_blocks = row_blocks(gate_partial)
    gate_x = swap_x(given(gate_blocks, x_bit, 0))
    up_partial = dot(after(second_all, t), grad_up, 0, 0).astype(BF)
    up_given = given(row_blocks(up_partial), x_bit, 0)
    t, up_partial, up_given, hidden = together(z, up_partial, up_given, hidden)

    grad_second = add(back[0][:rows], near_0, t)
    gain_mlp_term = jnp.sum(grad_second * normed_mid, axis=0)
    grad_middle = cotangent.astype(F32) + norm_back(grad_second * gain_two, normed_mid, scale_mid)
    grad_branch = grad_middle.astype(BF)
    grad_mixed_own = dot(w_out_all, grad_branch, 1, 1).astype(BF)

    t, hidden = together(grad_mixed_own, hidden)
    grad_mixed = lax.all_to_all(t.reshape(ctx, part, -1), "ctx", 0, 0, tiled=True)
    out_partial = dot(hidden, down_share, 1, 0).astype(BF)
    out = [chunk(out_partial, hop) for hop in range(hops)]
    out_near_1 = swap_core(out[1][rows:])
    out_weight = row_blocks(dot(mixed_own, after(grad_branch, t), 1, 0).astype(BF))
    weight_near = swap_core(given(out_weight, core, 1))

    t, weight_near, out_weight, out_near_1, out_partial, gate_x, hidden = together(
        grad_mixed, weight_near, out_weight, out_near_1, out_partial, gate_x, hidden
    )
    up_x = swap_x(up_given)
    out = [chunk(out_partial, hop) for hop in range(hops)]
    out_sum = add(out[1][:rows], out_near_1).astype(BF)
    out_z = ring_on(out_sum)
    out_near_2 = swap_core(after(out[2][rows:], t))
    grad_raw = attend_back(query, key, value, mixed, t, logs, cosine, sine, heads, ctx)
    grad_raw = grad_raw.reshape(-1, length)
    first_partial = dot(grad_raw, w_qkv, 0, 1).astype(BF)

    t, out_z, out_near_2, grad_raw = together(first_partial, out_z, out_near_2, grad_raw)
    first_blocks = t.reshape(ctx, rows, width)
    first_own = lambda hop: pick(first_blocks, block_of(hop))
    first_other = lambda hop: pick(first_blocks, block_of(hop) ^ 1)
    y = swap_y(first_other(1))
    out_sum = add(out[2][:rows], out_near_2, out_z).astype(BF)
    out_z = ring_on(out_sum)
    out_near_3 = swap_core(after(out[3][rows:], t))
    head_partial = dot(after(first_all, t), grad_raw, 0, 1).astype(BF).reshape(2, 2, ctx * own_rows, -1)
    head_near = swap_core(given(head_partial, core, 1))
    gate_sum = kept(gate_blocks, x_bit, 0, gate_x)
    gate_given = given(gate_sum, y_bit, 2)

    t, out_near_3, head_partial, head_near, gate_given, gate_sum, out_z, up_x = together(
        y, out_near_3, head_partial, head_near, gate_given, gate_sum, out_z, up_x
    )
    total = add(first_own(1), t).astype(BF)
    z, y = ring_on(total), swap_y(after(first_other(2), t))
    gate_y = swap_y(gate_given)
    weight = kept(out_weight, core, 1, weight_near)
    weight_x = swap_x(given(weight, x_bit, 0))
    out_sum = add(out[3][:rows], out_near_3, out_z).astype(BF)
    down_partial = dot(hidden, after(cot_all, t), 0, 0).astype(BF)

    t, y, out_sum, down_partial, weight = together(z, y, out_sum, down_partial, weight)
    total = add(first_own(2), y, t).astype(BF)
    z, y = ring_on(total), swap_y(after(first_other(3), t))
    out_near_0 = swap_core(after(out[0][rows:], t))
    head_sum = kept(head_partial, core, 1, head_near)
    head_given = given(head_sum, x_bit, 0)
    up_sum = kept(row_blocks(up_partial), x_bit, 0, up_x)
    up_given = given(up_sum, y_bit, 2)

    t, y, gate_y, up_given, up_sum, head_given, head_sum, weight_x, out_near_0 = together(
        z, y, gate_y, up_given, up_sum, head_given, head_sum, weight_x, out_near_0
    )
    total = add(first_own(3), y, t).astype(BF)
    z, y = ring_on(total), swap_y(after(first_other(0), t))
    out_z = ring_on(out_sum)
    head_x = swap_x(head_given)
    gate_sum = kept(gate_sum, y_bit, 2, gate_y)
    gate_near = swap_core(pick(gate_sum, 1 - core))
    weight = kept(weight, x_bit, 0, weight_x)
    weight_given = given(weight, y_bit, 1)

    t, y, gate_near, gate_sum, weight, weight_given, head_x = together(
        z, y, gate_near, gate_sum, weight, weight_given, head_x
    )
    grad_first = add(first_own(0), y, t)
    weight_y = swap_y(weight_given)
    up_y = swap_y(after(up_given, t))
    down_blocks = down_partial.reshape(2, 2, -1, width)
    down_x = swap_x(after(given(down_blocks, x_bit, 0), t))
    inputs_normed, scale_attn = norm_parts(inputs)
    gain_attn_term = jnp.sum(grad_first * inputs_normed, axis=0)
    input_grad = (grad_middle + norm_back(grad_first * gain_one, inputs_normed, scale_attn)).astype(BF)
    output = (middle + add(out[0][:rows], out_near_0, out_z)).astype(BF)
    head_rows = kept(head_sum, x_bit, 0, head_x)

    def deal_rows(summed, near):
        pair = halves(pick(summed, core), near, core)
        received = put(jnp.zeros((hops, 2) + pair.shape[2:], BF), pick(pair, ring, 1), ring)
        for steps in range(1, hops):
            arriving = ring_on(pick(pair, lax.rem(ring + steps, hops), 1), steps)
            received = put(received, arriving, lax.rem(ring + hops - steps, hops))
        blocks = received.astype(F32).reshape(ctx, own_rows, fsdp, -1)
        return blocks.transpose(1, 2, 0, 3).reshape(own_rows, -1)

    gate_grad = deal_rows(gate_sum, gate_near)
    up_sum = kept(up_sum, y_bit, 2, up_y)
    up_grad = deal_rows(up_sum, swap_core(pick(up_sum, 1 - core)))

    summed = kept(down_blocks, x_bit, 0, down_x)
    pairs = [(i * ctx + j, i * ctx + (j ^ 1)) for i in range(fsdp) for j in range(ctx) if (i ^ j) & 1]
    summed = add(summed, lax.ppermute(summed, ("fsdp", "ctx"), pairs)).astype(BF)
    near = swap_core(pick(summed, 1 - core))
    down_grad = jnp.where(core == y_bit, pick(summed, core), near).astype(F32)

    weight = kept(weight, y_bit, 1, weight_y)
    total = pick(weight, block_of(1) // 2)
    for hop in (2, 3, 0):
        total = add(pick(weight, block_of(hop) // 2), ring_on(total.astype(BF)))
    out_grad = total

    head_rows = lax.all_to_all(head_rows, "ctx", 0, 0, tiled=True).reshape(ctx, own_rows, -1).astype(F32)
    query_grad, key_grad, value_grad = [
        head_rows[:, :, i * part : (i + 1) * part].transpose(1, 0, 2).reshape(own_rows, -1) for i in range(3)
    ]

    gain_terms = jnp.stack([gain_attn_term, gain_mlp_term]).reshape(2, fsdp * ctx, own_rows)
    gain_grads = jnp.sum(
        lax.all_to_all(gain_terms.transpose(1, 0, 2), ("fsdp", "ctx"), 0, 0, tiled=True), axis=0
    )
    return (
        output,
        input_grad,
        gain_grads[0],
        query_grad,
        key_grad,
        value_grad,
        out_grad,
        gain_grads[1],
        gate_grad,
        up_grad,
        down_grad,
    )


def solution(mesh):
    both = ("fsdp", "ctx")
    matrix = P("fsdp", None)
    in_specs = (P(both, None), P("fsdp"), matrix, matrix, matrix, matrix, P("fsdp"), matrix, matrix, matrix, P(both, None))
    rows = P(both, None)
    out_specs = (rows, rows, P(both), rows, rows, rows, rows, P(both), rows, rows, rows)
    body = paired_body if mesh.shape["fsdp"] == 4 and mesh.shape["ctx"] == 8 else general_body
    return jax.shard_map(body, mesh=mesh, in_specs=in_specs, out_specs=out_specs, check_vma=False)
```

```python
import functools

import jax
import jax.numpy as jnp
import numpy as np
from jax import lax
from jax.experimental import pallas as pl
from jax.experimental.pallas import tpu as pltpu
from jax.sharding import PartitionSpec as P

HEADS = 32
EPS = 1e-05
THETA = 130000.0
MASKED = -1e30
BF = jnp.bfloat16
F32 = jnp.float32


def dot(left, right, left_axis, right_axis):
    return lax.dot_general(
        left, right, (((left_axis,), (right_axis,)), ((), ())), preferred_element_type=F32
    )


def norm_parts(matrix):
    scale = lax.rsqrt(jnp.mean(matrix * matrix, axis=-1, keepdims=True) + EPS)
    return (matrix * scale, scale)


def norm_back(grad_scaled, normed, scale):
    return scale * (grad_scaled - normed * jnp.mean(grad_scaled * normed, axis=-1, keepdims=True))


def angle_tables(length, head_width):
    half = head_width // 2
    freqs = np.float32(THETA) ** (-(np.arange(half, dtype=np.float32) * np.float32(2.0 / head_width)))
    angles = freqs[:, None].astype(np.float32) * np.arange(length, dtype=np.float32)[None, :]
    return jnp.asarray(np.cos(angles), F32), jnp.asarray(np.sin(angles), F32)


def low_lanes(block):
    return lax.broadcasted_iota(jnp.int32, block.shape, 1) < block.shape[1] // 2


def sort_columns(matrix, blocks):
    size = matrix.shape[1] // blocks
    early, late = [], []
    for j in range(blocks // 2):
        first = matrix[:, 2 * j * size : (2 * j + 1) * size]
        second = pltpu.roll(matrix[:, (2 * j + 1) * size : (2 * j + 2) * size], size // 2, 1)
        low = low_lanes(first)
        early.append(jnp.where(low, first, second))
        late.append(jnp.where(low, second, first))
    return jnp.concatenate(early + late[::-1], axis=1)


def deal_columns(matrix, blocks):
    size = matrix.shape[1] // blocks
    out = []
    for j in range(blocks // 2):
        early = matrix[:, j * size : (j + 1) * size]
        late = matrix[:, (blocks - 1 - j) * size : (blocks - j) * size]
        low = low_lanes(early)
        out.append(jnp.where(low, early, late))
        out.append(pltpu.roll(jnp.where(low, late, early), size // 2, 1))
    return jnp.concatenate(out, axis=1)


def turn(matrix, cosine, sine):
    half = matrix.shape[0] // 2
    first, second = matrix[:half], matrix[half:]
    return jnp.concatenate([first * cosine - second * sine, second * cosine + first * sine], axis=0)


def by_blocks(ref):
    return jnp.concatenate([ref[block].astype(F32) for block in range(ref.shape[0])], axis=1)


def masked_block(scores, chunk):
    keys = scores.shape[0]
    places = lax.broadcasted_iota(jnp.int32, (chunk, chunk), 0)
    wants = lax.broadcasted_iota(jnp.int32, (chunk, chunk), 1)
    last = jnp.where(places <= wants, scores[keys - chunk :], MASKED)
    if keys == chunk:
        return last
    return jnp.concatenate([scores[: keys - chunk], last], axis=0)


def attend_kernel(blocks, chunk, q_ref, k_ref, v_ref, cos_ref, sin_ref, o_ref, qs_ref, ks_ref, vs_ref, lse_ref):
    width, length = q_ref.shape
    cosine, sine = cos_ref[...], sin_ref[...]
    query = turn(sort_columns(q_ref[...], blocks), cosine, sine).astype(BF)
    key = turn(sort_columns(k_ref[...], blocks), cosine, sine).astype(BF)
    value = sort_columns(v_ref[...], blocks).astype(BF)
    scaled = query * jnp.asarray(width ** (-0.5), BF)
    qs_ref[...] = scaled
    ks_ref[...] = key
    vs_ref[...] = value
    mixed, logs = [], []
    for i in range(length // chunk):
        count = (i + 1) * chunk
        scores = dot(key[:, :count], scaled[:, i * chunk : count], 0, 0)
        scores = masked_block(scores, chunk)
        top = jnp.max(scores, axis=0, keepdims=True)
        raised = jnp.exp(scores - top)
        total = jnp.sum(raised, axis=0, keepdims=True)
        mixed.append(dot(value[:, :count], raised.astype(BF), 1, 0) / total)
        logs.append(top + jnp.log(total))
    size = length // blocks
    dealt = deal_columns(jnp.concatenate(mixed, axis=1), blocks).astype(BF)
    for block in range(blocks):
        o_ref[block] = dealt[:, block * size : (block + 1) * size]
    lse_ref[0] = jnp.concatenate(logs, axis=1)


def attend_back_kernel(blocks, chunk, q_ref, k_ref, v_ref, o_ref, do_ref, lse_ref, cos_ref, sin_ref, d_ref, dk_ref, dv_ref):
    width, length = q_ref.shape
    factor = width ** (-0.5)
    cosine, sine = cos_ref[...], -sin_ref[...]
    scaled, key, value = q_ref[...], k_ref[...], v_ref[...]
    grad_f32 = sort_columns(by_blocks(do_ref), blocks)
    center = jnp.sum(grad_f32 * sort_columns(by_blocks(o_ref), blocks), axis=0, keepdims=True)
    grad = grad_f32.astype(BF)
    logs = lse_ref[0]
    dq = []
    for i in reversed(range(length // chunk)):
        count = (i + 1) * chunk
        here = slice(i * chunk, count)
        scores = masked_block(dot(key[:, :count], scaled[:, here], 0, 0), chunk)
        shares = jnp.exp(scores - logs[:, here])
        grad_shares = dot(value[:, :count], grad[:, here], 0, 0)
        grad_scores = (shares * (grad_shares - center[:, here])).astype(BF)
        dq.append(dot(key[:, :count], grad_scores, 1, 0))
        dk_part = dot(scaled[:, here], grad_scores, 1, 1)
        dv_part = dot(grad[:, here], shares.astype(BF), 1, 1)
        if count == length:
            dk_ref[...] = dk_part
            dv_ref[...] = dv_part
        else:
            dk_ref[:, :count] += dk_part
            dv_ref[:, :count] += dv_part
    dq = turn(jnp.concatenate(dq[::-1], axis=1) * factor, cosine, sine)
    d_ref[0] = deal_columns(dq, blocks).astype(BF)
    d_ref[1] = deal_columns(turn(dk_ref[...], cosine, sine), blocks).astype(BF)
    d_ref[2] = deal_columns(dv_ref[...], blocks).astype(BF)


def attend(raw, cosine, sine, heads, blocks):
    width, length = 2 * cosine.shape[0], raw.shape[1]
    chunk = min(256, length)
    head = lambda shift: pl.BlockSpec((width, length), lambda h: (h + shift * heads, 0))
    table = pl.BlockSpec((width // 2, length), lambda h: (0, 0))
    flat = jax.ShapeDtypeStruct((heads * width, length), BF)
    return pl.pallas_call(
        functools.partial(attend_kernel, blocks, chunk),
        grid=(heads,),
        in_specs=[head(0), head(1), head(2), table, table],
        out_specs=[
            pl.BlockSpec((blocks, width, length // blocks), lambda h: (0, h, 0)),
            head(0),
            head(0),
            head(0),
            pl.BlockSpec((1, 1, length), lambda h: (h, 0, 0)),
        ],
        out_shape=[
            jax.ShapeDtypeStruct((blocks, heads * width, length // blocks), BF),
            flat,
            flat,
            flat, jax.ShapeDtypeStruct((heads, 1, length), F32),
        ],
        compiler_params=pltpu.CompilerParams(vmem_limit_bytes=40 * 1024 * 1024),
        name="attend",
    )(raw, raw, raw, cosine, sine)


def attend_back(query, key, value, mixed, grad, logs, cosine, sine, heads, blocks):
    width, length = query.shape[0] // heads, query.shape[1]
    chunk = min(256, length)
    head = pl.BlockSpec((width, length), lambda h: (h, 0))
    block = pl.BlockSpec((blocks, width, length // blocks), lambda h: (0, h, 0))
    table = pl.BlockSpec((width // 2, length), lambda h: (0, 0))
    return pl.pallas_call(
        functools.partial(attend_back_kernel, blocks, chunk),
        grid=(heads,),
        in_specs=[head, head, head, block, block, pl.BlockSpec((1, 1, length), lambda h: (h, 0, 0)), table, table],
        out_specs=pl.BlockSpec((3, width, length), lambda h: (0, h, 0)),
        out_shape=jax.ShapeDtypeStruct((3, heads * width, length), BF),
        scratch_shapes=[pltpu.VMEM((width, length), F32), pltpu.VMEM((width, length), F32)],
        compiler_params=pltpu.CompilerParams(vmem_limit_bytes=40 * 1024 * 1024),
        name="attend_back",
    )(query, key, value, mixed, grad, logs, cosine, sine)


def swap(item, axis, bit):
    pairs = [(i, i ^ bit) for i in range(lax.axis_size(axis))]
    return lax.ppermute(item, axis, pairs)


def step_on(item):
    count = lax.axis_size("ctx")
    return lax.ppermute(item, "ctx", [(i, (i + 2) % count) for i in range(count)])


def after(item, *others):
    return lax.optimization_barrier((item,) + others)[0]


def gather_rows(piece):
    count, place = lax.axis_size("ctx"), lax.axis_index("ctx")
    rows = jnp.zeros((count,) + piece.shape, piece.dtype)
    for hop in range(count // 2):
        if hop:
            piece = step_on(piece)
        source = lax.rem(place + count - 2 * hop, count)
        rows = lax.dynamic_update_slice(rows, piece[None], (source, 0, 0))
        rows = lax.dynamic_update_slice(rows, swap(piece, "ctx", 1)[None], (source ^ 1, 0, 0))
    return rows.reshape(-1, rows.shape[2])


def scatter_rows(partial):
    count, place = lax.axis_size("ctx"), lax.axis_index("ctx")
    blocks = partial.astype(BF).reshape(count, -1, partial.shape[1])
    total = None
    for hop in range(1, count // 2 + 1):
        target = lax.rem(place + count - 2 * hop, count)
        mine = lax.dynamic_index_in_dim(blocks, target, 0, keepdims=False)
        other = lax.dynamic_index_in_dim(blocks, target ^ 1, 0, keepdims=False)
        term = mine.astype(F32) + swap(other, "ctx", 1).astype(F32)
        total = term if total is None else term + total.astype(F32)
        if hop < count // 2:
            total = step_on(total.astype(BF))
    return total


def gather_weight(piece):
    if lax.axis_size("fsdp") != 4:
        return lax.all_gather(piece, "fsdp", axis=0, tiled=True)
    place = lax.axis_index("fsdp")
    rows = jnp.zeros((4,) + piece.shape, piece.dtype)
    far = swap(piece, "fsdp", 2)
    for source, item in (
        (place, piece),
        (place ^ 1, swap(piece, "fsdp", 1)),
        (place ^ 2, far),
        (place ^ 3, swap(far, "fsdp", 1)),
    ):
        rows = lax.dynamic_update_slice(rows, item[None], (source, 0, 0))
    return rows.reshape(-1, piece.shape[1])


def scatter(partial, axis):
    return lax.psum_scatter(partial.astype(BF), axis, scatter_dimension=0, tiled=True)


def general_body(
    tokens, gain_attn, w_query, w_key, w_value, w_out, gain_mlp, w_gate, w_up, w_down, cotangent
):
    width = tokens.shape[1]
    hidden_width = w_gate.shape[1]
    fsdp, ctx = lax.axis_size("fsdp"), lax.axis_size("ctx")
    place = lax.axis_index("ctx")
    length = tokens.shape[0] * ctx
    heads = HEADS // ctx
    part = width // ctx
    share = hidden_width // ctx
    own_rows = width // (fsdp * ctx)
    cosine, sine = angle_tables(length, width // HEADS)

    def head_columns(weight):
        return lax.dynamic_slice_in_dim(weight, place * part, part, 1)

    def hidden_columns(weight):
        rows = weight.shape[0]
        blocks = weight.reshape(rows, fsdp, ctx, share // fsdp)
        return lax.dynamic_index_in_dim(blocks, place, 2, keepdims=False).reshape(rows, share)

    def to_owners(partial):
        summed = scatter(partial, "fsdp")
        return lax.all_to_all(summed, "ctx", 0, 0, tiled=True).reshape(ctx, own_rows, -1).astype(F32)

    def of_heads(received):
        return received.transpose(1, 0, 2).reshape(own_rows, -1)

    def of_hidden(received):
        blocks = received.reshape(ctx, own_rows, fsdp, -1)
        return blocks.transpose(1, 2, 0, 3).reshape(own_rows, -1)

    def normed_rows(rows):
        return norm_parts(rows.astype(F32))[0]

    w_qkv_piece = jnp.concatenate([head_columns(item) for item in (w_query, w_key, w_value)], axis=1)
    w_qkv = gather_weight(w_qkv_piece)
    gains = lax.all_gather(jnp.stack([gain_attn, gain_mlp]), "fsdp", axis=1, tiled=True).astype(F32)
    gain_one, gain_two = gains[0], gains[1]
    tokens_all = gather_rows(tokens)
    first_all = (normed_rows(tokens_all) * gain_one).astype(BF)
    raw = dot(w_qkv, first_all, 0, 1)
    mixed, query, key, value, logs = attend(raw, cosine, sine, heads, ctx)
    w_out_all = gather_weight(after(w_out, w_qkv))
    w_gate_up = gather_weight(
        after(jnp.concatenate([hidden_columns(w_gate), hidden_columns(w_up)], axis=1), w_out_all)
    )
    down_size = w_down.shape[0] // ctx
    down_share = gather_weight(
        after(lax.dynamic_slice_in_dim(w_down, place * down_size, down_size, 0), w_gate_up)
    )
    cotangent_all = gather_rows(after(cotangent, tokens_all))

    inputs = tokens.astype(F32)
    mixed_own = lax.all_to_all(mixed, "ctx", 0, 0, tiled=True).reshape(width, -1)
    middle = inputs + dot(mixed_own, w_out_all, 0, 0)
    normed_mid, scale_mid = norm_parts(middle)
    second_all = gather_rows((normed_mid * gain_two).astype(BF))
    gate_up = dot(second_all, w_gate_up, 1, 0)
    gate, upward = gate_up[:, :share], gate_up[:, share:]
    grad_hidden = dot(cotangent_all, down_share, 1, 1)
    sigmoid = jax.nn.sigmoid(gate)
    hidden = (gate * sigmoid * upward).astype(BF)
    grad_gate = (grad_hidden * upward * (sigmoid + gate * sigmoid * (1.0 - sigmoid))).astype(BF)
    grad_up = (grad_hidden * (gate * sigmoid)).astype(BF)
    grad_gate_up = jnp.concatenate([grad_gate, grad_up], axis=1)
    grad_second = scatter_rows(dot(grad_gate_up, w_gate_up, 1, 1))
    output = (middle + scatter_rows(after(dot(hidden, down_share, 1, 0), grad_second))).astype(BF)

    gain_mlp_term = jnp.sum(grad_second * normed_mid, axis=0)
    grad_middle = cotangent.astype(F32) + norm_back(grad_second * gain_two, normed_mid, scale_mid)
    grad_branch = grad_middle.astype(BF)
    grad_mixed_own = dot(w_out_all, grad_branch, 1, 1).astype(BF)
    grad_mixed = lax.all_to_all(grad_mixed_own.reshape(ctx, part, -1), "ctx", 0, 0, tiled=True)
    grad_raw = attend_back(query, key, value, mixed, grad_mixed, logs, cosine, sine, heads, ctx)
    grad_raw = grad_raw.reshape(-1, length)
    branch_all = gather_rows(after(grad_branch, grad_mixed))
    first_partial = dot(grad_raw, w_qkv, 0, 1)
    grad_first = scatter_rows(first_partial)
    inputs_normed, scale_attn = norm_parts(inputs)
    gain_attn_term = jnp.sum(grad_first * inputs_normed, axis=0)
    input_grad = (grad_middle + norm_back(grad_first * gain_one, inputs_normed, scale_attn)).astype(BF)

    down_grad = scatter(dot(hidden, cotangent_all, 0, 0), "fsdp").astype(F32)
    mixed_rows = mixed.transpose(1, 0, 2).reshape(part, length)
    out_grad = scatter(dot(mixed_rows, branch_all, 1, 0), "fsdp")
    out_grad = lax.ppermute(
        out_grad,
        ("fsdp", "ctx"),
        [(i * ctx + j, j * fsdp + i) for i in range(fsdp) for j in range(ctx)],
    ).astype(F32)
    gate_up_rows = to_owners(dot(second_all, grad_gate_up, 0, 0))
    qkv_rows = to_owners(dot(first_all, grad_raw, 0, 1))
    gain_terms = jnp.stack([gain_attn_term, gain_mlp_term]).reshape(2, fsdp * ctx, own_rows)
    gain_grads = jnp.sum(
        lax.all_to_all(gain_terms.transpose(1, 0, 2), ("fsdp", "ctx"), 0, 0, tiled=True), axis=0
    )
    return (
        output,
        input_grad,
        gain_grads[0],
        of_heads(qkv_rows[:, :, :part]),
        of_heads(qkv_rows[:, :, part : 2 * part]),
        of_heads(qkv_rows[:, :, 2 * part :]),
        out_grad,
        gain_grads[1],
        of_hidden(gate_up_rows[:, :, :share]),
        of_hidden(gate_up_rows[:, :, share:]),
        down_grad,
    )


def together(*items):
    return lax.optimization_barrier(items)


def pick(blocks, index, axis=0):
    return lax.dynamic_index_in_dim(blocks, index, axis, keepdims=False)


def put(blocks, item, index):
    return lax.dynamic_update_slice(blocks, item[None], (index,) + (0,) * item.ndim)


def halves(own, other, index):
    return put(put(jnp.zeros((2,) + own.shape, own.dtype), own, index), other, 1 - index)


def add(*items):
    return sum(item.astype(F32) for item in items)


def swap_pair(item, axis):
    return lax.ppermute(item, axis, [(0, 1), (1, 0)])


def swap_x(item):
    return swap_pair(item, "x")


def swap_core(item):
    return swap_pair(item, "core")


def swap_y(item):
    return swap_pair(item, "y")


def ring_on(item, steps=1):
    count = lax.axis_size("z")
    return lax.ppermute(item, "z", [(i, (i + steps) % count) for i in range(count)])


def columns_kernel(place_ref, gate_ref, up_ref, own_ref, other_ref, halves_ref):
    step, steps = pl.program_id(0), pl.num_programs(0)
    size, half = own_ref.shape[1] // 2, halves_ref.shape[0] // 2
    rows = pl.ds(pl.multiple_of(place_ref[2] * half, half), half)

    def take(weight_ref):
        for block in range(2):
            own = pl.ds(pl.multiple_of((2 * block + place_ref[1]) * size, size), size)
            other = pl.ds(pl.multiple_of((2 * block + 1 - place_ref[1]) * size, size), size)
            into = slice(block * size, (block + 1) * size)
            own_ref[:, into] = weight_ref[:, own]
            other_ref[:, into] = weight_ref[:, other]
            halves_ref[:half, into] = weight_ref[rows, own]
            halves_ref[half:, into] = weight_ref[rows, other]

    @pl.when(step < steps // 2)
    def _():
        take(gate_ref)

    @pl.when(step >= steps // 2)
    def _():
        take(up_ref)


def shared_columns(w_gate, w_up, place, blocks, rings):
    rows, columns = w_gate.shape
    size = columns // (blocks * rings * 2)
    gate = pl.BlockSpec((rows, 2 * size), lambda s, at: (0, jnp.minimum(s, blocks - 1) * rings + at[0]))
    up = pl.BlockSpec((rows, 2 * size), lambda s, at: (0, jnp.maximum(s - blocks, 0) * rings + at[0]))
    wide = 2 * blocks * size
    return pl.pallas_call(
        columns_kernel,
        grid_spec=pltpu.PrefetchScalarGridSpec(
            num_scalar_prefetch=1,
            grid=(2 * blocks,),
            in_specs=[gate, up],
            out_specs=[pl.BlockSpec((rows, size), lambda s, at: (0, s))] * 3,
        ),
        out_shape=[jax.ShapeDtypeStruct((rows, wide), BF)] * 3,
        compiler_params=pltpu.CompilerParams(vmem_limit_bytes=56 * 1024 * 1024),
        name="columns",
    )(place, w_gate, w_up)


def mlp_middle(second, cotangent, w_gate_up, down_share):
    share = down_share.shape[0]
    gate_up = dot(second, w_gate_up, 1, 0)
    gate, upward = gate_up[:, :share], gate_up[:, share:]
    grad_hidden = dot(cotangent, down_share, 1, 1)
    sigmoid = jax.nn.sigmoid(gate)
    hidden = (gate * sigmoid * upward).astype(BF)
    grad_gate = (grad_hidden * upward * (sigmoid + gate * sigmoid * (1.0 - sigmoid))).astype(BF)
    grad_up = (grad_hidden * (gate * sigmoid)).astype(BF)
    return hidden, grad_gate, grad_up


def hidden_columns_kernel(in_ref, out_ref):
    cores, rings, _, wide = in_ref.shape
    size = wide // 2
    for ring in range(rings):
        for half in range(2):
            for core in range(cores):
                start = ((ring * 2 + half) * cores + core) * size
                out_ref[:, start : start + size] = in_ref[core, ring, :, half * size : (half + 1) * size].astype(F32)


def hidden_columns(received, blocks):
    cores, rings, rows, share = received.shape
    wide = share // blocks
    return pl.pallas_call(
        hidden_columns_kernel,
        grid=(blocks,),
        in_specs=[pl.BlockSpec((cores, rings, rows, wide), lambda s: (0, 0, 0, s))],
        out_specs=pl.BlockSpec((rows, cores * rings * wide), lambda s: (0, s)),
        out_shape=jax.ShapeDtypeStruct((rows, cores * rings * share), F32),
        compiler_params=pltpu.CompilerParams(vmem_limit_bytes=56 * 1024 * 1024),
        name="hidden_columns",
    )(received)


def head_columns_kernel(in_ref, *out_refs):
    count = in_ref.shape[0]
    part = in_ref.shape[2] // len(out_refs)
    for i, out_ref in enumerate(out_refs):
        for block in range(count):
            out_ref[:, block * part : (block + 1) * part] = in_ref[block, :, i * part : (i + 1) * part].astype(F32)


def head_columns(received):
    count, rows, wide = received.shape
    return pl.pallas_call(
        head_columns_kernel,
        out_shape=[jax.ShapeDtypeStruct((rows, count * wide // 3), F32)] * 3,
        compiler_params=pltpu.CompilerParams(vmem_limit_bytes=56 * 1024 * 1024),
        name="head_columns",
    )(received)


def paired_body(
    tokens, gain_attn, w_query, w_key, w_value, w_out, gain_mlp, w_gate, w_up, w_down, cotangent
):
    rows, width = tokens.shape
    hops = lax.axis_size("z")
    fsdp, ctx = 2 * lax.axis_size("x"), 2 * hops
    x_bit, core, ring, y_bit = [lax.axis_index(axis) for axis in ("x", "core", "z", "y")]
    place, fsdp_place = 2 * ring + y_bit, 2 * x_bit + core
    length = rows * ctx
    heads = HEADS // ctx
    part = width // ctx
    share = w_gate.shape[1] // ctx
    own_rows = width // (fsdp * ctx)
    sequence = ("z", "y")
    cosine, sine = angle_tables(length, width // HEADS)

    def block_of(hop):
        return 2 * lax.rem(ring + hops - hop, hops) + y_bit

    def blank(shape, *wait):
        return jnp.broadcast_to(together(jnp.zeros((), BF), *wait)[0], shape)

    def place_rows(buffer, item, index):
        return put(buffer, item, fsdp_place ^ index)

    def half_at(index, half):
        return 2 * (fsdp_place ^ index) + half

    def put_whole(buffer, item, index):
        return lax.dynamic_update_slice(buffer, item.reshape((2,) + buffer.shape[1:]), (half_at(index, 0), 0, 0))

    piece = jnp.concatenate(
        [lax.dynamic_slice_in_dim(item, place * part, part, 1) for item in (w_query, w_key, w_value)]
        + [jnp.pad(jnp.stack([gain_attn, gain_mlp], axis=1), ((0, 0), (0, 126)))],
        axis=1,
    )
    w_qkv = lax.all_gather(piece, ("x", "core"), axis=0, tiled=True)
    z, y = ring_on(tokens), swap_y(tokens)

    t, y = together(z, y)
    hop_1, y_0 = t, y
    z, y = ring_on(hop_1), swap_y(hop_1)
    out_near = lax.all_gather(after(w_out, t), "core", axis=0, tiled=True)
    out_half = lax.dynamic_slice_in_dim(after(w_out, t), y_bit * (width // 8), width // 8, 0)
    size = w_down.shape[0] // ctx
    down_both = lax.dynamic_slice_in_dim(after(w_down, t), 2 * ring * size, 2 * size, 0)
    own, other, to_send = shared_columns(
        after(w_gate, t), w_up, jnp.stack([ring, core, y_bit]).astype(jnp.int32), fsdp, hops
    )
    half_rows = width // 8

    t, y, to_send, down_both, out_half = together(z, y, to_send, down_both, out_half)
    hop_2, y_1 = t, y
    z, y = ring_on(hop_2), swap_y(hop_2)
    out_straight = swap_x(out_half)
    first_all = blank((ctx,) + tokens.shape, t)

    t, y, first_all, w_qkv = together(z, y, first_all, w_qkv)
    hop_3, y_2 = t, y
    y = swap_y(hop_3)
    cot_1 = ring_on(after(cotangent, t))
    gains_all = w_qkv[:, 3 * part :].astype(F32).T
    gain_one, gain_two = gains_all[0], gains_all[1]

    def take_rows(buffer, item, hop, mate):
        normed = (norm_parts(item.astype(F32))[0] * gain_one).astype(BF)
        return put(buffer, normed, block_of(hop) ^ mate)

    for item, hop, mate in ((tokens, 0, 0), (y_0, 0, 1), (hop_1, 1, 0), (y_1, 1, 1), (hop_2, 2, 0), (y_2, 2, 1)):
        first_all = take_rows(first_all, item, hop, mate)
    first_all = take_rows(first_all, hop_3, 3, 0)

    t, cot_1, first_all, out_straight = together(y, cot_1, first_all, out_straight)
    cot_2 = ring_on(cot_1)
    out_far = lax.all_gather(out_straight, ("core", "y"), axis=0, tiled=True)
    arriving_own = swap_x(after(to_send[:half_rows], t))
    first_all = take_rows(first_all, t, 3, 1).reshape(length, width)
    raw = dot(w_qkv, first_all, 0, 1)
    mixed, query, key, value, logs = attend(raw, cosine, sine, heads, ctx)

    t, cot_2, down_both, arriving_own = together(mixed, cot_2, down_both, arriving_own)
    arriving_other = swap_x(after(to_send[half_rows:], t))
    down_both = lax.all_gather(down_both.reshape(1, 2, 2, size // 2, width), "x", axis=0, tiled=True)
    mixed_own = lax.all_to_all(t, sequence, 0, 0, tiled=True)
    gate_up_near = swap_core(after(other, t))
    cot_near, cot_near_1, cot_near_2 = [swap_core(after(item, t)) for item in (cotangent, cot_1, cot_2)]
    w_gate_up = put_whole(blank((8, half_rows, own.shape[1]), t), own, 0)

    t, gate_up_near, cot_near, cot_near_1, cot_near_2, w_gate_up, out_near, out_far, arriving_other = together(
        mixed_own, gate_up_near, cot_near, cot_near_1, cot_near_2, w_gate_up, out_near, out_far, arriving_other
    )
    crossing_own = swap_y(after(arriving_own, t))
    cot_3 = ring_on(after(cot_2, t))
    mixed_own = t.reshape(width, rows)
    inputs = tokens.astype(F32)
    mixed_halves = mixed_own.reshape(2, width // 2, rows)
    middle = inputs + dot(pick(mixed_halves, x_bit), out_near, 0, 0) + dot(pick(mixed_halves, 1 - x_bit), out_far, 0, 0)
    normed_mid, scale_mid = norm_parts(middle)
    second = (normed_mid * gain_two).astype(BF)

    t, cot_3, w_gate_up, gate_up_near = together(second, cot_3, w_gate_up, gate_up_near)
    z, near_0 = ring_on(t), swap_core(t)
    last_straight = swap_core(after(arriving_other, t))
    cot_near_3 = swap_core(after(cot_3, t))
    w_gate_up = put_whole(w_gate_up, gate_up_near, 1)
    w_gate_up = put(w_gate_up, arriving_own, half_at(2, y_bit))

    t, near_0, cot_near_3, w_gate_up, crossing_own, last_straight = together(
        z, near_0, cot_near_3, w_gate_up, crossing_own, last_straight
    )
    hop_1 = t
    z, near_1 = ring_on(t), swap_core(t)
    crossing_other = swap_y(after(arriving_other, t))
    w_gate_up = put(w_gate_up, crossing_own, half_at(2, 1 - y_bit))
    w_gate_up = put(w_gate_up, last_straight, half_at(3, y_bit))
    down_share = blank((2, 2, 2, size // 2, width), t)

    t, near_1, w_gate_up, down_share = together(z, near_1, w_gate_up, down_share)
    hop_2 = t
    z, near_2 = ring_on(t), swap_core(t)
    cot_all = jnp.concatenate(
        [cot_1, cot_near_1, cot_2, cot_near_2, cot_3, cot_near_3, cotangent, cot_near], axis=0
    )

    t, near_2, crossing_other, cot_all, w_gate_up, down_both = together(
        z, near_2, crossing_other, cot_all, w_gate_up, down_both
    )
    down_near = swap_core(pick(down_both, 1 - core, 2))
    down_at = lambda blocks, item, i: lax.dynamic_update_slice(blocks, item[:, None], (0, i, 0, 0, 0))
    down_share = down_at(down_share, pick(down_both, core, 2), core)
    near_3 = swap_core(t)
    last_crossed = swap_core(crossing_other)
    second_all = jnp.concatenate([hop_1, near_1, hop_2, near_2, t, near_3, second, near_0], axis=0)
    w_gate_up = put(w_gate_up, last_crossed, half_at(3, 1 - y_bit)).reshape(width, -1)
    down_share = down_at(down_share, down_near, 1 - core).reshape(-1, width)

    buffers = [blank((length, share), t) for _ in range(3)]
    half = length // 2

    def run_middle(start, buffers, rows_in):
        items = mlp_middle(rows_in, cot_all[start : start + half], w_gate_up, down_share)
        return items, [lax.dynamic_update_slice(buffer, item, (start, 0)) for buffer, item in zip(buffers, items)]

    def run_back(items):
        back = dot(jnp.concatenate(items[1:], axis=1), w_gate_up, 1, 1).astype(BF)
        return [back[i * rows : (i + 1) * rows] for i in range(4)]

    items, buffers = run_middle(0, buffers, second_all[:half])
    own_1, other_1, own_2, other_2 = run_back(items)
    near_1, near_2 = swap_core(other_1), swap_core(other_2)
    t = add(own_1, near_1).astype(BF)
    z = ring_on(t)
    items, buffers = run_middle(half, buffers, after(second_all[half:], t))
    z, near_2, *items = together(z, near_2, *items)
    t = add(own_2, near_2, z).astype(BF)
    z = ring_on(t)
    items[0] = after(items[0], t)
    items[1] = after(items[1], t)
    own_3, other_3, own_0, other_0 = run_back(items)
    near_3, near_0 = swap_core(other_3), swap_core(other_0)
    z, near_3, near_0, hidden, grad_gate, grad_up = together(z, near_3, near_0, *buffers)

    def given(blocks, bit, dim):
        return pick(blocks, 1 - bit, dim)

    def kept(blocks, bit, dim, arrived):
        return add(pick(blocks, bit, dim), arrived).astype(BF)

    def half_sum(partial):
        return lax.psum_scatter(partial.astype(BF), "x", scatter_dimension=0, tiled=True)

    t = add(own_3, near_3, z).astype(BF)
    z = ring_on(t)
    gate_partial = dot(after(second_all, t), grad_gate, 0, 0).astype(BF)
    gate_sum = half_sum(gate_partial)
    t, gate_partial = together(z, gate_partial)

    grad_second = add(own_0, near_0, t)
    gain_mlp_term = jnp.sum(grad_second * normed_mid, axis=0)
    grad_middle = cotangent.astype(F32) + norm_back(grad_second * gain_two, normed_mid, scale_mid)
    grad_branch = grad_middle.astype(BF)
    grad_mixed_own = halves(
        dot(out_near, grad_branch, 1, 1).astype(BF), dot(out_far, grad_branch, 1, 1).astype(BF), x_bit
    )

    t, hidden = together(grad_mixed_own, hidden)
    grad_mixed = lax.all_to_all(t.reshape(ctx, part, -1), sequence, 0, 0, tiled=True)
    branch_1, branch_y0 = ring_on(after(grad_branch, t)), swap_y(after(grad_branch, t))
    up_partial = dot(after(second_all, t), grad_up, 0, 0).astype(BF)
    out_partial = dot(hidden, down_share, 1, 0).astype(BF)
    out_near_1 = swap_core(out_partial[rows : 2 * rows])

    t, out_near_1, out_partial, up_partial, gate_sum, branch_1, branch_y0 = together(
        grad_mixed, out_near_1, out_partial, up_partial, gate_sum, branch_1, branch_y0
    )
    up_sum = half_sum(up_partial)
    out = [out_partial[i * rows : (i + 1) * rows] for i in range(2 * hops)]
    gate_sum = gate_sum.reshape(2, hops, 2, own_rows, share)
    gate_y = swap_y(given(gate_sum, y_bit, 2))
    branch_2 = ring_on(after(branch_1, t))
    out_sum = add(out[0], out_near_1).astype(BF)
    out_z = ring_on(out_sum)
    out_near_2 = swap_core(after(out[3], t))
    grad_raw = attend_back(query, key, value, mixed, t, logs, cosine, sine, heads, ctx)
    grad_raw = grad_raw.reshape(-1, length)
    first_partial = dot(grad_raw, w_qkv[:, : 3 * part], 0, 1).astype(BF)

    t, out_near_2, grad_raw, out_z, branch_2 = together(first_partial, out_near_2, grad_raw, out_z, branch_2)
    first_blocks = t.reshape(ctx, rows, width)
    first_own = lambda hop: pick(first_blocks, block_of(hop))
    first_other = lambda hop: pick(first_blocks, block_of(hop) ^ 1)
    y = swap_y(first_other(1))
    out_sum = add(out[2], out_near_2, out_z).astype(BF)
    out_z = ring_on(out_sum)
    out_near_3 = swap_core(after(out[5], t))
    down_partial = dot(hidden, after(cot_all, t), 0, 0).astype(BF)
    head_partial = dot(after(first_all, t), grad_raw, 0, 1).astype(BF).reshape(2, 2, ctx * own_rows, -1)
    head_near = swap_core(given(head_partial, core, 1))

    t, out_near_3, head_partial, head_near, out_z, gate_y, down_partial = together(
        y, out_near_3, head_partial, head_near, out_z, gate_y, down_partial
    )
    down_sum = half_sum(down_partial).reshape(2, 2, -1, width)
    total = add(first_own(1), t).astype(BF)
    z, y = ring_on(total), swap_y(after(first_other(2), t))
    out_sum = add(out[4], out_near_3, out_z).astype(BF)
    head_sum = kept(head_partial, core, 1, head_near)
    head_given = given(head_sum, x_bit, 0)
    gate_sum = kept(gate_sum, y_bit, 2, gate_y)
    products = first_partial.astype(F32) * after(first_all, t).astype(F32)
    gain_attn_term = jnp.sum(products, axis=0) / gain_one

    t, y, out_sum, head_sum, head_given, gate_sum, gain_attn_term = together(
        z, y, out_sum, head_sum, head_given, gate_sum, gain_attn_term
    )
    total = add(first_own(2), y, t).astype(BF)
    z, y = ring_on(total), swap_y(after(first_other(3), t))
    out_near_0 = swap_core(after(out[7], t))

    gain_terms = jnp.stack([gain_attn_term, gain_mlp_term]).reshape(2, fsdp * ctx, own_rows).transpose(1, 0, 2)
    gain_terms = lax.all_to_all(after(gain_terms, t), ("x", "core") + sequence, 0, 0, tiled=True)

    t, y, out_near_0, up_sum, gain_terms = together(z, y, out_near_0, up_sum, gain_terms)
    total = add(first_own(3), y, t).astype(BF)
    z, y = ring_on(total), swap_y(after(first_other(0), t))
    head_x = swap_x(after(head_given, t))
    up_sum = up_sum.reshape(2, hops, 2, own_rows, share)
    up_given = given(up_sum, y_bit, 2)

    def deal_rows(summed):
        received = lax.all_to_all(summed.reshape(2 * hops, own_rows, -1), ("core", "z"), 0, 0, tiled=True)
        return hidden_columns(received.reshape(2, hops, own_rows, -1), fsdp)

    t, y, up_given = together(z, y, up_given)
    up_y = swap_y(up_given)
    gate_grad = deal_rows(after(gate_sum, t))
    branch_3 = ring_on(after(branch_2, t))
    grad_first = add(first_own(0), y, t)
    inputs_normed, scale_attn = norm_parts(inputs)
    input_grad = (grad_middle + norm_back(grad_first * gain_one, inputs_normed, scale_attn)).astype(BF)

    t, branch_3, input_grad = together(up_y, branch_3, input_grad)
    up_grad = deal_rows(kept(up_sum, y_bit, 2, t))
    branch_y1, branch_y2, branch_y3 = [swap_y(after(item, t)) for item in (branch_1, branch_2, branch_3)]
    out_z = ring_on(after(out_sum, t))
    down_given = given(down_sum, y_bit, 1)

    t, branch_y1, branch_y2, branch_y3, head_x, down_given = together(
        out_z, branch_y1, branch_y2, branch_y3, head_x, down_given
    )
    down_y = swap_y(down_given)
    head_rows = lax.all_to_all(kept(head_sum, x_bit, 0, head_x), sequence, 0, 0, tiled=True)
    output = (middle + add(out[6], out_near_0, t)).astype(BF)
    branches = ((grad_branch, branch_y0), (branch_1, branch_y1), (branch_2, branch_y2), (branch_3, branch_y3))
    branch_all = jnp.concatenate([item for pair in branches for item in pair], axis=0)
    mixed_rows = jnp.concatenate([pick(mixed, block_of(hop) ^ i) for hop in range(hops) for i in range(2)], axis=1)
    out_weight = dot(mixed_rows, branch_all, 1, 0).astype(BF).reshape(2, 2, own_rows, width)
    weight = kept(out_weight, core, 1, swap_core(given(out_weight, core, 1)))
    weight_x = swap_x(given(weight, x_bit, 0))

    down_y, weight_x = together(down_y, weight_x)
    weight = kept(weight, x_bit, 0, weight_x)
    pairs = [(i * ctx + j, j * fsdp + i) for i in range(fsdp) for j in range(ctx)]
    out_grad = lax.ppermute(weight, ("x", "core") + sequence, pairs).astype(F32)
    down_sum = kept(down_sum, y_bit, 1, down_y)
    down_near = swap_core(pick(down_sum, 1 - core))
    down_grad = halves(pick(down_sum, core), down_near, core).reshape(-1, width).astype(F32)
    query_grad, key_grad, value_grad = head_columns(head_rows.reshape(ctx, own_rows, -1))

    gain_grads = jnp.sum(gain_terms, axis=0)
    return (
        output,
        input_grad,
        gain_grads[0],
        query_grad,
        key_grad,
        value_grad,
        out_grad,
        gain_grads[1],
        gate_grad,
        up_grad,
        down_grad,
    )


def solution(mesh):
    fsdp, ctx = ("fsdp",), ("ctx",)
    body = general_body
    if mesh.devices.shape == (4, 8):
        body, fsdp, ctx = paired_body, ("x", "core"), ("z", "y")
        mesh = jax.sharding.Mesh(mesh.devices.reshape(2, 2, 4, 2), fsdp + ctx)
    rows, matrix = P(fsdp + ctx, None), P(fsdp, None)
    in_specs = (rows, P(fsdp), matrix, matrix, matrix, matrix, P(fsdp), matrix, matrix, matrix, rows)
    out_specs = (rows, rows, P(fsdp + ctx), rows, rows, rows, rows, P(fsdp + ctx), rows, rows, rows)
    return jax.shard_map(body, mesh=mesh, in_specs=in_specs, out_specs=out_specs, check_vma=False)
```

```python
import functools

import jax
import jax.numpy as jnp
import numpy as np
from jax import lax
from jax.experimental import pallas as pl
from jax.experimental.pallas import tpu as pltpu
from jax.sharding import PartitionSpec as P

HEADS = 32
EPS = 1e-05
THETA = 130000.0
MASKED = -1e30
BF = jnp.bfloat16
F32 = jnp.float32


def dot(left, right, left_axis, right_axis):
    return lax.dot_general(
        left, right, (((left_axis,), (right_axis,)), ((), ())), preferred_element_type=F32
    )


def norm_parts(matrix):
    scale = lax.rsqrt(jnp.mean(matrix * matrix, axis=-1, keepdims=True) + EPS)
    return (matrix * scale, scale)


def norm_back(grad_scaled, normed, scale):
    return scale * (grad_scaled - normed * jnp.mean(grad_scaled * normed, axis=-1, keepdims=True))


def angle_tables(length, head_width):
    half = head_width // 2
    freqs = np.float32(THETA) ** (-(np.arange(half, dtype=np.float32) * np.float32(2.0 / head_width)))
    angles = freqs[:, None].astype(np.float32) * np.arange(length, dtype=np.float32)[None, :]
    return jnp.asarray(np.cos(angles), F32), jnp.asarray(np.sin(angles), F32)


def low_lanes(block):
    return lax.broadcasted_iota(jnp.int32, block.shape, 1) < block.shape[1] // 2


def sort_columns(matrix, blocks):
    size = matrix.shape[1] // blocks
    early, late = [], []
    for j in range(blocks // 2):
        first = matrix[:, 2 * j * size : (2 * j + 1) * size]
        second = pltpu.roll(matrix[:, (2 * j + 1) * size : (2 * j + 2) * size], size // 2, 1)
        low = low_lanes(first)
        early.append(jnp.where(low, first, second))
        late.append(jnp.where(low, second, first))
    return jnp.concatenate(early + late[::-1], axis=1)


def deal_columns(matrix, blocks):
    size = matrix.shape[1] // blocks
    out = []
    for j in range(blocks // 2):
        early = matrix[:, j * size : (j + 1) * size]
        late = matrix[:, (blocks - 1 - j) * size : (blocks - j) * size]
        low = low_lanes(early)
        out.append(jnp.where(low, early, late))
        out.append(pltpu.roll(jnp.where(low, late, early), size // 2, 1))
    return jnp.concatenate(out, axis=1)


def turn(matrix, cosine, sine):
    half = matrix.shape[0] // 2
    first, second = matrix[:half], matrix[half:]
    return jnp.concatenate([first * cosine - second * sine, second * cosine + first * sine], axis=0)


def by_blocks(ref):
    return jnp.concatenate([ref[block].astype(F32) for block in range(ref.shape[0])], axis=1)


def masked_block(scores, chunk):
    keys = scores.shape[0]
    places = lax.broadcasted_iota(jnp.int32, (chunk, chunk), 0)
    wants = lax.broadcasted_iota(jnp.int32, (chunk, chunk), 1)
    last = jnp.where(places <= wants, scores[keys - chunk :], MASKED)
    if keys == chunk:
        return last
    return jnp.concatenate([scores[: keys - chunk], last], axis=0)


def attend_kernel(blocks, chunk, q_ref, k_ref, v_ref, cos_ref, sin_ref, o_ref, qs_ref, ks_ref, vs_ref, lse_ref):
    width, length = q_ref.shape
    cosine, sine = cos_ref[...], sin_ref[...]
    query = turn(sort_columns(q_ref[...], blocks), cosine, sine).astype(BF)
    key = turn(sort_columns(k_ref[...], blocks), cosine, sine).astype(BF)
    value = sort_columns(v_ref[...], blocks).astype(BF)
    scaled = query * jnp.asarray(width ** (-0.5), BF)
    qs_ref[...] = scaled
    ks_ref[...] = key
    vs_ref[...] = value
    mixed, logs = [], []
    for i in range(length // chunk):
        count = (i + 1) * chunk
        scores = dot(key[:, :count], scaled[:, i * chunk : count], 0, 0)
        scores = masked_block(scores, chunk)
        top = jnp.max(scores, axis=0, keepdims=True)
        raised = jnp.exp(scores - top)
        total = jnp.sum(raised, axis=0, keepdims=True)
        mixed.append(dot(value[:, :count], raised.astype(BF), 1, 0) / total)
        logs.append(top + jnp.log(total))
    size = length // blocks
    dealt = deal_columns(jnp.concatenate(mixed, axis=1), blocks).astype(BF)
    for block in range(blocks):
        o_ref[block] = dealt[:, block * size : (block + 1) * size]
    lse_ref[0] = jnp.concatenate(logs, axis=1)


def attend_back_kernel(blocks, chunk, q_ref, k_ref, v_ref, o_ref, do_ref, lse_ref, cos_ref, sin_ref, d_ref, dk_ref, dv_ref):
    width, length = q_ref.shape
    factor = width ** (-0.5)
    cosine, sine = cos_ref[...], -sin_ref[...]
    scaled, key, value = q_ref[...], k_ref[...], v_ref[...]
    grad_f32 = sort_columns(by_blocks(do_ref), blocks)
    center = jnp.sum(grad_f32 * sort_columns(by_blocks(o_ref), blocks), axis=0, keepdims=True)
    grad = grad_f32.astype(BF)
    logs = lse_ref[0]
    dq = []
    for i in reversed(range(length // chunk)):
        count = (i + 1) * chunk
        here = slice(i * chunk, count)
        scores = masked_block(dot(key[:, :count], scaled[:, here], 0, 0), chunk)
        shares = jnp.exp(scores - logs[:, here])
        grad_shares = dot(value[:, :count], grad[:, here], 0, 0)
        grad_scores = (shares * (grad_shares - center[:, here])).astype(BF)
        dq.append(dot(key[:, :count], grad_scores, 1, 0))
        dk_part = dot(scaled[:, here], grad_scores, 1, 1)
        dv_part = dot(grad[:, here], shares.astype(BF), 1, 1)
        if count == length:
            dk_ref[...] = dk_part
            dv_ref[...] = dv_part
        else:
            dk_ref[:, :count] += dk_part
            dv_ref[:, :count] += dv_part
    dq = turn(jnp.concatenate(dq[::-1], axis=1) * factor, cosine, sine)
    d_ref[0] = deal_columns(dq, blocks).astype(BF)
    d_ref[1] = deal_columns(turn(dk_ref[...], cosine, sine), blocks).astype(BF)
    d_ref[2] = deal_columns(dv_ref[...], blocks).astype(BF)


def attend(raw, cosine, sine, heads, blocks):
    width, length = 2 * cosine.shape[0], raw.shape[1]
    chunk = min(256, length)
    head = lambda shift: pl.BlockSpec((width, length), lambda h: (h + shift * heads, 0))
    table = pl.BlockSpec((width // 2, length), lambda h: (0, 0))
    flat = jax.ShapeDtypeStruct((heads * width, length), BF)
    return pl.pallas_call(
        functools.partial(attend_kernel, blocks, chunk),
        grid=(heads,),
        in_specs=[head(0), head(1), head(2), table, table],
        out_specs=[
            pl.BlockSpec((blocks, width, length // blocks), lambda h: (0, h, 0)),
            head(0),
            head(0),
            head(0),
            pl.BlockSpec((1, 1, length), lambda h: (h, 0, 0)),
        ],
        out_shape=[
            jax.ShapeDtypeStruct((blocks, heads * width, length // blocks), BF),
            flat,
            flat,
            flat, jax.ShapeDtypeStruct((heads, 1, length), F32),
        ],
        compiler_params=pltpu.CompilerParams(vmem_limit_bytes=40 * 1024 * 1024),
        name="attend",
    )(raw, raw, raw, cosine, sine)


def attend_back(query, key, value, mixed, grad, logs, cosine, sine, heads, blocks):
    width, length = query.shape[0] // heads, query.shape[1]
    chunk = min(256, length)
    head = pl.BlockSpec((width, length), lambda h: (h, 0))
    block = pl.BlockSpec((blocks, width, length // blocks), lambda h: (0, h, 0))
    table = pl.BlockSpec((width // 2, length), lambda h: (0, 0))
    return pl.pallas_call(
        functools.partial(attend_back_kernel, blocks, chunk),
        grid=(heads,),
        in_specs=[head, head, head, block, block, pl.BlockSpec((1, 1, length), lambda h: (h, 0, 0)), table, table],
        out_specs=pl.BlockSpec((3, width, length), lambda h: (0, h, 0)),
        out_shape=jax.ShapeDtypeStruct((3, heads * width, length), BF),
        scratch_shapes=[pltpu.VMEM((width, length), F32), pltpu.VMEM((width, length), F32)],
        compiler_params=pltpu.CompilerParams(vmem_limit_bytes=40 * 1024 * 1024),
        name="attend_back",
    )(query, key, value, mixed, grad, logs, cosine, sine)


def swap(item, axis, bit):
    pairs = [(i, i ^ bit) for i in range(lax.axis_size(axis))]
    return lax.ppermute(item, axis, pairs)


def step_on(item):
    count = lax.axis_size("ctx")
    return lax.ppermute(item, "ctx", [(i, (i + 2) % count) for i in range(count)])


def after(item, *others):
    return lax.optimization_barrier((item,) + others)[0]


def gather_rows(piece):
    count, place = lax.axis_size("ctx"), lax.axis_index("ctx")
    rows = jnp.zeros((count,) + piece.shape, piece.dtype)
    for hop in range(count // 2):
        if hop:
            piece = step_on(piece)
        source = lax.rem(place + count - 2 * hop, count)
        rows = lax.dynamic_update_slice(rows, piece[None], (source, 0, 0))
        rows = lax.dynamic_update_slice(rows, swap(piece, "ctx", 1)[None], (source ^ 1, 0, 0))
    return rows.reshape(-1, rows.shape[2])


def scatter_rows(partial):
    count, place = lax.axis_size("ctx"), lax.axis_index("ctx")
    blocks = partial.astype(BF).reshape(count, -1, partial.shape[1])
    total = None
    for hop in range(1, count // 2 + 1):
        target = lax.rem(place + count - 2 * hop, count)
        mine = lax.dynamic_index_in_dim(blocks, target, 0, keepdims=False)
        other = lax.dynamic_index_in_dim(blocks, target ^ 1, 0, keepdims=False)
        term = mine.astype(F32) + swap(other, "ctx", 1).astype(F32)
        total = term if total is None else term + total.astype(F32)
        if hop < count // 2:
            total = step_on(total.astype(BF))
    return total


def gather_weight(piece):
    if lax.axis_size("fsdp") != 4:
        return lax.all_gather(piece, "fsdp", axis=0, tiled=True)
    place = lax.axis_index("fsdp")
    rows = jnp.zeros((4,) + piece.shape, piece.dtype)
    far = swap(piece, "fsdp", 2)
    for source, item in (
        (place, piece),
        (place ^ 1, swap(piece, "fsdp", 1)),
        (place ^ 2, far),
        (place ^ 3, swap(far, "fsdp", 1)),
    ):
        rows = lax.dynamic_update_slice(rows, item[None], (source, 0, 0))
    return rows.reshape(-1, piece.shape[1])


def scatter(partial, axis):
    return lax.psum_scatter(partial.astype(BF), axis, scatter_dimension=0, tiled=True)


def general_body(
    tokens, gain_attn, w_query, w_key, w_value, w_out, gain_mlp, w_gate, w_up, w_down, cotangent
):
    width = tokens.shape[1]
    hidden_width = w_gate.shape[1]
    fsdp, ctx = lax.axis_size("fsdp"), lax.axis_size("ctx")
    place = lax.axis_index("ctx")
    length = tokens.shape[0] * ctx
    heads = HEADS // ctx
    part = width // ctx
    share = hidden_width // ctx
    own_rows = width // (fsdp * ctx)
    cosine, sine = angle_tables(length, width // HEADS)

    def head_columns(weight):
        return lax.dynamic_slice_in_dim(weight, place * part, part, 1)

    def hidden_columns(weight):
        rows = weight.shape[0]
        blocks = weight.reshape(rows, fsdp, ctx, share // fsdp)
        return lax.dynamic_index_in_dim(blocks, place, 2, keepdims=False).reshape(rows, share)

    def to_owners(partial):
        summed = scatter(partial, "fsdp")
        return lax.all_to_all(summed, "ctx", 0, 0, tiled=True).reshape(ctx, own_rows, -1).astype(F32)

    def of_heads(received):
        return received.transpose(1, 0, 2).reshape(own_rows, -1)

    def of_hidden(received):
        blocks = received.reshape(ctx, own_rows, fsdp, -1)
        return blocks.transpose(1, 2, 0, 3).reshape(own_rows, -1)

    def normed_rows(rows):
        return norm_parts(rows.astype(F32))[0]

    w_qkv_piece = jnp.concatenate([head_columns(item) for item in (w_query, w_key, w_value)], axis=1)
    w_qkv = gather_weight(w_qkv_piece)
    gains = lax.all_gather(jnp.stack([gain_attn, gain_mlp]), "fsdp", axis=1, tiled=True).astype(F32)
    gain_one, gain_two = gains[0], gains[1]
    tokens_all = gather_rows(tokens)
    first_all = (normed_rows(tokens_all) * gain_one).astype(BF)
    raw = dot(w_qkv, first_all, 0, 1)
    mixed, query, key, value, logs = attend(raw, cosine, sine, heads, ctx)
    w_out_all = gather_weight(after(w_out, w_qkv))
    w_gate_up = gather_weight(
        after(jnp.concatenate([hidden_columns(w_gate), hidden_columns(w_up)], axis=1), w_out_all)
    )
    down_size = w_down.shape[0] // ctx
    down_share = gather_weight(
        after(lax.dynamic_slice_in_dim(w_down, place * down_size, down_size, 0), w_gate_up)
    )
    cotangent_all = gather_rows(after(cotangent, tokens_all))

    inputs = tokens.astype(F32)
    mixed_own = lax.all_to_all(mixed, "ctx", 0, 0, tiled=True).reshape(width, -1)
    middle = inputs + dot(mixed_own, w_out_all, 0, 0)
    normed_mid, scale_mid = norm_parts(middle)
    second_all = gather_rows((normed_mid * gain_two).astype(BF))
    gate_up = dot(second_all, w_gate_up, 1, 0)
    gate, upward = gate_up[:, :share], gate_up[:, share:]
    grad_hidden = dot(cotangent_all, down_share, 1, 1)
    sigmoid = jax.nn.sigmoid(gate)
    hidden = (gate * sigmoid * upward).astype(BF)
    grad_gate = (grad_hidden * upward * (sigmoid + gate * sigmoid * (1.0 - sigmoid))).astype(BF)
    grad_up = (grad_hidden * (gate * sigmoid)).astype(BF)
    grad_gate_up = jnp.concatenate([grad_gate, grad_up], axis=1)
    grad_second = scatter_rows(dot(grad_gate_up, w_gate_up, 1, 1))
    output = (middle + scatter_rows(after(dot(hidden, down_share, 1, 0), grad_second))).astype(BF)

    gain_mlp_term = jnp.sum(grad_second * normed_mid, axis=0)
    grad_middle = cotangent.astype(F32) + norm_back(grad_second * gain_two, normed_mid, scale_mid)
    grad_branch = grad_middle.astype(BF)
    grad_mixed_own = dot(w_out_all, grad_branch, 1, 1).astype(BF)
    grad_mixed = lax.all_to_all(grad_mixed_own.reshape(ctx, part, -1), "ctx", 0, 0, tiled=True)
    grad_raw = attend_back(query, key, value, mixed, grad_mixed, logs, cosine, sine, heads, ctx)
    grad_raw = grad_raw.reshape(-1, length)
    branch_all = gather_rows(after(grad_branch, grad_mixed))
    first_partial = dot(grad_raw, w_qkv, 0, 1)
    grad_first = scatter_rows(first_partial)
    inputs_normed, scale_attn = norm_parts(inputs)
    gain_attn_term = jnp.sum(grad_first * inputs_normed, axis=0)
    input_grad = (grad_middle + norm_back(grad_first * gain_one, inputs_normed, scale_attn)).astype(BF)

    down_grad = scatter(dot(hidden, cotangent_all, 0, 0), "fsdp").astype(F32)
    mixed_rows = mixed.transpose(1, 0, 2).reshape(part, length)
    out_grad = scatter(dot(mixed_rows, branch_all, 1, 0), "fsdp")
    out_grad = lax.ppermute(
        out_grad,
        ("fsdp", "ctx"),
        [(i * ctx + j, j * fsdp + i) for i in range(fsdp) for j in range(ctx)],
    ).astype(F32)
    gate_up_rows = to_owners(dot(second_all, grad_gate_up, 0, 0))
    qkv_rows = to_owners(dot(first_all, grad_raw, 0, 1))
    gain_terms = jnp.stack([gain_attn_term, gain_mlp_term]).reshape(2, fsdp * ctx, own_rows)
    gain_grads = jnp.sum(
        lax.all_to_all(gain_terms.transpose(1, 0, 2), ("fsdp", "ctx"), 0, 0, tiled=True), axis=0
    )
    return (
        output,
        input_grad,
        gain_grads[0],
        of_heads(qkv_rows[:, :, :part]),
        of_heads(qkv_rows[:, :, part : 2 * part]),
        of_heads(qkv_rows[:, :, 2 * part :]),
        out_grad,
        gain_grads[1],
        of_hidden(gate_up_rows[:, :, :share]),
        of_hidden(gate_up_rows[:, :, share:]),
        down_grad,
    )


def together(*items):
    return lax.optimization_barrier(items)


def pick(blocks, index, axis=0):
    return lax.dynamic_index_in_dim(blocks, index, axis, keepdims=False)


def put(blocks, item, index):
    return lax.dynamic_update_slice(blocks, item[None], (index,) + (0,) * item.ndim)


def halves(own, other, index):
    return put(put(jnp.zeros((2,) + own.shape, own.dtype), own, index), other, 1 - index)


def add(*items):
    return sum(item.astype(F32) for item in items)


def swap_pair(item, axis):
    return lax.ppermute(item, axis, [(0, 1), (1, 0)])


def swap_x(item):
    return swap_pair(item, "x")


def swap_core(item):
    return swap_pair(item, "core")


def swap_y(item):
    return swap_pair(item, "y")


def ring_on(item, steps=1):
    count = lax.axis_size("z")
    return lax.ppermute(item, "z", [(i, (i + steps) % count) for i in range(count)])


def columns_kernel(place_ref, gate_ref, up_ref, own_ref, other_ref, halves_ref):
    step, steps = pl.program_id(0), pl.num_programs(0)
    size, half = own_ref.shape[1] // 2, halves_ref.shape[0] // 2
    rows = pl.ds(pl.multiple_of(place_ref[2] * half, half), half)

    def take(weight_ref):
        for block in range(2):
            own = pl.ds(pl.multiple_of((2 * block + place_ref[1]) * size, size), size)
            other = pl.ds(pl.multiple_of((2 * block + 1 - place_ref[1]) * size, size), size)
            into = slice(block * size, (block + 1) * size)
            own_ref[:, into] = weight_ref[:, own]
            other_ref[:, into] = weight_ref[:, other]
            halves_ref[:half, into] = weight_ref[rows, own]
            halves_ref[half:, into] = weight_ref[rows, other]

    @pl.when(step < steps // 2)
    def _():
        take(gate_ref)

    @pl.when(step >= steps // 2)
    def _():
        take(up_ref)


def shared_columns(w_gate, w_up, place, blocks, rings):
    rows, columns = w_gate.shape
    size = columns // (blocks * rings * 2)
    gate = pl.BlockSpec((rows, 2 * size), lambda s, at: (0, jnp.minimum(s, blocks - 1) * rings + at[0]))
    up = pl.BlockSpec((rows, 2 * size), lambda s, at: (0, jnp.maximum(s - blocks, 0) * rings + at[0]))
    wide = 2 * blocks * size
    return pl.pallas_call(
        columns_kernel,
        grid_spec=pltpu.PrefetchScalarGridSpec(
            num_scalar_prefetch=1,
            grid=(2 * blocks,),
            in_specs=[gate, up],
            out_specs=[pl.BlockSpec((rows, size), lambda s, at: (0, s))] * 3,
        ),
        out_shape=[jax.ShapeDtypeStruct((rows, wide), BF)] * 3,
        compiler_params=pltpu.CompilerParams(vmem_limit_bytes=56 * 1024 * 1024),
        name="columns",
    )(place, w_gate, w_up)


def mlp_middle(second, cotangent, w_gate_up, down_share):
    share = down_share.shape[0]
    gate_up = dot(second, w_gate_up, 1, 0)
    gate, upward = gate_up[:, :share], gate_up[:, share:]
    grad_hidden = dot(cotangent, down_share, 1, 1)
    sigmoid = jax.nn.sigmoid(gate)
    hidden = (gate * sigmoid * upward).astype(BF)
    grad_gate = (grad_hidden * upward * (sigmoid + gate * sigmoid * (1.0 - sigmoid))).astype(BF)
    grad_up = (grad_hidden * (gate * sigmoid)).astype(BF)
    return hidden, grad_gate, grad_up


def hidden_columns_kernel(in_ref, out_ref):
    cores, rings, _, wide = in_ref.shape
    size = wide // 2
    for ring in range(rings):
        for half in range(2):
            for core in range(cores):
                start = ((ring * 2 + half) * cores + core) * size
                out_ref[:, start : start + size] = in_ref[core, ring, :, half * size : (half + 1) * size].astype(F32)


def hidden_columns(received, blocks):
    cores, rings, rows, share = received.shape
    wide = share // blocks
    return pl.pallas_call(
        hidden_columns_kernel,
        grid=(blocks,),
        in_specs=[pl.BlockSpec((cores, rings, rows, wide), lambda s: (0, 0, 0, s))],
        out_specs=pl.BlockSpec((rows, cores * rings * wide), lambda s: (0, s)),
        out_shape=jax.ShapeDtypeStruct((rows, cores * rings * share), F32),
        compiler_params=pltpu.CompilerParams(vmem_limit_bytes=56 * 1024 * 1024),
        name="hidden_columns",
    )(received)


def head_columns_kernel(in_ref, *out_refs):
    count = in_ref.shape[0]
    part = in_ref.shape[2] // len(out_refs)
    for i, out_ref in enumerate(out_refs):
        for block in range(count):
            out_ref[:, block * part : (block + 1) * part] = in_ref[block, :, i * part : (i + 1) * part].astype(F32)


def head_columns(received):
    count, rows, wide = received.shape
    return pl.pallas_call(
        head_columns_kernel,
        out_shape=[jax.ShapeDtypeStruct((rows, count * wide // 3), F32)] * 3,
        compiler_params=pltpu.CompilerParams(vmem_limit_bytes=56 * 1024 * 1024),
        name="head_columns",
    )(received)


def paired_body(
    tokens, gain_attn, w_query, w_key, w_value, w_out, gain_mlp, w_gate, w_up, w_down, cotangent
):
    rows, width = tokens.shape
    hops = lax.axis_size("z")
    fsdp, ctx = 2 * lax.axis_size("x"), 2 * hops
    x_bit, core, ring, y_bit = [lax.axis_index(axis) for axis in ("x", "core", "z", "y")]
    place, fsdp_place = 2 * ring + y_bit, 2 * x_bit + core
    length = rows * ctx
    heads = HEADS // ctx
    part = width // ctx
    share = w_gate.shape[1] // ctx
    own_rows = width // (fsdp * ctx)
    sequence = ("z", "y")
    cosine, sine = angle_tables(length, width // HEADS)

    def block_of(hop):
        return 2 * lax.rem(ring + hops - hop, hops) + y_bit

    def blank(shape, *wait):
        return jnp.broadcast_to(together(jnp.zeros((), BF), *wait)[0], shape)

    def place_rows(buffer, item, index):
        return put(buffer, item, fsdp_place ^ index)

    def half_at(index, half):
        return 2 * (fsdp_place ^ index) + half

    def put_whole(buffer, item, index):
        return lax.dynamic_update_slice(buffer, item.reshape((2,) + buffer.shape[1:]), (half_at(index, 0), 0, 0))

    piece = jnp.concatenate(
        [lax.dynamic_slice_in_dim(item, place * part, part, 1) for item in (w_query, w_key, w_value)]
        + [jnp.pad(jnp.stack([gain_attn, gain_mlp], axis=1), ((0, 0), (0, 126)))],
        axis=1,
    )
    w_qkv = lax.all_gather(piece, ("x", "core"), axis=0, tiled=True)
    z, y = ring_on(tokens), swap_y(tokens)

    t, y = together(z, y)
    hop_1, y_0 = t, y
    z, y = ring_on(hop_1), swap_y(hop_1)
    out_near = lax.all_gather(after(w_out, t), "core", axis=0, tiled=True)
    out_half = lax.dynamic_slice_in_dim(after(w_out, t), y_bit * (width // 8), width // 8, 0)
    size = w_down.shape[0] // ctx
    down_both = lax.dynamic_slice_in_dim(after(w_down, t), 2 * ring * size, 2 * size, 0)
    own, other, to_send = shared_columns(
        after(w_gate, t), w_up, jnp.stack([ring, core, y_bit]).astype(jnp.int32), fsdp, hops
    )
    half_rows = width // 8

    t, y, to_send, down_both, out_half = together(z, y, to_send, down_both, out_half)
    hop_2, y_1 = t, y
    z, y = ring_on(hop_2), swap_y(hop_2)
    out_straight = swap_x(out_half)
    first_all = blank((ctx,) + tokens.shape, t)

    t, y, first_all, w_qkv = together(z, y, first_all, w_qkv)
    hop_3, y_2 = t, y
    y = swap_y(hop_3)
    cot_1 = ring_on(after(cotangent, t))
    gains_all = w_qkv[:, 3 * part :].astype(F32).T
    gain_one, gain_two = gains_all[0], gains_all[1]

    def take_rows(buffer, item, hop, mate):
        normed = (norm_parts(item.astype(F32))[0] * gain_one).astype(BF)
        return put(buffer, normed, block_of(hop) ^ mate)

    for item, hop, mate in ((tokens, 0, 0), (y_0, 0, 1), (hop_1, 1, 0), (y_1, 1, 1), (hop_2, 2, 0), (y_2, 2, 1)):
        first_all = take_rows(first_all, item, hop, mate)
    first_all = take_rows(first_all, hop_3, 3, 0)

    t, cot_1, first_all, out_straight = together(y, cot_1, first_all, out_straight)
    cot_2 = ring_on(cot_1)
    out_far = lax.all_gather(out_straight, ("core", "y"), axis=0, tiled=True)
    arriving_own = swap_x(after(to_send[:half_rows], t))
    first_all = take_rows(first_all, t, 3, 1).reshape(length, width)
    raw = dot(w_qkv, first_all, 0, 1)
    mixed, query, key, value, logs = attend(raw, cosine, sine, heads, ctx)

    t, cot_2, down_both, arriving_own = together(mixed, cot_2, down_both, arriving_own)
    arriving_other = swap_x(after(to_send[half_rows:], t))
    down_both = lax.all_gather(down_both.reshape(1, 2, 2, size // 2, width), "x", axis=0, tiled=True)
    mixed_own = lax.all_to_all(t, sequence, 0, 0, tiled=True)
    gate_up_near = swap_core(after(other, t))
    cot_near, cot_near_1, cot_near_2 = [swap_core(after(item, t)) for item in (cotangent, cot_1, cot_2)]
    w_gate_up = put_whole(blank((8, half_rows, own.shape[1]), t), own, 0)

    t, gate_up_near, cot_near, cot_near_1, cot_near_2, w_gate_up, out_near, out_far = together(
        mixed_own, gate_up_near, cot_near, cot_near_1, cot_near_2, w_gate_up, out_near, out_far
    )
    crossing_own = swap_y(after(arriving_own, t))
    cot_3 = ring_on(after(cot_2, t))
    mixed_own = t.reshape(width, rows)
    inputs = tokens.astype(F32)
    mixed_halves = mixed_own.reshape(2, width // 2, rows)
    middle = inputs + dot(pick(mixed_halves, x_bit), out_near, 0, 0) + dot(pick(mixed_halves, 1 - x_bit), out_far, 0, 0)
    normed_mid, scale_mid = norm_parts(middle)
    second = (normed_mid * gain_two).astype(BF)

    t, cot_3, w_gate_up, gate_up_near, arriving_other = together(
        second, cot_3, w_gate_up, gate_up_near, arriving_other
    )
    z, near_0 = ring_on(t), swap_core(t)
    last_straight = swap_core(after(arriving_other, t))
    cot_near_3 = swap_core(after(cot_3, t))
    w_gate_up = put_whole(w_gate_up, gate_up_near, 1)
    w_gate_up = put(w_gate_up, arriving_own, half_at(2, y_bit))

    t, near_0, cot_near_3, w_gate_up, crossing_own, last_straight = together(
        z, near_0, cot_near_3, w_gate_up, crossing_own, last_straight
    )
    hop_1 = t
    z, near_1 = ring_on(t), swap_core(t)
    crossing_other = swap_y(after(arriving_other, t))
    w_gate_up = put(w_gate_up, crossing_own, half_at(2, 1 - y_bit))
    w_gate_up = put(w_gate_up, last_straight, half_at(3, y_bit))
    down_share = blank((2, 2, 2, size // 2, width), t)

    t, near_1, w_gate_up, down_share = together(z, near_1, w_gate_up, down_share)
    hop_2 = t
    z, near_2 = ring_on(t), swap_core(t)
    cot_all = jnp.concatenate(
        [cot_1, cot_near_1, cot_2, cot_near_2, cot_3, cot_near_3, cotangent, cot_near], axis=0
    )

    t, near_2, crossing_other, cot_all, w_gate_up, down_both = together(
        z, near_2, crossing_other, cot_all, w_gate_up, down_both
    )
    down_near = swap_core(pick(down_both, 1 - core, 2))
    down_at = lambda blocks, item, i: lax.dynamic_update_slice(blocks, item[:, None], (0, i, 0, 0, 0))
    down_share = down_at(down_share, pick(down_both, core, 2), core)
    near_3 = swap_core(t)
    last_crossed = swap_core(crossing_other)
    second_all = jnp.concatenate([hop_1, near_1, hop_2, near_2, t, near_3, second, near_0], axis=0)
    w_gate_up = put(w_gate_up, last_crossed, half_at(3, 1 - y_bit)).reshape(width, -1)
    down_share = down_at(down_share, down_near, 1 - core).reshape(-1, width)

    buffers = [blank((length, share), t) for _ in range(3)]
    half = length // 2

    def run_middle(start, buffers, rows_in):
        items = mlp_middle(rows_in, cot_all[start : start + half], w_gate_up, down_share)
        return items, [lax.dynamic_update_slice(buffer, item, (start, 0)) for buffer, item in zip(buffers, items)]

    def run_back(items):
        back = dot(jnp.concatenate(items[1:], axis=1), w_gate_up, 1, 1).astype(BF)
        return [back[i * rows : (i + 1) * rows] for i in range(4)]

    items, buffers = run_middle(0, buffers, second_all[:half])
    own_1, other_1, own_2, other_2 = run_back(items)
    near_1, near_2 = swap_core(other_1), swap_core(other_2)
    t = add(own_1, near_1).astype(BF)
    z = ring_on(t)
    items, buffers = run_middle(half, buffers, after(second_all[half:], t))
    z, near_2, *items = together(z, near_2, *items)
    t = add(own_2, near_2, z).astype(BF)
    z = ring_on(t)
    items[0] = after(items[0], t)
    items[1] = after(items[1], t)
    own_3, other_3, own_0, other_0 = run_back(items)
    near_3, near_0 = swap_core(other_3), swap_core(other_0)
    z, near_3, near_0, hidden, grad_gate, grad_up = together(z, near_3, near_0, *buffers)

    def given(blocks, bit, dim):
        return pick(blocks, 1 - bit, dim)

    def kept(blocks, bit, dim, arrived):
        return add(pick(blocks, bit, dim), arrived).astype(BF)

    def half_sum(partial):
        return lax.psum_scatter(partial.astype(BF), "x", scatter_dimension=0, tiled=True)

    t = add(own_3, near_3, z).astype(BF)
    z = ring_on(t)
    gate_partial = dot(after(second_all, t), grad_gate, 0, 0).astype(BF)
    gate_sum = half_sum(gate_partial)
    t, gate_partial = together(z, gate_partial)

    grad_second = add(own_0, near_0, t)
    gain_mlp_term = jnp.sum(grad_second * normed_mid, axis=0)
    grad_middle = cotangent.astype(F32) + norm_back(grad_second * gain_two, normed_mid, scale_mid)
    grad_branch = grad_middle.astype(BF)
    grad_mixed_own = halves(
        dot(out_near, grad_branch, 1, 1).astype(BF), dot(out_far, grad_branch, 1, 1).astype(BF), x_bit
    )

    t, hidden = together(grad_mixed_own, hidden)
    grad_mixed = lax.all_to_all(t.reshape(ctx, part, -1), sequence, 0, 0, tiled=True)
    branch_1, branch_y0 = ring_on(after(grad_branch, t)), swap_y(after(grad_branch, t))
    up_partial = dot(after(second_all, t), grad_up, 0, 0).astype(BF)
    out_partial = dot(hidden, down_share, 1, 0).astype(BF)
    out_near_1 = swap_core(out_partial[rows : 2 * rows])

    t, out_near_1, out_partial, up_partial, gate_sum, branch_1, branch_y0 = together(
        grad_mixed, out_near_1, out_partial, up_partial, gate_sum, branch_1, branch_y0
    )
    up_sum = half_sum(up_partial)
    out = [out_partial[i * rows : (i + 1) * rows] for i in range(2 * hops)]
    gate_sum = gate_sum.reshape(2, hops, 2, own_rows, share)
    gate_y = swap_y(given(gate_sum, y_bit, 2))
    branch_2 = ring_on(after(branch_1, t))
    out_sum = add(out[0], out_near_1).astype(BF)
    out_z = ring_on(out_sum)
    out_near_2 = swap_core(after(out[3], t))
    grad_raw = attend_back(query, key, value, mixed, t, logs, cosine, sine, heads, ctx)
    grad_raw = grad_raw.reshape(-1, length)
    first_partial = dot(grad_raw, w_qkv[:, : 3 * part], 0, 1).astype(BF)

    t, out_near_2, grad_raw, branch_2, gate_y = together(first_partial, out_near_2, grad_raw, branch_2, gate_y)
    first_blocks = t.reshape(ctx, rows, width)
    first_own = lambda hop: pick(first_blocks, block_of(hop))
    first_other = lambda hop: pick(first_blocks, block_of(hop) ^ 1)
    y = swap_y(first_other(1))
    out_near_3 = swap_core(after(out[5], t))
    down_partial = dot(hidden, after(cot_all, t), 0, 0).astype(BF)
    head_partial = dot(after(first_all, t), grad_raw, 0, 1).astype(BF).reshape(2, 2, ctx * own_rows, -1)
    head_near = swap_core(given(head_partial, core, 1))

    t, out_near_3, head_partial, head_near, out_z, down_partial = together(
        y, out_near_3, head_partial, head_near, out_z, down_partial
    )
    down_sum = half_sum(down_partial).reshape(2, 2, -1, width)
    total = add(first_own(1), t).astype(BF)
    z, y = ring_on(total), swap_y(after(first_other(2), t))
    out_sum = add(out[2], out_near_2, out_z).astype(BF)
    head_sum = kept(head_partial, core, 1, head_near)
    head_given = given(head_sum, x_bit, 0)
    gate_sum = kept(gate_sum, y_bit, 2, gate_y)
    products = first_partial.astype(F32) * after(first_all, t).astype(F32)
    gain_attn_term = jnp.sum(products, axis=0) / gain_one

    t, y, out_sum, head_sum, head_given, gate_sum, gain_attn_term = together(
        z, y, out_sum, head_sum, head_given, gate_sum, gain_attn_term
    )
    total = add(first_own(2), y, t).astype(BF)
    z, y = ring_on(total), swap_y(after(first_other(3), t))
    out_near_0 = swap_core(after(out[7], t))

    gain_terms = jnp.stack([gain_attn_term, gain_mlp_term]).reshape(2, fsdp * ctx, own_rows).transpose(1, 0, 2)
    gain_terms = lax.all_to_all(after(gain_terms, t), ("x", "core") + sequence, 0, 0, tiled=True)

    t, y, out_near_0, up_sum, gain_terms = together(z, y, out_near_0, up_sum, gain_terms)
    total = add(first_own(3), y, t).astype(BF)
    z, y = ring_on(total), swap_y(after(first_other(0), t))
    head_x = swap_x(after(head_given, t))
    up_sum = up_sum.reshape(2, hops, 2, own_rows, share)
    up_given = given(up_sum, y_bit, 2)

    def deal_rows(summed):
        received = lax.all_to_all(summed.reshape(2 * hops, own_rows, -1), ("core", "z"), 0, 0, tiled=True)
        return received.reshape(2, hops, own_rows, -1)

    t, y, up_given = together(z, y, up_given)
    up_y = swap_y(up_given)
    gate_dealt = deal_rows(after(gate_sum, t))
    branch_3, branch_y1, branch_y2 = ring_on(after(branch_2, t)), swap_y(after(branch_1, t)), swap_y(after(branch_2, t))
    out_z = ring_on(after(out_sum, t))
    grad_first = add(first_own(0), y, t)
    inputs_normed, scale_attn = norm_parts(inputs)
    input_grad = (grad_middle + norm_back(grad_first * gain_one, inputs_normed, scale_attn)).astype(BF)
    down_given = given(down_sum, y_bit, 1)

    t, branch_3, out_z, input_grad, down_given = together(up_y, branch_3, out_z, input_grad, down_given)
    branch_y3 = swap_y(branch_3)
    up_both = kept(up_sum, y_bit, 2, t)
    out_z = ring_on(add(out[4], out_near_3, out_z).astype(BF))

    t, branch_y1, branch_y2, branch_y3, head_x, gate_dealt, up_both = together(
        out_z, branch_y1, branch_y2, branch_y3, head_x, gate_dealt, up_both
    )
    up_dealt = deal_rows(up_both)
    down_y = swap_y(after(down_given, t))
    gate_grad, up_grad = hidden_columns(gate_dealt, fsdp), hidden_columns(up_dealt, fsdp)
    branches = ((grad_branch, branch_y0), (branch_1, branch_y1), (branch_2, branch_y2), (branch_3, branch_y3))
    branch_all = jnp.concatenate([item for pair in branches for item in pair], axis=0)
    mixed_rows = jnp.concatenate([pick(mixed, block_of(hop) ^ i) for hop in range(hops) for i in range(2)], axis=1)
    out_weight = dot(mixed_rows, branch_all, 1, 0).astype(BF).reshape(2, 2, own_rows, width)
    weight = kept(out_weight, core, 1, swap_core(given(out_weight, core, 1)))
    weight_x = swap_x(given(weight, x_bit, 0))
    output = (middle + add(out[6], out_near_0, t)).astype(BF)
    head_rows = lax.all_to_all(after(kept(head_sum, x_bit, 0, head_x), up_dealt), sequence, 0, 0, tiled=True)

    weight = kept(weight, x_bit, 0, weight_x)
    pairs = [(i * ctx + j, j * fsdp + i) for i in range(fsdp) for j in range(ctx)]
    out_grad = lax.ppermute(weight, ("x", "core") + sequence, pairs).astype(F32)
    down_sum = kept(down_sum, y_bit, 1, down_y)
    down_near = swap_core(pick(down_sum, 1 - core))
    down_grad = halves(pick(down_sum, core), down_near, core).reshape(-1, width).astype(F32)
    query_grad, key_grad, value_grad = head_columns(head_rows.reshape(ctx, own_rows, -1))

    gain_grads = jnp.sum(gain_terms, axis=0)
    return (
        output,
        input_grad,
        gain_grads[0],
        query_grad,
        key_grad,
        value_grad,
        out_grad,
        gain_grads[1],
        gate_grad,
        up_grad,
        down_grad,
    )


def solution(mesh):
    fsdp, ctx = ("fsdp",), ("ctx",)
    body = general_body
    if mesh.devices.shape == (4, 8):
        body, fsdp, ctx = paired_body, ("x", "core"), ("z", "y")
        mesh = jax.sharding.Mesh(mesh.devices.reshape(2, 2, 4, 2), fsdp + ctx)
    rows, matrix = P(fsdp + ctx, None), P(fsdp, None)
    in_specs = (rows, P(fsdp), matrix, matrix, matrix, matrix, P(fsdp), matrix, matrix, matrix, rows)
    out_specs = (rows, rows, P(fsdp + ctx), rows, rows, rows, rows, P(fsdp + ctx), rows, rows, rows)
    return jax.shard_map(body, mesh=mesh, in_specs=in_specs, out_specs=out_specs, check_vma=False)
```

```python
import functools

import jax
import jax.numpy as jnp
import numpy as np
from jax import lax
from jax.experimental import pallas as pl
from jax.experimental.pallas import tpu as pltpu
from jax.sharding import PartitionSpec as P

HEADS = 32
EPS = 1e-05
THETA = 130000.0
MASKED = -1e30
BF = jnp.bfloat16
F32 = jnp.float32


def dot(left, right, left_axis, right_axis):
    return lax.dot_general(
        left, right, (((left_axis,), (right_axis,)), ((), ())), preferred_element_type=F32
    )


def norm_parts(matrix):
    scale = lax.rsqrt(jnp.mean(matrix * matrix, axis=-1, keepdims=True) + EPS)
    return (matrix * scale, scale)


def norm_back(grad_scaled, normed, scale):
    return scale * (grad_scaled - normed * jnp.mean(grad_scaled * normed, axis=-1, keepdims=True))


def angle_tables(length, head_width):
    half = head_width // 2
    freqs = np.float32(THETA) ** (-(np.arange(half, dtype=np.float32) * np.float32(2.0 / head_width)))
    angles = freqs[:, None].astype(np.float32) * np.arange(length, dtype=np.float32)[None, :]
    return jnp.asarray(np.cos(angles), F32), jnp.asarray(np.sin(angles), F32)


def low_lanes(block):
    return lax.broadcasted_iota(jnp.int32, block.shape, 1) < block.shape[1] // 2


def sort_columns(matrix, blocks):
    size = matrix.shape[1] // blocks
    early, late = [], []
    for j in range(blocks // 2):
        first = matrix[:, 2 * j * size : (2 * j + 1) * size]
        second = pltpu.roll(matrix[:, (2 * j + 1) * size : (2 * j + 2) * size], size // 2, 1)
        low = low_lanes(first)
        early.append(jnp.where(low, first, second))
        late.append(jnp.where(low, second, first))
    return jnp.concatenate(early + late[::-1], axis=1)


def deal_columns(matrix, blocks):
    size = matrix.shape[1] // blocks
    out = []
    for j in range(blocks // 2):
        early = matrix[:, j * size : (j + 1) * size]
        late = matrix[:, (blocks - 1 - j) * size : (blocks - j) * size]
        low = low_lanes(early)
        out.append(jnp.where(low, early, late))
        out.append(pltpu.roll(jnp.where(low, late, early), size // 2, 1))
    return jnp.concatenate(out, axis=1)


def turn(matrix, cosine, sine):
    half = matrix.shape[0] // 2
    first, second = matrix[:half], matrix[half:]
    return jnp.concatenate([first * cosine - second * sine, second * cosine + first * sine], axis=0)


def by_blocks(ref):
    return jnp.concatenate([ref[block].astype(F32) for block in range(ref.shape[0])], axis=1)


def masked_block(scores, chunk):
    keys = scores.shape[0]
    places = lax.broadcasted_iota(jnp.int32, (chunk, chunk), 0)
    wants = lax.broadcasted_iota(jnp.int32, (chunk, chunk), 1)
    last = jnp.where(places <= wants, scores[keys - chunk :], MASKED)
    if keys == chunk:
        return last
    return jnp.concatenate([scores[: keys - chunk], last], axis=0)


def attend_kernel(blocks, chunk, q_ref, k_ref, v_ref, cos_ref, sin_ref, o_ref, qs_ref, ks_ref, vs_ref, lse_ref):
    width, length = q_ref.shape
    cosine, sine = cos_ref[...], sin_ref[...]
    query = turn(sort_columns(q_ref[...], blocks), cosine, sine).astype(BF)
    key = turn(sort_columns(k_ref[...], blocks), cosine, sine).astype(BF)
    value = sort_columns(v_ref[...], blocks).astype(BF)
    scaled = query * jnp.asarray(width ** (-0.5), BF)
    qs_ref[...] = scaled
    ks_ref[...] = key
    vs_ref[...] = value
    mixed, logs = [], []
    for i in range(length // chunk):
        count = (i + 1) * chunk
        scores = dot(key[:, :count], scaled[:, i * chunk : count], 0, 0)
        scores = masked_block(scores, chunk)
        top = jnp.max(scores, axis=0, keepdims=True)
        raised = jnp.exp(scores - top)
        total = jnp.sum(raised, axis=0, keepdims=True)
        mixed.append(dot(value[:, :count], raised.astype(BF), 1, 0) / total)
        logs.append(top + jnp.log(total))
    size = length // blocks
    dealt = deal_columns(jnp.concatenate(mixed, axis=1), blocks).astype(BF)
    for block in range(blocks):
        o_ref[block] = dealt[:, block * size : (block + 1) * size]
    lse_ref[0] = jnp.concatenate(logs, axis=1)


def attend_back_kernel(blocks, chunk, q_ref, k_ref, v_ref, o_ref, do_ref, lse_ref, cos_ref, sin_ref, d_ref, dk_ref, dv_ref):
    width, length = q_ref.shape
    factor = width ** (-0.5)
    cosine, sine = cos_ref[...], -sin_ref[...]
    scaled, key, value = q_ref[...], k_ref[...], v_ref[...]
    grad_f32 = sort_columns(by_blocks(do_ref), blocks)
    center = jnp.sum(grad_f32 * sort_columns(by_blocks(o_ref), blocks), axis=0, keepdims=True)
    grad = grad_f32.astype(BF)
    logs = lse_ref[0]
    dq = []
    for i in reversed(range(length // chunk)):
        count = (i + 1) * chunk
        here = slice(i * chunk, count)
        scores = masked_block(dot(key[:, :count], scaled[:, here], 0, 0), chunk)
        shares = jnp.exp(scores - logs[:, here])
        grad_shares = dot(value[:, :count], grad[:, here], 0, 0)
        grad_scores = (shares * (grad_shares - center[:, here])).astype(BF)
        dq.append(dot(key[:, :count], grad_scores, 1, 0))
        dk_part = dot(scaled[:, here], grad_scores, 1, 1)
        dv_part = dot(grad[:, here], shares.astype(BF), 1, 1)
        if count == length:
            dk_ref[...] = dk_part
            dv_ref[...] = dv_part
        else:
            dk_ref[:, :count] += dk_part
            dv_ref[:, :count] += dv_part
    dq = turn(jnp.concatenate(dq[::-1], axis=1) * factor, cosine, sine)
    d_ref[0] = deal_columns(dq, blocks).astype(BF)
    d_ref[1] = deal_columns(turn(dk_ref[...], cosine, sine), blocks).astype(BF)
    d_ref[2] = deal_columns(dv_ref[...], blocks).astype(BF)


def attend(raw, cosine, sine, heads, blocks):
    width, length = 2 * cosine.shape[0], raw.shape[1]
    chunk = min(256, length)
    head = lambda shift: pl.BlockSpec((width, length), lambda h: (h + shift * heads, 0))
    table = pl.BlockSpec((width // 2, length), lambda h: (0, 0))
    flat = jax.ShapeDtypeStruct((heads * width, length), BF)
    return pl.pallas_call(
        functools.partial(attend_kernel, blocks, chunk),
        grid=(heads,),
        in_specs=[head(0), head(1), head(2), table, table],
        out_specs=[
            pl.BlockSpec((blocks, width, length // blocks), lambda h: (0, h, 0)),
            head(0),
            head(0),
            head(0),
            pl.BlockSpec((1, 1, length), lambda h: (h, 0, 0)),
        ],
        out_shape=[
            jax.ShapeDtypeStruct((blocks, heads * width, length // blocks), BF),
            flat,
            flat,
            flat, jax.ShapeDtypeStruct((heads, 1, length), F32),
        ],
        compiler_params=pltpu.CompilerParams(vmem_limit_bytes=40 * 1024 * 1024),
        name="attend",
    )(raw, raw, raw, cosine, sine)


def attend_back(query, key, value, mixed, grad, logs, cosine, sine, heads, blocks):
    width, length = query.shape[0] // heads, query.shape[1]
    chunk = min(256, length)
    head = pl.BlockSpec((width, length), lambda h: (h, 0))
    block = pl.BlockSpec((blocks, width, length // blocks), lambda h: (0, h, 0))
    table = pl.BlockSpec((width // 2, length), lambda h: (0, 0))
    return pl.pallas_call(
        functools.partial(attend_back_kernel, blocks, chunk),
        grid=(heads,),
        in_specs=[head, head, head, block, block, pl.BlockSpec((1, 1, length), lambda h: (h, 0, 0)), table, table],
        out_specs=pl.BlockSpec((3, width, length), lambda h: (0, h, 0)),
        out_shape=jax.ShapeDtypeStruct((3, heads * width, length), BF),
        scratch_shapes=[pltpu.VMEM((width, length), F32), pltpu.VMEM((width, length), F32)],
        compiler_params=pltpu.CompilerParams(vmem_limit_bytes=40 * 1024 * 1024),
        name="attend_back",
    )(query, key, value, mixed, grad, logs, cosine, sine)


def swap(item, axis, bit):
    pairs = [(i, i ^ bit) for i in range(lax.axis_size(axis))]
    return lax.ppermute(item, axis, pairs)


def step_on(item):
    count = lax.axis_size("ctx")
    return lax.ppermute(item, "ctx", [(i, (i + 2) % count) for i in range(count)])


def after(item, *others):
    return lax.optimization_barrier((item,) + others)[0]


def gather_rows(piece):
    count, place = lax.axis_size("ctx"), lax.axis_index("ctx")
    rows = jnp.zeros((count,) + piece.shape, piece.dtype)
    for hop in range(count // 2):
        if hop:
            piece = step_on(piece)
        source = lax.rem(place + count - 2 * hop, count)
        rows = lax.dynamic_update_slice(rows, piece[None], (source, 0, 0))
        rows = lax.dynamic_update_slice(rows, swap(piece, "ctx", 1)[None], (source ^ 1, 0, 0))
    return rows.reshape(-1, rows.shape[2])


def scatter_rows(partial):
    count, place = lax.axis_size("ctx"), lax.axis_index("ctx")
    blocks = partial.astype(BF).reshape(count, -1, partial.shape[1])
    total = None
    for hop in range(1, count // 2 + 1):
        target = lax.rem(place + count - 2 * hop, count)
        mine = lax.dynamic_index_in_dim(blocks, target, 0, keepdims=False)
        other = lax.dynamic_index_in_dim(blocks, target ^ 1, 0, keepdims=False)
        term = mine.astype(F32) + swap(other, "ctx", 1).astype(F32)
        total = term if total is None else term + total.astype(F32)
        if hop < count // 2:
            total = step_on(total.astype(BF))
    return total


def gather_weight(piece):
    if lax.axis_size("fsdp") != 4:
        return lax.all_gather(piece, "fsdp", axis=0, tiled=True)
    place = lax.axis_index("fsdp")
    rows = jnp.zeros((4,) + piece.shape, piece.dtype)
    far = swap(piece, "fsdp", 2)
    for source, item in (
        (place, piece),
        (place ^ 1, swap(piece, "fsdp", 1)),
        (place ^ 2, far),
        (place ^ 3, swap(far, "fsdp", 1)),
    ):
        rows = lax.dynamic_update_slice(rows, item[None], (source, 0, 0))
    return rows.reshape(-1, piece.shape[1])


def scatter(partial, axis):
    return lax.psum_scatter(partial.astype(BF), axis, scatter_dimension=0, tiled=True)


def general_body(
    tokens, gain_attn, w_query, w_key, w_value, w_out, gain_mlp, w_gate, w_up, w_down, cotangent
):
    width = tokens.shape[1]
    hidden_width = w_gate.shape[1]
    fsdp, ctx = lax.axis_size("fsdp"), lax.axis_size("ctx")
    place = lax.axis_index("ctx")
    length = tokens.shape[0] * ctx
    heads = HEADS // ctx
    part = width // ctx
    share = hidden_width // ctx
    own_rows = width // (fsdp * ctx)
    cosine, sine = angle_tables(length, width // HEADS)

    def head_columns(weight):
        return lax.dynamic_slice_in_dim(weight, place * part, part, 1)

    def hidden_columns(weight):
        rows = weight.shape[0]
        blocks = weight.reshape(rows, fsdp, ctx, share // fsdp)
        return lax.dynamic_index_in_dim(blocks, place, 2, keepdims=False).reshape(rows, share)

    def to_owners(partial):
        summed = scatter(partial, "fsdp")
        return lax.all_to_all(summed, "ctx", 0, 0, tiled=True).reshape(ctx, own_rows, -1).astype(F32)

    def of_heads(received):
        return received.transpose(1, 0, 2).reshape(own_rows, -1)

    def of_hidden(received):
        blocks = received.reshape(ctx, own_rows, fsdp, -1)
        return blocks.transpose(1, 2, 0, 3).reshape(own_rows, -1)

    def normed_rows(rows):
        return norm_parts(rows.astype(F32))[0]

    w_qkv_piece = jnp.concatenate([head_columns(item) for item in (w_query, w_key, w_value)], axis=1)
    w_qkv = gather_weight(w_qkv_piece)
    gains = lax.all_gather(jnp.stack([gain_attn, gain_mlp]), "fsdp", axis=1, tiled=True).astype(F32)
    gain_one, gain_two = gains[0], gains[1]
    tokens_all = gather_rows(tokens)
    first_all = (normed_rows(tokens_all) * gain_one).astype(BF)
    raw = dot(w_qkv, first_all, 0, 1)
    mixed, query, key, value, logs = attend(raw, cosine, sine, heads, ctx)
    w_out_all = gather_weight(after(w_out, w_qkv))
    w_gate_up = gather_weight(
        after(jnp.concatenate([hidden_columns(w_gate), hidden_columns(w_up)], axis=1), w_out_all)
    )
    down_size = w_down.shape[0] // ctx
    down_share = gather_weight(
        after(lax.dynamic_slice_in_dim(w_down, place * down_size, down_size, 0), w_gate_up)
    )
    cotangent_all = gather_rows(after(cotangent, tokens_all))

    inputs = tokens.astype(F32)
    mixed_own = lax.all_to_all(mixed, "ctx", 0, 0, tiled=True).reshape(width, -1)
    middle = inputs + dot(mixed_own, w_out_all, 0, 0)
    normed_mid, scale_mid = norm_parts(middle)
    second_all = gather_rows((normed_mid * gain_two).astype(BF))
    gate_up = dot(second_all, w_gate_up, 1, 0)
    gate, upward = gate_up[:, :share], gate_up[:, share:]
    grad_hidden = dot(cotangent_all, down_share, 1, 1)
    sigmoid = jax.nn.sigmoid(gate)
    hidden = (gate * sigmoid * upward).astype(BF)
    grad_gate = (grad_hidden * upward * (sigmoid + gate * sigmoid * (1.0 - sigmoid))).astype(BF)
    grad_up = (grad_hidden * (gate * sigmoid)).astype(BF)
    grad_gate_up = jnp.concatenate([grad_gate, grad_up], axis=1)
    grad_second = scatter_rows(dot(grad_gate_up, w_gate_up, 1, 1))
    output = (middle + scatter_rows(after(dot(hidden, down_share, 1, 0), grad_second))).astype(BF)

    gain_mlp_term = jnp.sum(grad_second * normed_mid, axis=0)
    grad_middle = cotangent.astype(F32) + norm_back(grad_second * gain_two, normed_mid, scale_mid)
    grad_branch = grad_middle.astype(BF)
    grad_mixed_own = dot(w_out_all, grad_branch, 1, 1).astype(BF)
    grad_mixed = lax.all_to_all(grad_mixed_own.reshape(ctx, part, -1), "ctx", 0, 0, tiled=True)
    grad_raw = attend_back(query, key, value, mixed, grad_mixed, logs, cosine, sine, heads, ctx)
    grad_raw = grad_raw.reshape(-1, length)
    branch_all = gather_rows(after(grad_branch, grad_mixed))
    first_partial = dot(grad_raw, w_qkv, 0, 1)
    grad_first = scatter_rows(first_partial)
    inputs_normed, scale_attn = norm_parts(inputs)
    gain_attn_term = jnp.sum(grad_first * inputs_normed, axis=0)
    input_grad = (grad_middle + norm_back(grad_first * gain_one, inputs_normed, scale_attn)).astype(BF)

    down_grad = scatter(dot(hidden, cotangent_all, 0, 0), "fsdp").astype(F32)
    mixed_rows = mixed.transpose(1, 0, 2).reshape(part, length)
    out_grad = scatter(dot(mixed_rows, branch_all, 1, 0), "fsdp")
    out_grad = lax.ppermute(
        out_grad,
        ("fsdp", "ctx"),
        [(i * ctx + j, j * fsdp + i) for i in range(fsdp) for j in range(ctx)],
    ).astype(F32)
    gate_up_rows = to_owners(dot(second_all, grad_gate_up, 0, 0))
    qkv_rows = to_owners(dot(first_all, grad_raw, 0, 1))
    gain_terms = jnp.stack([gain_attn_term, gain_mlp_term]).reshape(2, fsdp * ctx, own_rows)
    gain_grads = jnp.sum(
        lax.all_to_all(gain_terms.transpose(1, 0, 2), ("fsdp", "ctx"), 0, 0, tiled=True), axis=0
    )
    return (
        output,
        input_grad,
        gain_grads[0],
        of_heads(qkv_rows[:, :, :part]),
        of_heads(qkv_rows[:, :, part : 2 * part]),
        of_heads(qkv_rows[:, :, 2 * part :]),
        out_grad,
        gain_grads[1],
        of_hidden(gate_up_rows[:, :, :share]),
        of_hidden(gate_up_rows[:, :, share:]),
        down_grad,
    )


def together(*items):
    return lax.optimization_barrier(items)


def pick(blocks, index, axis=0):
    return lax.dynamic_index_in_dim(blocks, index, axis, keepdims=False)


def put(blocks, item, index):
    return lax.dynamic_update_slice(blocks, item[None], (index,) + (0,) * item.ndim)


def halves(own, other, index):
    return put(put(jnp.zeros((2,) + own.shape, own.dtype), own, index), other, 1 - index)


def add(*items):
    return sum(item.astype(F32) for item in items)


def swap_pair(item, axis):
    return lax.ppermute(item, axis, [(0, 1), (1, 0)])


def swap_x(item):
    return swap_pair(item, "x")


def swap_core(item):
    return swap_pair(item, "core")


def swap_y(item):
    return swap_pair(item, "y")


def ring_on(item, steps=1):
    count = lax.axis_size("z")
    return lax.ppermute(item, "z", [(i, (i + steps) % count) for i in range(count)])


def columns_kernel(place_ref, gate_ref, up_ref, own_ref, other_ref, halves_ref):
    step, steps = pl.program_id(0), pl.num_programs(0)
    size, half = own_ref.shape[1] // 2, halves_ref.shape[0] // 2
    rows = pl.ds(pl.multiple_of(place_ref[2] * half, half), half)

    def take(weight_ref):
        for block in range(2):
            own = pl.ds(pl.multiple_of((2 * block + place_ref[1]) * size, size), size)
            other = pl.ds(pl.multiple_of((2 * block + 1 - place_ref[1]) * size, size), size)
            into = slice(block * size, (block + 1) * size)
            own_ref[:, into] = weight_ref[:, own]
            other_ref[:, into] = weight_ref[:, other]
            halves_ref[:half, into] = weight_ref[rows, own]
            halves_ref[half:, into] = weight_ref[rows, other]

    @pl.when(step < steps // 2)
    def _():
        take(gate_ref)

    @pl.when(step >= steps // 2)
    def _():
        take(up_ref)


def shared_columns(w_gate, w_up, place, blocks, rings):
    rows, columns = w_gate.shape
    size = columns // (blocks * rings * 2)
    gate = pl.BlockSpec((rows, 2 * size), lambda s, at: (0, jnp.minimum(s, blocks - 1) * rings + at[0]))
    up = pl.BlockSpec((rows, 2 * size), lambda s, at: (0, jnp.maximum(s - blocks, 0) * rings + at[0]))
    wide = 2 * blocks * size
    return pl.pallas_call(
        columns_kernel,
        grid_spec=pltpu.PrefetchScalarGridSpec(
            num_scalar_prefetch=1,
            grid=(2 * blocks,),
            in_specs=[gate, up],
            out_specs=[pl.BlockSpec((rows, size), lambda s, at: (0, s))] * 3,
        ),
        out_shape=[jax.ShapeDtypeStruct((rows, wide), BF)] * 3,
        compiler_params=pltpu.CompilerParams(vmem_limit_bytes=56 * 1024 * 1024),
        name="columns",
    )(place, w_gate, w_up)


def mlp_middle(second, cotangent, w_gate_up, down_share):
    share = down_share.shape[0]
    gate_up = dot(second, w_gate_up, 1, 0)
    gate, upward = gate_up[:, :share], gate_up[:, share:]
    grad_hidden = dot(cotangent, down_share, 1, 1)
    sigmoid = jax.nn.sigmoid(gate)
    hidden = (gate * sigmoid * upward).astype(BF)
    grad_gate = (grad_hidden * upward * (sigmoid + gate * sigmoid * (1.0 - sigmoid))).astype(BF)
    grad_up = (grad_hidden * (gate * sigmoid)).astype(BF)
    return hidden, grad_gate, grad_up


def hidden_columns_kernel(in_ref, out_ref):
    cores, rings, _, wide = in_ref.shape
    size = wide // 2
    for ring in range(rings):
        for half in range(2):
            for core in range(cores):
                start = ((ring * 2 + half) * cores + core) * size
                out_ref[:, start : start + size] = in_ref[core, ring, :, half * size : (half + 1) * size].astype(F32)


def hidden_columns(received, blocks):
    cores, rings, rows, share = received.shape
    wide = share // blocks
    return pl.pallas_call(
        hidden_columns_kernel,
        grid=(blocks,),
        in_specs=[pl.BlockSpec((cores, rings, rows, wide), lambda s: (0, 0, 0, s))],
        out_specs=pl.BlockSpec((rows, cores * rings * wide), lambda s: (0, s)),
        out_shape=jax.ShapeDtypeStruct((rows, cores * rings * share), F32),
        compiler_params=pltpu.CompilerParams(vmem_limit_bytes=56 * 1024 * 1024),
        name="hidden_columns",
    )(received)


def head_columns_kernel(in_ref, *out_refs):
    count = in_ref.shape[0]
    part = in_ref.shape[2] // len(out_refs)
    for i, out_ref in enumerate(out_refs):
        for block in range(count):
            out_ref[:, block * part : (block + 1) * part] = in_ref[block, :, i * part : (i + 1) * part].astype(F32)


def head_columns(received):
    count, rows, wide = received.shape
    return pl.pallas_call(
        head_columns_kernel,
        out_shape=[jax.ShapeDtypeStruct((rows, count * wide // 3), F32)] * 3,
        compiler_params=pltpu.CompilerParams(vmem_limit_bytes=56 * 1024 * 1024),
        name="head_columns",
    )(received)


def paired_body(
    tokens, gain_attn, w_query, w_key, w_value, w_out, gain_mlp, w_gate, w_up, w_down, cotangent
):
    rows, width = tokens.shape
    hops = lax.axis_size("z")
    fsdp, ctx = 2 * lax.axis_size("x"), 2 * hops
    x_bit, core, ring, y_bit = [lax.axis_index(axis) for axis in ("x", "core", "z", "y")]
    place, fsdp_place = 2 * ring + y_bit, 2 * x_bit + core
    length = rows * ctx
    heads = HEADS // ctx
    part = width // ctx
    share = w_gate.shape[1] // ctx
    own_rows = width // (fsdp * ctx)
    sequence = ("z", "y")
    cosine, sine = angle_tables(length, width // HEADS)

    def block_of(hop):
        return 2 * lax.rem(ring + hops - hop, hops) + y_bit

    def blank(shape, *wait):
        return jnp.broadcast_to(together(jnp.zeros((), BF), *wait)[0], shape)

    def place_rows(buffer, item, index):
        return put(buffer, item, fsdp_place ^ index)

    def half_at(index, half):
        return 2 * (fsdp_place ^ index) + half

    def put_whole(buffer, item, index):
        return lax.dynamic_update_slice(buffer, item.reshape((2,) + buffer.shape[1:]), (half_at(index, 0), 0, 0))

    piece = jnp.concatenate(
        [lax.dynamic_slice_in_dim(item, place * part, part, 1) for item in (w_query, w_key, w_value)]
        + [jnp.pad(jnp.stack([gain_attn, gain_mlp], axis=1), ((0, 0), (0, 126)))],
        axis=1,
    )
    w_qkv = lax.all_gather(piece, ("x", "core"), axis=0, tiled=True)
    z, y = ring_on(tokens), swap_y(tokens)

    t, y = together(z, y)
    hop_1, y_0 = t, y
    z, y = ring_on(hop_1), swap_y(hop_1)
    out_near = lax.all_gather(after(w_out, t), "core", axis=0, tiled=True)
    out_half = lax.dynamic_slice_in_dim(after(w_out, t), y_bit * (width // 8), width // 8, 0)
    size = w_down.shape[0] // ctx
    down_both = lax.dynamic_slice_in_dim(after(w_down, t), 2 * ring * size, 2 * size, 0)
    own, other, to_send = shared_columns(
        after(w_gate, t), w_up, jnp.stack([ring, core, y_bit]).astype(jnp.int32), fsdp, hops
    )
    half_rows = width // 8

    t, y, to_send, down_both, out_half = together(z, y, to_send, down_both, out_half)
    hop_2, y_1 = t, y
    z, y = ring_on(hop_2), swap_y(hop_2)
    out_straight = swap_x(out_half)
    first_all = blank((ctx,) + tokens.shape, t)

    t, y, first_all, w_qkv = together(z, y, first_all, w_qkv)
    hop_3, y_2 = t, y
    y = swap_y(hop_3)
    cot_1 = ring_on(after(cotangent, t))
    gains_all = w_qkv[:, 3 * part :].astype(F32).T
    gain_one, gain_two = gains_all[0], gains_all[1]

    def take_rows(buffer, item, hop, mate):
        normed = (norm_parts(item.astype(F32))[0] * gain_one).astype(BF)
        return put(buffer, normed, block_of(hop) ^ mate)

    for item, hop, mate in ((tokens, 0, 0), (y_0, 0, 1), (hop_1, 1, 0), (y_1, 1, 1), (hop_2, 2, 0), (y_2, 2, 1)):
        first_all = take_rows(first_all, item, hop, mate)
    first_all = take_rows(first_all, hop_3, 3, 0)

    t, cot_1, first_all, out_straight = together(y, cot_1, first_all, out_straight)
    cot_2 = ring_on(cot_1)
    out_far = lax.all_gather(out_straight, ("core", "y"), axis=0, tiled=True)
    arriving_own = swap_x(after(to_send[:half_rows], t))
    first_all = take_rows(first_all, t, 3, 1).reshape(length, width)
    raw = dot(w_qkv, first_all, 0, 1)
    mixed, query, key, value, logs = attend(raw, cosine, sine, heads, ctx)

    t, cot_2, down_both, arriving_own = together(mixed, cot_2, down_both, arriving_own)
    arriving_other = swap_x(after(to_send[half_rows:], t))
    down_both = lax.all_gather(down_both.reshape(1, 2, 2, size // 2, width), "x", axis=0, tiled=True)
    mixed_own = lax.all_to_all(t, sequence, 0, 0, tiled=True)
    gate_up_near = swap_core(after(other, t))
    cot_near, cot_near_1, cot_near_2 = [swap_core(after(item, t)) for item in (cotangent, cot_1, cot_2)]
    w_gate_up = put_whole(blank((8, half_rows, own.shape[1]), t), own, 0)

    t, gate_up_near, cot_near, cot_near_1, cot_near_2, w_gate_up, out_near, out_far = together(
        mixed_own, gate_up_near, cot_near, cot_near_1, cot_near_2, w_gate_up, out_near, out_far
    )
    crossing_own = swap_y(after(arriving_own, t))
    cot_3 = ring_on(after(cot_2, t))
    mixed_own = t.reshape(width, rows)
    inputs = tokens.astype(F32)
    mixed_halves = mixed_own.reshape(2, width // 2, rows)
    middle = inputs + dot(pick(mixed_halves, x_bit), out_near, 0, 0) + dot(pick(mixed_halves, 1 - x_bit), out_far, 0, 0)
    normed_mid, scale_mid = norm_parts(middle)
    second = (normed_mid * gain_two).astype(BF)

    t, cot_3, w_gate_up, gate_up_near, arriving_other = together(
        second, cot_3, w_gate_up, gate_up_near, arriving_other
    )
    z, near_0 = ring_on(t), swap_core(t)
    last_straight = swap_core(after(arriving_other, t))
    cot_near_3 = swap_core(after(cot_3, t))
    w_gate_up = put_whole(w_gate_up, gate_up_near, 1)
    w_gate_up = put(w_gate_up, arriving_own, half_at(2, y_bit))

    t, near_0, cot_near_3, w_gate_up, crossing_own, last_straight = together(
        z, near_0, cot_near_3, w_gate_up, crossing_own, last_straight
    )
    hop_1 = t
    z, near_1 = ring_on(t), swap_core(t)
    crossing_other = swap_y(after(arriving_other, t))
    w_gate_up = put(w_gate_up, crossing_own, half_at(2, 1 - y_bit))
    w_gate_up = put(w_gate_up, last_straight, half_at(3, y_bit))
    down_share = blank((2, 2, 2, size // 2, width), t)

    t, near_1, w_gate_up, down_share = together(z, near_1, w_gate_up, down_share)
    hop_2 = t
    z, near_2 = ring_on(t), swap_core(t)
    cot_all = jnp.concatenate(
        [cot_1, cot_near_1, cot_2, cot_near_2, cot_3, cot_near_3, cotangent, cot_near], axis=0
    )

    t, near_2, crossing_other, cot_all, w_gate_up, down_both = together(
        z, near_2, crossing_other, cot_all, w_gate_up, down_both
    )
    down_near = swap_core(pick(down_both, 1 - core, 2))
    down_at = lambda blocks, item, i: lax.dynamic_update_slice(blocks, item[:, None], (0, i, 0, 0, 0))
    down_share = down_at(down_share, pick(down_both, core, 2), core)
    near_3 = swap_core(t)
    last_crossed = swap_core(crossing_other)
    second_all = jnp.concatenate([hop_1, near_1, hop_2, near_2, t, near_3, second, near_0], axis=0)
    w_gate_up = put(w_gate_up, last_crossed, half_at(3, 1 - y_bit)).reshape(width, -1)
    down_share = down_at(down_share, down_near, 1 - core).reshape(-1, width)

    def given(blocks, bit, dim):
        return pick(blocks, 1 - bit, dim)

    def kept(blocks, bit, dim, arrived):
        return add(pick(blocks, bit, dim), arrived).astype(BF)

    def half_sum(partial):
        return lax.psum_scatter(partial.astype(BF), "x", scatter_dimension=0, tiled=True)

    buffers = [blank((length, share), t) for _ in range(3)]
    half = length // 2

    def run_middle(start, buffers, rows_in):
        items = mlp_middle(rows_in, cot_all[start : start + half], w_gate_up, down_share)
        return items, [lax.dynamic_update_slice(buffer, item, (start, 0)) for buffer, item in zip(buffers, items)]

    def run_back(items):
        back = dot(jnp.concatenate(items[1:], axis=1), w_gate_up, 1, 1).astype(BF)
        return [back[i * rows : (i + 1) * rows] for i in range(4)]

    items, buffers = run_middle(0, buffers, second_all[:half])
    own_1, other_1, own_2, other_2 = run_back(items)
    near_1, near_2 = swap_core(other_1), swap_core(other_2)
    t = add(own_1, near_1).astype(BF)
    z = ring_on(t)
    items, buffers = run_middle(half, buffers, after(second_all[half:], t))
    z, near_2, *items = together(z, near_2, *items)
    t = add(own_2, near_2, z).astype(BF)
    z = ring_on(t)
    items[0] = after(items[0], t)
    items[1] = after(items[1], t)
    own_3, other_3, own_0, other_0 = run_back(items)
    near_3, near_0 = swap_core(other_3), swap_core(other_0)
    gate_partial = dot(after(second_all, t), buffers[1], 0, 0).astype(BF)
    z, near_3, near_0, gate_partial, hidden, grad_up = together(
        z, near_3, near_0, gate_partial, buffers[0], buffers[2]
    )
    gate_sum = half_sum(gate_partial)

    t = add(own_3, near_3, z).astype(BF)
    z = ring_on(t)
    up_partial = dot(after(second_all, t), grad_up, 0, 0).astype(BF)
    t, up_partial = together(z, up_partial)
    up_sum = half_sum(up_partial)

    grad_second = add(own_0, near_0, t)
    gain_mlp_term = jnp.sum(grad_second * normed_mid, axis=0)
    grad_middle = cotangent.astype(F32) + norm_back(grad_second * gain_two, normed_mid, scale_mid)
    grad_branch = grad_middle.astype(BF)
    grad_mixed_own = halves(
        dot(out_near, grad_branch, 1, 1).astype(BF), dot(out_far, grad_branch, 1, 1).astype(BF), x_bit
    )

    t, hidden = together(grad_mixed_own, hidden)
    grad_mixed = lax.all_to_all(t.reshape(ctx, part, -1), sequence, 0, 0, tiled=True)
    branch_1, branch_y0 = ring_on(after(grad_branch, t)), swap_y(after(grad_branch, t))
    out_partial = dot(hidden, down_share, 1, 0).astype(BF)
    out_near_1 = swap_core(out_partial[rows : 2 * rows])
    down_partial = dot(hidden, after(cot_all, t), 0, 0).astype(BF)

    t, out_near_1, out_partial, down_partial, gate_sum, branch_1, branch_y0 = together(
        grad_mixed, out_near_1, out_partial, down_partial, gate_sum, branch_1, branch_y0
    )
    down_sum = half_sum(down_partial).reshape(2, 2, -1, width)
    out = [out_partial[i * rows : (i + 1) * rows] for i in range(2 * hops)]
    gate_sum = gate_sum.reshape(2, hops, 2, own_rows, share)
    gate_y = swap_y(given(gate_sum, y_bit, 2))
    branch_2 = ring_on(after(branch_1, t))
    out_sum = add(out[0], out_near_1).astype(BF)
    out_z = ring_on(out_sum)
    out_near_2 = swap_core(after(out[3], t))
    grad_raw = attend_back(query, key, value, mixed, t, logs, cosine, sine, heads, ctx)
    grad_raw = grad_raw.reshape(-1, length)
    first_partial = dot(grad_raw, w_qkv[:, : 3 * part], 0, 1).astype(BF)

    t, out_near_2, grad_raw, branch_2, gate_y = together(first_partial, out_near_2, grad_raw, branch_2, gate_y)
    first_blocks = t.reshape(ctx, rows, width)
    first_own = lambda hop: pick(first_blocks, block_of(hop))
    first_other = lambda hop: pick(first_blocks, block_of(hop) ^ 1)
    y = swap_y(first_other(1))
    out_near_3 = swap_core(after(out[5], t))
    head_partial = dot(after(first_all, t), grad_raw, 0, 1).astype(BF).reshape(2, 2, ctx * own_rows, -1)
    head_near = swap_core(given(head_partial, core, 1))

    t, out_near_3, head_partial, head_near, out_z = together(y, out_near_3, head_partial, head_near, out_z)
    total = add(first_own(1), t).astype(BF)
    z, y = ring_on(total), swap_y(after(first_other(2), t))
    out_sum = add(out[2], out_near_2, out_z).astype(BF)
    head_sum = kept(head_partial, core, 1, head_near)
    head_given = given(head_sum, x_bit, 0)
    gate_sum = kept(gate_sum, y_bit, 2, gate_y)
    products = first_partial.astype(F32) * after(first_all, t).astype(F32)
    gain_attn_term = jnp.sum(products, axis=0) / gain_one

    t, y, out_sum, head_sum, head_given, gate_sum, gain_attn_term = together(
        z, y, out_sum, head_sum, head_given, gate_sum, gain_attn_term
    )
    total = add(first_own(2), y, t).astype(BF)
    z, y = ring_on(total), swap_y(after(first_other(3), t))
    out_near_0 = swap_core(after(out[7], t))

    gain_terms = jnp.stack([gain_attn_term, gain_mlp_term]).reshape(2, fsdp * ctx, own_rows).transpose(1, 0, 2)
    gain_terms = lax.all_to_all(after(gain_terms, t), ("x", "core") + sequence, 0, 0, tiled=True)

    t, y, out_near_0, up_sum, gain_terms = together(z, y, out_near_0, up_sum, gain_terms)
    total = add(first_own(3), y, t).astype(BF)
    z, y = ring_on(total), swap_y(after(first_other(0), t))
    head_x = swap_x(after(head_given, t))
    up_sum = up_sum.reshape(2, hops, 2, own_rows, share)
    up_given = given(up_sum, y_bit, 2)

    def deal_rows(summed):
        received = lax.all_to_all(summed.reshape(2 * hops, own_rows, -1), ("core", "z"), 0, 0, tiled=True)
        return received.reshape(2, hops, own_rows, -1)

    t, y, up_given = together(z, y, up_given)
    up_y = swap_y(up_given)
    gate_dealt = deal_rows(after(gate_sum, t))
    branch_3, branch_y1, branch_y2 = ring_on(after(branch_2, t)), swap_y(after(branch_1, t)), swap_y(after(branch_2, t))
    out_z = ring_on(after(out_sum, t))
    grad_first = add(first_own(0), y, t)
    inputs_normed, scale_attn = norm_parts(inputs)
    input_grad = (grad_middle + norm_back(grad_first * gain_one, inputs_normed, scale_attn)).astype(BF)
    down_given = given(down_sum, y_bit, 1)

    t, branch_3, out_z, input_grad, down_given = together(up_y, branch_3, out_z, input_grad, down_given)
    branch_y3 = swap_y(branch_3)
    up_both = kept(up_sum, y_bit, 2, t)
    out_z = ring_on(add(out[4], out_near_3, out_z).astype(BF))

    t, branch_y1, branch_y2, branch_y3, head_x, gate_dealt, up_both = together(
        out_z, branch_y1, branch_y2, branch_y3, head_x, gate_dealt, up_both
    )
    up_dealt = deal_rows(up_both)
    down_y = swap_y(after(down_given, t))
    gate_grad, up_grad = hidden_columns(gate_dealt, fsdp), hidden_columns(up_dealt, fsdp)
    branches = ((grad_branch, branch_y0), (branch_1, branch_y1), (branch_2, branch_y2), (branch_3, branch_y3))
    branch_all = jnp.concatenate([item for pair in branches for item in pair], axis=0)
    mixed_rows = jnp.concatenate([pick(mixed, block_of(hop) ^ i) for hop in range(hops) for i in range(2)], axis=1)
    out_weight = dot(mixed_rows, branch_all, 1, 0).astype(BF).reshape(2, 2, own_rows, width)
    weight = kept(out_weight, core, 1, swap_core(given(out_weight, core, 1)))
    weight_x = swap_x(given(weight, x_bit, 0))
    output = (middle + add(out[6], out_near_0, t)).astype(BF)
    head_rows = lax.all_to_all(after(kept(head_sum, x_bit, 0, head_x), up_dealt), sequence, 0, 0, tiled=True)

    weight = kept(weight, x_bit, 0, weight_x)
    pairs = [(i * ctx + j, j * fsdp + i) for i in range(fsdp) for j in range(ctx)]
    out_grad = lax.ppermute(weight, ("x", "core") + sequence, pairs).astype(F32)
    down_sum = kept(down_sum, y_bit, 1, down_y)
    down_near = swap_core(pick(down_sum, 1 - core))
    down_grad = halves(pick(down_sum, core), down_near, core).reshape(-1, width).astype(F32)
    query_grad, key_grad, value_grad = head_columns(head_rows.reshape(ctx, own_rows, -1))

    gain_grads = jnp.sum(gain_terms, axis=0)
    return (
        output,
        input_grad,
        gain_grads[0],
        query_grad,
        key_grad,
        value_grad,
        out_grad,
        gain_grads[1],
        gate_grad,
        up_grad,
        down_grad,
    )


def solution(mesh):
    fsdp, ctx = ("fsdp",), ("ctx",)
    body = general_body
    if mesh.devices.shape == (4, 8):
        body, fsdp, ctx = paired_body, ("x", "core"), ("z", "y")
        mesh = jax.sharding.Mesh(mesh.devices.reshape(2, 2, 4, 2), fsdp + ctx)
    rows, matrix = P(fsdp + ctx, None), P(fsdp, None)
    in_specs = (rows, P(fsdp), matrix, matrix, matrix, matrix, P(fsdp), matrix, matrix, matrix, rows)
    out_specs = (rows, rows, P(fsdp + ctx), rows, rows, rows, rows, P(fsdp + ctx), rows, rows, rows)
    return jax.shard_map(body, mesh=mesh, in_specs=in_specs, out_specs=out_specs, check_vma=False)
```

```python
import functools

import jax
import jax.numpy as jnp
import numpy as np
from jax import lax
from jax.experimental import pallas as pl
from jax.experimental.pallas import tpu as pltpu
from jax.sharding import PartitionSpec as P

HEADS = 32
EPS = 1e-05
THETA = 130000.0
MASKED = -1e30
BF = jnp.bfloat16
F32 = jnp.float32


def dot(left, right, left_axis, right_axis):
    return lax.dot_general(
        left, right, (((left_axis,), (right_axis,)), ((), ())), preferred_element_type=F32
    )


def norm_parts(matrix):
    scale = lax.rsqrt(jnp.mean(matrix * matrix, axis=-1, keepdims=True) + EPS)
    return (matrix * scale, scale)


def norm_back(grad_scaled, normed, scale):
    return scale * (grad_scaled - normed * jnp.mean(grad_scaled * normed, axis=-1, keepdims=True))


def angle_tables(length, head_width):
    half = head_width // 2
    freqs = np.float32(THETA) ** (-(np.arange(half, dtype=np.float32) * np.float32(2.0 / head_width)))
    angles = freqs[:, None].astype(np.float32) * np.arange(length, dtype=np.float32)[None, :]
    return jnp.asarray(np.cos(angles), F32), jnp.asarray(np.sin(angles), F32)


def low_lanes(block):
    return lax.broadcasted_iota(jnp.int32, block.shape, 1) < block.shape[1] // 2


def sort_columns(matrix, blocks):
    size = matrix.shape[1] // blocks
    early, late = [], []
    for j in range(blocks // 2):
        first = matrix[:, 2 * j * size : (2 * j + 1) * size]
        second = pltpu.roll(matrix[:, (2 * j + 1) * size : (2 * j + 2) * size], size // 2, 1)
        low = low_lanes(first)
        early.append(jnp.where(low, first, second))
        late.append(jnp.where(low, second, first))
    return jnp.concatenate(early + late[::-1], axis=1)


def deal_columns(matrix, blocks):
    size = matrix.shape[1] // blocks
    out = []
    for j in range(blocks // 2):
        early = matrix[:, j * size : (j + 1) * size]
        late = matrix[:, (blocks - 1 - j) * size : (blocks - j) * size]
        low = low_lanes(early)
        out.append(jnp.where(low, early, late))
        out.append(pltpu.roll(jnp.where(low, late, early), size // 2, 1))
    return jnp.concatenate(out, axis=1)


def turn(matrix, cosine, sine):
    half = matrix.shape[0] // 2
    first, second = matrix[:half], matrix[half:]
    return jnp.concatenate([first * cosine - second * sine, second * cosine + first * sine], axis=0)


def by_blocks(ref):
    return jnp.concatenate([ref[block].astype(F32) for block in range(ref.shape[0])], axis=1)


def masked_block(scores, chunk):
    keys = scores.shape[0]
    places = lax.broadcasted_iota(jnp.int32, (chunk, chunk), 0)
    wants = lax.broadcasted_iota(jnp.int32, (chunk, chunk), 1)
    last = jnp.where(places <= wants, scores[keys - chunk :], MASKED)
    if keys == chunk:
        return last
    return jnp.concatenate([scores[: keys - chunk], last], axis=0)


def attend_kernel(blocks, chunk, q_ref, k_ref, v_ref, cos_ref, sin_ref, o_ref, qs_ref, ks_ref, vs_ref, lse_ref):
    width, length = q_ref.shape
    cosine, sine = cos_ref[...], sin_ref[...]
    query = turn(sort_columns(q_ref[...], blocks), cosine, sine).astype(BF)
    key = turn(sort_columns(k_ref[...], blocks), cosine, sine).astype(BF)
    value = sort_columns(v_ref[...], blocks).astype(BF)
    scaled = query * jnp.asarray(width ** (-0.5), BF)
    qs_ref[...] = scaled
    ks_ref[...] = key
    vs_ref[...] = value
    mixed, logs = [], []
    for i in range(length // chunk):
        count = (i + 1) * chunk
        scores = dot(key[:, :count], scaled[:, i * chunk : count], 0, 0)
        scores = masked_block(scores, chunk)
        top = jnp.max(scores, axis=0, keepdims=True)
        raised = jnp.exp(scores - top)
        total = jnp.sum(raised, axis=0, keepdims=True)
        mixed.append(dot(value[:, :count], raised.astype(BF), 1, 0) / total)
        logs.append(top + jnp.log(total))
    size = length // blocks
    dealt = deal_columns(jnp.concatenate(mixed, axis=1), blocks).astype(BF)
    for block in range(blocks):
        o_ref[block] = dealt[:, block * size : (block + 1) * size]
    lse_ref[0] = jnp.concatenate(logs, axis=1)


def attend_back_kernel(blocks, chunk, q_ref, k_ref, v_ref, o_ref, do_ref, lse_ref, cos_ref, sin_ref, d_ref, dk_ref, dv_ref):
    width, length = q_ref.shape
    factor = width ** (-0.5)
    cosine, sine = cos_ref[...], -sin_ref[...]
    scaled, key, value = q_ref[...], k_ref[...], v_ref[...]
    grad_f32 = sort_columns(by_blocks(do_ref), blocks)
    center = jnp.sum(grad_f32 * sort_columns(by_blocks(o_ref), blocks), axis=0, keepdims=True)
    grad = grad_f32.astype(BF)
    logs = lse_ref[0]
    dq = []
    for i in reversed(range(length // chunk)):
        count = (i + 1) * chunk
        here = slice(i * chunk, count)
        scores = masked_block(dot(key[:, :count], scaled[:, here], 0, 0), chunk)
        shares = jnp.exp(scores - logs[:, here])
        grad_shares = dot(value[:, :count], grad[:, here], 0, 0)
        grad_scores = (shares * (grad_shares - center[:, here])).astype(BF)
        dq.append(dot(key[:, :count], grad_scores, 1, 0))
        dk_part = dot(scaled[:, here], grad_scores, 1, 1)
        dv_part = dot(grad[:, here], shares.astype(BF), 1, 1)
        if count == length:
            dk_ref[...] = dk_part
            dv_ref[...] = dv_part
        else:
            dk_ref[:, :count] += dk_part
            dv_ref[:, :count] += dv_part
    dq = turn(jnp.concatenate(dq[::-1], axis=1) * factor, cosine, sine)
    d_ref[0] = deal_columns(dq, blocks).astype(BF)
    d_ref[1] = deal_columns(turn(dk_ref[...], cosine, sine), blocks).astype(BF)
    d_ref[2] = deal_columns(dv_ref[...], blocks).astype(BF)


def attend(raw, cosine, sine, heads, blocks):
    width, length = 2 * cosine.shape[0], raw.shape[1]
    chunk = min(256, length)
    head = lambda shift: pl.BlockSpec((width, length), lambda h: (h + shift * heads, 0))
    table = pl.BlockSpec((width // 2, length), lambda h: (0, 0))
    flat = jax.ShapeDtypeStruct((heads * width, length), BF)
    return pl.pallas_call(
        functools.partial(attend_kernel, blocks, chunk),
        grid=(heads,),
        in_specs=[head(0), head(1), head(2), table, table],
        out_specs=[
            pl.BlockSpec((blocks, width, length // blocks), lambda h: (0, h, 0)),
            head(0),
            head(0),
            head(0),
            pl.BlockSpec((1, 1, length), lambda h: (h, 0, 0)),
        ],
        out_shape=[
            jax.ShapeDtypeStruct((blocks, heads * width, length // blocks), BF),
            flat,
            flat,
            flat, jax.ShapeDtypeStruct((heads, 1, length), F32),
        ],
        compiler_params=pltpu.CompilerParams(vmem_limit_bytes=40 * 1024 * 1024),
        name="attend",
    )(raw, raw, raw, cosine, sine)


def attend_back(query, key, value, mixed, grad, logs, cosine, sine, heads, blocks):
    width, length = query.shape[0] // heads, query.shape[1]
    chunk = min(256, length)
    head = pl.BlockSpec((width, length), lambda h: (h, 0))
    block = pl.BlockSpec((blocks, width, length // blocks), lambda h: (0, h, 0))
    table = pl.BlockSpec((width // 2, length), lambda h: (0, 0))
    return pl.pallas_call(
        functools.partial(attend_back_kernel, blocks, chunk),
        grid=(heads,),
        in_specs=[head, head, head, block, block, pl.BlockSpec((1, 1, length), lambda h: (h, 0, 0)), table, table],
        out_specs=pl.BlockSpec((3, width, length), lambda h: (0, h, 0)),
        out_shape=jax.ShapeDtypeStruct((3, heads * width, length), BF),
        scratch_shapes=[pltpu.VMEM((width, length), F32), pltpu.VMEM((width, length), F32)],
        compiler_params=pltpu.CompilerParams(vmem_limit_bytes=40 * 1024 * 1024),
        name="attend_back",
    )(query, key, value, mixed, grad, logs, cosine, sine)


def swap(item, axis, bit):
    pairs = [(i, i ^ bit) for i in range(lax.axis_size(axis))]
    return lax.ppermute(item, axis, pairs)


def step_on(item):
    count = lax.axis_size("ctx")
    return lax.ppermute(item, "ctx", [(i, (i + 2) % count) for i in range(count)])


def after(item, *others):
    return lax.optimization_barrier((item,) + others)[0]


def gather_rows(piece):
    count, place = lax.axis_size("ctx"), lax.axis_index("ctx")
    rows = jnp.zeros((count,) + piece.shape, piece.dtype)
    for hop in range(count // 2):
        if hop:
            piece = step_on(piece)
        source = lax.rem(place + count - 2 * hop, count)
        rows = lax.dynamic_update_slice(rows, piece[None], (source, 0, 0))
        rows = lax.dynamic_update_slice(rows, swap(piece, "ctx", 1)[None], (source ^ 1, 0, 0))
    return rows.reshape(-1, rows.shape[2])


def scatter_rows(partial):
    count, place = lax.axis_size("ctx"), lax.axis_index("ctx")
    blocks = partial.astype(BF).reshape(count, -1, partial.shape[1])
    total = None
    for hop in range(1, count // 2 + 1):
        target = lax.rem(place + count - 2 * hop, count)
        mine = lax.dynamic_index_in_dim(blocks, target, 0, keepdims=False)
        other = lax.dynamic_index_in_dim(blocks, target ^ 1, 0, keepdims=False)
        term = mine.astype(F32) + swap(other, "ctx", 1).astype(F32)
        total = term if total is None else term + total.astype(F32)
        if hop < count // 2:
            total = step_on(total.astype(BF))
    return total


def gather_weight(piece):
    if lax.axis_size("fsdp") != 4:
        return lax.all_gather(piece, "fsdp", axis=0, tiled=True)
    place = lax.axis_index("fsdp")
    rows = jnp.zeros((4,) + piece.shape, piece.dtype)
    far = swap(piece, "fsdp", 2)
    for source, item in (
        (place, piece),
        (place ^ 1, swap(piece, "fsdp", 1)),
        (place ^ 2, far),
        (place ^ 3, swap(far, "fsdp", 1)),
    ):
        rows = lax.dynamic_update_slice(rows, item[None], (source, 0, 0))
    return rows.reshape(-1, piece.shape[1])


def scatter(partial, axis):
    return lax.psum_scatter(partial.astype(BF), axis, scatter_dimension=0, tiled=True)


def general_body(
    tokens, gain_attn, w_query, w_key, w_value, w_out, gain_mlp, w_gate, w_up, w_down, cotangent
):
    width = tokens.shape[1]
    hidden_width = w_gate.shape[1]
    fsdp, ctx = lax.axis_size("fsdp"), lax.axis_size("ctx")
    place = lax.axis_index("ctx")
    length = tokens.shape[0] * ctx
    heads = HEADS // ctx
    part = width // ctx
    share = hidden_width // ctx
    own_rows = width // (fsdp * ctx)
    cosine, sine = angle_tables(length, width // HEADS)

    def head_columns(weight):
        return lax.dynamic_slice_in_dim(weight, place * part, part, 1)

    def hidden_columns(weight):
        rows = weight.shape[0]
        blocks = weight.reshape(rows, fsdp, ctx, share // fsdp)
        return lax.dynamic_index_in_dim(blocks, place, 2, keepdims=False).reshape(rows, share)

    def to_owners(partial):
        summed = scatter(partial, "fsdp")
        return lax.all_to_all(summed, "ctx", 0, 0, tiled=True).reshape(ctx, own_rows, -1).astype(F32)

    def of_heads(received):
        return received.transpose(1, 0, 2).reshape(own_rows, -1)

    def of_hidden(received):
        blocks = received.reshape(ctx, own_rows, fsdp, -1)
        return blocks.transpose(1, 2, 0, 3).reshape(own_rows, -1)

    def normed_rows(rows):
        return norm_parts(rows.astype(F32))[0]

    w_qkv_piece = jnp.concatenate([head_columns(item) for item in (w_query, w_key, w_value)], axis=1)
    w_qkv = gather_weight(w_qkv_piece)
    gains = lax.all_gather(jnp.stack([gain_attn, gain_mlp]), "fsdp", axis=1, tiled=True).astype(F32)
    gain_one, gain_two = gains[0], gains[1]
    tokens_all = gather_rows(tokens)
    first_all = (normed_rows(tokens_all) * gain_one).astype(BF)
    raw = dot(w_qkv, first_all, 0, 1)
    mixed, query, key, value, logs = attend(raw, cosine, sine, heads, ctx)
    w_out_all = gather_weight(after(w_out, w_qkv))
    w_gate_up = gather_weight(
        after(jnp.concatenate([hidden_columns(w_gate), hidden_columns(w_up)], axis=1), w_out_all)
    )
    down_size = w_down.shape[0] // ctx
    down_share = gather_weight(
        after(lax.dynamic_slice_in_dim(w_down, place * down_size, down_size, 0), w_gate_up)
    )
    cotangent_all = gather_rows(after(cotangent, tokens_all))

    inputs = tokens.astype(F32)
    mixed_own = lax.all_to_all(mixed, "ctx", 0, 0, tiled=True).reshape(width, -1)
    middle = inputs + dot(mixed_own, w_out_all, 0, 0)
    normed_mid, scale_mid = norm_parts(middle)
    second_all = gather_rows((normed_mid * gain_two).astype(BF))
    gate_up = dot(second_all, w_gate_up, 1, 0)
    gate, upward = gate_up[:, :share], gate_up[:, share:]
    grad_hidden = dot(cotangent_all, down_share, 1, 1)
    sigmoid = jax.nn.sigmoid(gate)
    hidden = (gate * sigmoid * upward).astype(BF)
    grad_gate = (grad_hidden * upward * (sigmoid + gate * sigmoid * (1.0 - sigmoid))).astype(BF)
    grad_up = (grad_hidden * (gate * sigmoid)).astype(BF)
    grad_gate_up = jnp.concatenate([grad_gate, grad_up], axis=1)
    grad_second = scatter_rows(dot(grad_gate_up, w_gate_up, 1, 1))
    output = (middle + scatter_rows(after(dot(hidden, down_share, 1, 0), grad_second))).astype(BF)

    gain_mlp_term = jnp.sum(grad_second * normed_mid, axis=0)
    grad_middle = cotangent.astype(F32) + norm_back(grad_second * gain_two, normed_mid, scale_mid)
    grad_branch = grad_middle.astype(BF)
    grad_mixed_own = dot(w_out_all, grad_branch, 1, 1).astype(BF)
    grad_mixed = lax.all_to_all(grad_mixed_own.reshape(ctx, part, -1), "ctx", 0, 0, tiled=True)
    grad_raw = attend_back(query, key, value, mixed, grad_mixed, logs, cosine, sine, heads, ctx)
    grad_raw = grad_raw.reshape(-1, length)
    branch_all = gather_rows(after(grad_branch, grad_mixed))
    first_partial = dot(grad_raw, w_qkv, 0, 1)
    grad_first = scatter_rows(first_partial)
    inputs_normed, scale_attn = norm_parts(inputs)
    gain_attn_term = jnp.sum(grad_first * inputs_normed, axis=0)
    input_grad = (grad_middle + norm_back(grad_first * gain_one, inputs_normed, scale_attn)).astype(BF)

    down_grad = scatter(dot(hidden, cotangent_all, 0, 0), "fsdp").astype(F32)
    mixed_rows = mixed.transpose(1, 0, 2).reshape(part, length)
    out_grad = scatter(dot(mixed_rows, branch_all, 1, 0), "fsdp")
    out_grad = lax.ppermute(
        out_grad,
        ("fsdp", "ctx"),
        [(i * ctx + j, j * fsdp + i) for i in range(fsdp) for j in range(ctx)],
    ).astype(F32)
    gate_up_rows = to_owners(dot(second_all, grad_gate_up, 0, 0))
    qkv_rows = to_owners(dot(first_all, grad_raw, 0, 1))
    gain_terms = jnp.stack([gain_attn_term, gain_mlp_term]).reshape(2, fsdp * ctx, own_rows)
    gain_grads = jnp.sum(
        lax.all_to_all(gain_terms.transpose(1, 0, 2), ("fsdp", "ctx"), 0, 0, tiled=True), axis=0
    )
    return (
        output,
        input_grad,
        gain_grads[0],
        of_heads(qkv_rows[:, :, :part]),
        of_heads(qkv_rows[:, :, part : 2 * part]),
        of_heads(qkv_rows[:, :, 2 * part :]),
        out_grad,
        gain_grads[1],
        of_hidden(gate_up_rows[:, :, :share]),
        of_hidden(gate_up_rows[:, :, share:]),
        down_grad,
    )


def together(*items):
    return lax.optimization_barrier(items)


def pick(blocks, index, axis=0):
    return lax.dynamic_index_in_dim(blocks, index, axis, keepdims=False)


def put(blocks, item, index):
    return lax.dynamic_update_slice(blocks, item[None], (index,) + (0,) * item.ndim)


def halves(own, other, index):
    return put(put(jnp.zeros((2,) + own.shape, own.dtype), own, index), other, 1 - index)


def add(*items):
    return sum(item.astype(F32) for item in items)


def swap_pair(item, axis):
    return lax.ppermute(item, axis, [(0, 1), (1, 0)])


def swap_x(item):
    return swap_pair(item, "x")


def swap_core(item):
    return swap_pair(item, "core")


def swap_y(item):
    return swap_pair(item, "y")


def ring_on(item, steps=1):
    count = lax.axis_size("z")
    return lax.ppermute(item, "z", [(i, (i + steps) % count) for i in range(count)])


def columns_kernel(place_ref, gate_ref, up_ref, own_ref, other_ref, halves_ref):
    step, steps = pl.program_id(0), pl.num_programs(0)
    size, half = own_ref.shape[1] // 2, halves_ref.shape[0] // 2
    rows = pl.ds(pl.multiple_of(place_ref[2] * half, half), half)

    def take(weight_ref):
        for block in range(2):
            own = pl.ds(pl.multiple_of((2 * block + place_ref[1]) * size, size), size)
            other = pl.ds(pl.multiple_of((2 * block + 1 - place_ref[1]) * size, size), size)
            into = slice(block * size, (block + 1) * size)
            own_ref[:, into] = weight_ref[:, own]
            other_ref[:, into] = weight_ref[:, other]
            halves_ref[:half, into] = weight_ref[rows, own]
            halves_ref[half:, into] = weight_ref[rows, other]

    @pl.when(step < steps // 2)
    def _():
        take(gate_ref)

    @pl.when(step >= steps // 2)
    def _():
        take(up_ref)


def shared_columns(w_gate, w_up, place, blocks, rings):
    rows, columns = w_gate.shape
    size = columns // (blocks * rings * 2)
    gate = pl.BlockSpec((rows, 2 * size), lambda s, at: (0, jnp.minimum(s, blocks - 1) * rings + at[0]))
    up = pl.BlockSpec((rows, 2 * size), lambda s, at: (0, jnp.maximum(s - blocks, 0) * rings + at[0]))
    wide = 2 * blocks * size
    return pl.pallas_call(
        columns_kernel,
        grid_spec=pltpu.PrefetchScalarGridSpec(
            num_scalar_prefetch=1,
            grid=(2 * blocks,),
            in_specs=[gate, up],
            out_specs=[pl.BlockSpec((rows, size), lambda s, at: (0, s))] * 3,
        ),
        out_shape=[jax.ShapeDtypeStruct((rows, wide), BF)] * 3,
        compiler_params=pltpu.CompilerParams(vmem_limit_bytes=56 * 1024 * 1024),
        name="columns",
    )(place, w_gate, w_up)


def mlp_middle(second, cotangent, w_gate_up, down_share):
    share = down_share.shape[0]
    gate_up = dot(second, w_gate_up, 1, 0)
    gate, upward = gate_up[:, :share], gate_up[:, share:]
    grad_hidden = dot(cotangent, down_share, 1, 1)
    sigmoid = jax.nn.sigmoid(gate)
    hidden = (gate * sigmoid * upward).astype(BF)
    grad_gate = (grad_hidden * upward * (sigmoid + gate * sigmoid * (1.0 - sigmoid))).astype(BF)
    grad_up = (grad_hidden * (gate * sigmoid)).astype(BF)
    return hidden, grad_gate, grad_up


def hidden_columns_kernel(in_ref, out_ref):
    cores, rings, _, wide = in_ref.shape
    size = wide // 2
    for ring in range(rings):
        for half in range(2):
            for core in range(cores):
                start = ((ring * 2 + half) * cores + core) * size
                out_ref[:, start : start + size] = in_ref[core, ring, :, half * size : (half + 1) * size].astype(F32)


def hidden_columns(received, blocks):
    cores, rings, rows, share = received.shape
    wide = share // blocks
    return pl.pallas_call(
        hidden_columns_kernel,
        grid=(blocks,),
        in_specs=[pl.BlockSpec((cores, rings, rows, wide), lambda s: (0, 0, 0, s))],
        out_specs=pl.BlockSpec((rows, cores * rings * wide), lambda s: (0, s)),
        out_shape=jax.ShapeDtypeStruct((rows, cores * rings * share), F32),
        compiler_params=pltpu.CompilerParams(vmem_limit_bytes=56 * 1024 * 1024),
        name="hidden_columns",
    )(received)


def head_columns_kernel(in_ref, *out_refs):
    count = in_ref.shape[0]
    part = in_ref.shape[2] // len(out_refs)
    for i, out_ref in enumerate(out_refs):
        for block in range(count):
            out_ref[:, block * part : (block + 1) * part] = in_ref[block, :, i * part : (i + 1) * part].astype(F32)


def head_columns(received):
    count, rows, wide = received.shape
    return pl.pallas_call(
        head_columns_kernel,
        out_shape=[jax.ShapeDtypeStruct((rows, count * wide // 3), F32)] * 3,
        compiler_params=pltpu.CompilerParams(vmem_limit_bytes=56 * 1024 * 1024),
        name="head_columns",
    )(received)


def paired_body(
    tokens, gain_attn, w_query, w_key, w_value, w_out, gain_mlp, w_gate, w_up, w_down, cotangent
):
    rows, width = tokens.shape
    hops = lax.axis_size("z")
    fsdp, ctx = 2 * lax.axis_size("x"), 2 * hops
    x_bit, core, ring, y_bit = [lax.axis_index(axis) for axis in ("x", "core", "z", "y")]
    place, fsdp_place = 2 * ring + y_bit, 2 * x_bit + core
    length = rows * ctx
    heads = HEADS // ctx
    part = width // ctx
    share = w_gate.shape[1] // ctx
    own_rows = width // (fsdp * ctx)
    sequence = ("z", "y")
    cosine, sine = angle_tables(length, width // HEADS)

    def block_of(hop):
        return 2 * lax.rem(ring + hops - hop, hops) + y_bit

    def blank(shape, *wait):
        return jnp.broadcast_to(together(jnp.zeros((), BF), *wait)[0], shape)

    def place_rows(buffer, item, index):
        return put(buffer, item, fsdp_place ^ index)

    def half_at(index, half):
        return 2 * (fsdp_place ^ index) + half

    def put_whole(buffer, item, index):
        return lax.dynamic_update_slice(buffer, item.reshape((2,) + buffer.shape[1:]), (half_at(index, 0), 0, 0))

    piece = jnp.concatenate(
        [lax.dynamic_slice_in_dim(item, place * part, part, 1) for item in (w_query, w_key, w_value)]
        + [jnp.pad(jnp.stack([gain_attn, gain_mlp], axis=1), ((0, 0), (0, 126)))],
        axis=1,
    )
    w_qkv = lax.all_gather(piece, ("x", "core"), axis=0, tiled=True)
    z, y = ring_on(tokens), swap_y(tokens)

    t, y = together(z, y)
    hop_1, y_0 = t, y
    z, y = ring_on(hop_1), swap_y(hop_1)
    out_near = lax.all_gather(after(w_out, t), "core", axis=0, tiled=True)
    out_half = lax.dynamic_slice_in_dim(after(w_out, t), y_bit * (width // 8), width // 8, 0)
    size = w_down.shape[0] // ctx
    down_both = lax.dynamic_slice_in_dim(after(w_down, t), 2 * ring * size, 2 * size, 0)
    own, other, to_send = shared_columns(
        after(w_gate, t), w_up, jnp.stack([ring, core, y_bit]).astype(jnp.int32), fsdp, hops
    )
    half_rows = width // 8

    t, y, to_send, down_both, out_half = together(z, y, to_send, down_both, out_half)
    hop_2, y_1 = t, y
    z, y = ring_on(hop_2), swap_y(hop_2)
    out_straight = swap_x(out_half)
    first_all = blank((ctx,) + tokens.shape, t)

    t, y, first_all, w_qkv = together(z, y, first_all, w_qkv)
    hop_3, y_2 = t, y
    y = swap_y(hop_3)
    cot_1 = ring_on(after(cotangent, t))
    gains_all = w_qkv[:, 3 * part :].astype(F32).T
    gain_one, gain_two = gains_all[0], gains_all[1]

    def take_rows(buffer, item, hop, mate):
        normed = (norm_parts(item.astype(F32))[0] * gain_one).astype(BF)
        return put(buffer, normed, block_of(hop) ^ mate)

    for item, hop, mate in ((tokens, 0, 0), (y_0, 0, 1), (hop_1, 1, 0), (y_1, 1, 1), (hop_2, 2, 0), (y_2, 2, 1)):
        first_all = take_rows(first_all, item, hop, mate)
    first_all = take_rows(first_all, hop_3, 3, 0)

    t, cot_1, first_all, out_straight = together(y, cot_1, first_all, out_straight)
    cot_2 = ring_on(cot_1)
    out_far = lax.all_gather(out_straight, ("core", "y"), axis=0, tiled=True)
    arriving_own = swap_x(after(to_send[:half_rows], t))
    first_all = take_rows(first_all, t, 3, 1).reshape(length, width)
    raw = dot(w_qkv, first_all, 0, 1)
    mixed, query, key, value, logs = attend(raw, cosine, sine, heads, ctx)

    t, cot_2, down_both, arriving_own = together(mixed, cot_2, down_both, arriving_own)
    arriving_other = swap_x(after(to_send[half_rows:], t))
    down_both = lax.all_gather(down_both.reshape(1, 2, 2, size // 2, width), "x", axis=0, tiled=True)
    mixed_own = lax.all_to_all(t, sequence, 0, 0, tiled=True)
    gate_up_near = swap_core(after(other, t))
    cot_near, cot_near_1, cot_near_2 = [swap_core(after(item, t)) for item in (cotangent, cot_1, cot_2)]
    w_gate_up = put_whole(blank((8, half_rows, own.shape[1]), t), own, 0)

    t, gate_up_near, cot_near, cot_near_1, cot_near_2, w_gate_up, out_near, out_far = together(
        mixed_own, gate_up_near, cot_near, cot_near_1, cot_near_2, w_gate_up, out_near, out_far
    )
    crossing_own = swap_y(after(arriving_own, t))
    cot_3 = ring_on(after(cot_2, t))
    mixed_own = t.reshape(width, rows)
    inputs = tokens.astype(F32)
    mixed_halves = mixed_own.reshape(2, width // 2, rows)
    middle = inputs + dot(pick(mixed_halves, x_bit), out_near, 0, 0) + dot(pick(mixed_halves, 1 - x_bit), out_far, 0, 0)
    normed_mid, scale_mid = norm_parts(middle)
    second = (normed_mid * gain_two).astype(BF)

    t, cot_3, w_gate_up, gate_up_near, arriving_other = together(
        second, cot_3, w_gate_up, gate_up_near, arriving_other
    )
    z, near_0 = ring_on(t), swap_core(t)
    last_straight = swap_core(after(arriving_other, t))
    cot_near_3 = swap_core(after(cot_3, t))
    w_gate_up = put_whole(w_gate_up, gate_up_near, 1)
    w_gate_up = put(w_gate_up, arriving_own, half_at(2, y_bit))

    t, near_0, cot_near_3, w_gate_up, crossing_own, last_straight = together(
        z, near_0, cot_near_3, w_gate_up, crossing_own, last_straight
    )
    hop_1 = t
    z, near_1 = ring_on(t), swap_core(t)
    crossing_other = swap_y(after(arriving_other, t))
    w_gate_up = put(w_gate_up, crossing_own, half_at(2, 1 - y_bit))
    w_gate_up = put(w_gate_up, last_straight, half_at(3, y_bit))
    down_share = blank((2, 2, 2, size // 2, width), t)

    t, near_1, w_gate_up, down_share = together(z, near_1, w_gate_up, down_share)
    hop_2 = t
    z, near_2 = ring_on(t), swap_core(t)
    cot_all = jnp.concatenate(
        [cot_1, cot_near_1, cot_2, cot_near_2, cot_3, cot_near_3, cotangent, cot_near], axis=0
    )

    t, near_2, crossing_other, cot_all, w_gate_up, down_both = together(
        z, near_2, crossing_other, cot_all, w_gate_up, down_both
    )
    down_near = swap_core(pick(down_both, 1 - core, 2))
    down_at = lambda blocks, item, i: lax.dynamic_update_slice(blocks, item[:, None], (0, i, 0, 0, 0))
    down_share = down_at(down_share, pick(down_both, core, 2), core)
    near_3 = swap_core(t)
    last_crossed = swap_core(crossing_other)
    second_all = jnp.concatenate([hop_1, near_1, hop_2, near_2, t, near_3, second, near_0], axis=0)
    w_gate_up = put(w_gate_up, last_crossed, half_at(3, 1 - y_bit)).reshape(width, -1)
    down_share = down_at(down_share, down_near, 1 - core).reshape(-1, width)

    def given(blocks, bit, dim):
        return pick(blocks, 1 - bit, dim)

    def kept(blocks, bit, dim, arrived):
        return add(pick(blocks, bit, dim), arrived).astype(BF)

    def half_sum(partial):
        return lax.psum_scatter(partial.astype(BF), "x", scatter_dimension=0, tiled=True)

    buffers = [blank((length, share), t) for _ in range(3)]
    half = length // 2

    def run_middle(start, buffers, rows_in):
        items = mlp_middle(rows_in, cot_all[start : start + half], w_gate_up, down_share)
        return items, [lax.dynamic_update_slice(buffer, item, (start, 0)) for buffer, item in zip(buffers, items)]

    def run_back(items):
        back = dot(jnp.concatenate(items[1:], axis=1), w_gate_up, 1, 1).astype(BF)
        return [back[i * rows : (i + 1) * rows] for i in range(4)]

    items, buffers = run_middle(0, buffers, second_all[:half])
    own_1, other_1, own_2, other_2 = run_back(items)
    near_1, near_2 = swap_core(other_1), swap_core(other_2)
    t = add(own_1, near_1).astype(BF)
    z = ring_on(t)
    items, buffers = run_middle(half, buffers, after(second_all[half:], t))
    z, near_2, *items = together(z, near_2, *items)
    t = add(own_2, near_2, z).astype(BF)
    z = ring_on(t)
    items[0] = after(items[0], t)
    items[1] = after(items[1], t)
    own_3, other_3, own_0, other_0 = run_back(items)
    near_3, near_0 = swap_core(other_3), swap_core(other_0)
    gate_partial = dot(after(second_all, t), buffers[1], 0, 0).astype(BF)
    z, near_3, near_0, gate_partial, hidden, grad_up = together(
        z, near_3, near_0, gate_partial, buffers[0], buffers[2]
    )
    gate_sum = half_sum(gate_partial)

    t = add(own_3, near_3, z).astype(BF)
    z = ring_on(t)
    up_partial = dot(after(second_all, t), grad_up, 0, 0).astype(BF)
    t, up_partial = together(z, up_partial)
    up_sum = half_sum(up_partial)

    grad_second = add(own_0, near_0, t)
    gain_mlp_term = jnp.sum(grad_second * normed_mid, axis=0)
    grad_middle = cotangent.astype(F32) + norm_back(grad_second * gain_two, normed_mid, scale_mid)
    grad_branch = grad_middle.astype(BF)
    grad_mixed_own = halves(
        dot(out_near, grad_branch, 1, 1).astype(BF), dot(out_far, grad_branch, 1, 1).astype(BF), x_bit
    )

    t, hidden = together(grad_mixed_own, hidden)
    grad_mixed = lax.all_to_all(t.reshape(ctx, part, -1), sequence, 0, 0, tiled=True)
    branch_1, branch_y0 = ring_on(after(grad_branch, t)), swap_y(after(grad_branch, t))
    out_partial = dot(hidden, down_share, 1, 0).astype(BF)
    out_near_1 = swap_core(out_partial[rows : 2 * rows])
    down_partial = dot(hidden, after(cot_all, t), 0, 0).astype(BF)

    t, out_near_1, out_partial, down_partial, gate_sum, branch_1, branch_y0 = together(
        grad_mixed, out_near_1, out_partial, down_partial, gate_sum, branch_1, branch_y0
    )
    down_sum = half_sum(down_partial).reshape(2, 2, -1, width)
    out = [out_partial[i * rows : (i + 1) * rows] for i in range(2 * hops)]
    gate_sum = gate_sum.reshape(2, hops, 2, own_rows, share)
    gate_y = swap_y(given(gate_sum, y_bit, 2))
    branch_2 = ring_on(after(branch_1, t))
    out_sum = add(out[0], out_near_1).astype(BF)
    out_z = ring_on(out_sum)
    out_near_2 = swap_core(after(out[3], t))
    grad_raw = attend_back(query, key, value, mixed, t, logs, cosine, sine, heads, ctx)
    grad_raw = grad_raw.reshape(-1, length)
    first_partial = dot(grad_raw, w_qkv[:, : 3 * part], 0, 1).astype(BF)

    t, out_near_2, grad_raw, branch_2, gate_y = together(first_partial, out_near_2, grad_raw, branch_2, gate_y)
    first_blocks = t.reshape(ctx, rows, width)
    first_own = lambda hop: pick(first_blocks, block_of(hop))
    first_other = lambda hop: pick(first_blocks, block_of(hop) ^ 1)
    y = swap_y(first_other(1))
    out_near_3 = swap_core(after(out[5], t))
    head_partial = dot(after(first_all, t), grad_raw, 0, 1).astype(BF).reshape(2, 2, ctx * own_rows, -1)
    head_near = swap_core(given(head_partial, core, 1))

    t, out_near_3, head_partial, head_near, out_z = together(y, out_near_3, head_partial, head_near, out_z)
    total = add(first_own(1), t).astype(BF)
    z, y = ring_on(total), swap_y(after(first_other(2), t))
    out_sum = add(out[2], out_near_2, out_z).astype(BF)
    head_sum = kept(head_partial, core, 1, head_near)
    head_given = given(head_sum, x_bit, 0)
    gate_sum = kept(gate_sum, y_bit, 2, gate_y)
    products = first_partial.astype(F32) * after(first_all, t).astype(F32)
    gain_attn_term = jnp.sum(products, axis=0) / gain_one

    t, y, out_sum, head_sum, head_given, gate_sum, gain_attn_term = together(
        z, y, out_sum, head_sum, head_given, gate_sum, gain_attn_term
    )
    total = add(first_own(2), y, t).astype(BF)
    z, y = ring_on(total), swap_y(after(first_other(3), t))
    out_near_0 = swap_core(after(out[7], t))

    gain_terms = jnp.stack([gain_attn_term, gain_mlp_term]).reshape(2, fsdp * ctx, own_rows).transpose(1, 0, 2)
    gain_terms = lax.all_to_all(after(gain_terms, t), ("x", "core") + sequence, 0, 0, tiled=True)

    t, y, out_near_0, up_sum, gain_terms = together(z, y, out_near_0, up_sum, gain_terms)
    total = add(first_own(3), y, t).astype(BF)
    z, y = ring_on(total), swap_y(after(first_other(0), t))
    head_x = swap_x(after(head_given, t))
    up_sum = up_sum.reshape(2, hops, 2, own_rows, share)
    up_given = given(up_sum, y_bit, 2)

    def deal_rows(summed):
        received = lax.all_to_all(summed.reshape(2 * hops, own_rows, -1), ("core", "z"), 0, 0, tiled=True)
        return received.reshape(2, hops, own_rows, -1)

    t, y, up_given = together(z, y, up_given)
    up_y = swap_y(up_given)
    gate_dealt = deal_rows(after(gate_sum, t))
    branch_3 = ring_on(after(branch_2, t))
    out_z = ring_on(after(out_sum, t))
    grad_first = add(first_own(0), y, t)
    inputs_normed, scale_attn = norm_parts(inputs)
    input_grad = (grad_middle + norm_back(grad_first * gain_one, inputs_normed, scale_attn)).astype(BF)
    down_given = given(down_sum, y_bit, 1)

    t, branch_3, out_z, input_grad, down_given = together(up_y, branch_3, out_z, input_grad, down_given)
    branch_y1, branch_y2, branch_y3 = [swap_y(after(item, t)) for item in (branch_1, branch_2, branch_3)]
    up_both = kept(up_sum, y_bit, 2, t)
    out_z = ring_on(add(out[4], out_near_3, out_z).astype(BF))

    t, head_x, gate_dealt, up_both = together(out_z, head_x, gate_dealt, up_both)
    up_dealt = deal_rows(up_both)
    down_y = swap_y(after(down_given, t))
    gate_grad, up_grad = hidden_columns(gate_dealt, fsdp), hidden_columns(up_dealt, fsdp)
    branches = ((grad_branch, branch_y0), (branch_1, branch_y1), (branch_2, branch_y2), (branch_3, branch_y3))
    branch_all = jnp.concatenate([item for pair in branches for item in pair], axis=0)
    mixed_rows = jnp.concatenate([pick(mixed, block_of(hop) ^ i) for hop in range(hops) for i in range(2)], axis=1)
    branch_all = after(branch_all, up_dealt)
    out_weight = dot(mixed_rows, branch_all, 1, 0).astype(BF).reshape(2, 2, own_rows, width)
    weight = kept(out_weight, core, 1, swap_core(given(out_weight, core, 1)))
    weight_x = swap_x(given(weight, x_bit, 0))
    output = (middle + add(out[6], out_near_0, t)).astype(BF)
    head_rows = lax.all_to_all(after(kept(head_sum, x_bit, 0, head_x), up_dealt), sequence, 0, 0, tiled=True)

    weight = kept(weight, x_bit, 0, weight_x)
    pairs = [(i * ctx + j, j * fsdp + i) for i in range(fsdp) for j in range(ctx)]
    out_grad = lax.ppermute(weight, ("x", "core") + sequence, pairs).astype(F32)
    down_sum = kept(down_sum, y_bit, 1, down_y)
    down_near = swap_core(pick(down_sum, 1 - core))
    down_grad = halves(pick(down_sum, core), down_near, core).reshape(-1, width).astype(F32)
    query_grad, key_grad, value_grad = head_columns(head_rows.reshape(ctx, own_rows, -1))

    gain_grads = jnp.sum(gain_terms, axis=0)
    return (
        output,
        input_grad,
        gain_grads[0],
        query_grad,
        key_grad,
        value_grad,
        out_grad,
        gain_grads[1],
        gate_grad,
        up_grad,
        down_grad,
    )


def solution(mesh):
    fsdp, ctx = ("fsdp",), ("ctx",)
    body = general_body
    if mesh.devices.shape == (4, 8):
        body, fsdp, ctx = paired_body, ("x", "core"), ("z", "y")
        mesh = jax.sharding.Mesh(mesh.devices.reshape(2, 2, 4, 2), fsdp + ctx)
    rows, matrix = P(fsdp + ctx, None), P(fsdp, None)
    in_specs = (rows, P(fsdp), matrix, matrix, matrix, matrix, P(fsdp), matrix, matrix, matrix, rows)
    out_specs = (rows, rows, P(fsdp + ctx), rows, rows, rows, rows, P(fsdp + ctx), rows, rows, rows)
    return jax.shard_map(body, mesh=mesh, in_specs=in_specs, out_specs=out_specs, check_vma=False)
```
